32 devices in a mesh: fsdp: 4 (over y, x), blk: 8 (over z, core).
Axes of the slice: x: 2, y: 2, z: 4, core: 2. Of those that a mesh axis runs over, the one named last changes fastest.
Arguments:
- inputs: bfloat16 [8192, 1152], P(('fsdp', 'blk')), may hold values from -6 to 6
- segments: int32 [4, 2048], P('fsdp'), may hold values from 0 to 2, as said below
- cotangent: bfloat16 [8192, 1152], P(('fsdp', 'blk')), may hold values from -6 to 6
- norm_gain_rows: bfloat16 [2, 1152], P(None, ('fsdp', 'blk')), may hold values from 0.5 to 1.5
- query_key_value_weight: bfloat16 [1152, 1536], P(('fsdp', 'blk')), may hold values from -0.1875 to 0.1875
- output_weight: bfloat16 [1024, 1152], P(('fsdp', 'blk')), may hold values from -1.5 to 1.5
- gate_up_weight: bfloat16 [1152, 13824], P(('fsdp', 'blk')), may hold values from -0.1875 to 0.1875
- down_weight: bfloat16 [6912, 1152], P(('fsdp', 'blk')), may hold values from -0.078125 to 0.078125
- adapter_query_down: bfloat16 [2, 1152, 256], P(None, ('fsdp', 'blk')), may hold values from -0.1875 to 0.1875
- adapter_query_lift: bfloat16 [2, 256, 1536], P(None, ('fsdp', 'blk')), may hold values from -0.1875 to 0.1875
- adapter_output_down: bfloat16 [2, 1024, 256], P(None, ('fsdp', 'blk')), may hold values from -1.5 to 1.5
- adapter_output_lift: bfloat16 [2, 256, 1152], P(None, ('fsdp', 'blk')), may hold values from -0.1875 to 0.1875
Outputs:
- result: bfloat16 [8192, 1152], P(('fsdp', 'blk'))
- d_inputs: float32 [8192, 1152], P(('fsdp', 'blk'))
- d_norm_gains: float32 [2, 1152], P(None, ('fsdp', 'blk'))
- d_w_qkv: float32 [1152, 1536], P(('fsdp', 'blk'))
- d_w_out: float32 [1024, 1152], P(('fsdp', 'blk'))
- d_w_gate_up: float32 [1152, 13824], P(('fsdp', 'blk'))
- d_w_down: float32 [6912, 1152], P(('fsdp', 'blk'))
- d_lora_qkv_in: float32 [2, 1152, 256], P(None, ('fsdp', 'blk'))
- d_lora_qkv_up: float32 [2, 256, 1536], P(None, ('fsdp', 'blk'))
- d_lora_out_in: float32 [2, 1024, 256], P(None, ('fsdp', 'blk'))
- d_lora_out_up: float32 [2, 256, 1152], P(None, ('fsdp', 'blk'))
The draws below stay inside these ranges and needn't reach their ends.
Inputs may be any that keep to these rules, and one draw needn't show every extreme that they name: `segments`: each row holds document numbers 0, 1, 2 in order, each document nonempty; document 1 begins within the first 256 tokens of the row and ends within its last 256 tokens.
All inputs are finite; a program needn't handle non-finite values.
Results may differ from the reference program's by a relative error of at most 0.038.
Values may be sent and summed in bfloat16 or wider, within the bound.
No kernel may reach another device: no remote copies, remote signals or barrier semaphores. Data moves between devices by JAX's collectives and lax.ppermute only.
A program may use at most 448 MiB of HBM per device.

```python
import math
import jax
import jax.numpy as jnp
from jax import lax

MODEL_WIDTH = 1152
FF = 6912
H = 4
HD = 256
ADAPTER_RANK = 256
SEQ = 2048
QUERY_WIDTH = 1024
QUERY_KEY_VALUE = 1536
TOK_DEV = 256
GROUPS = 4
TOKENS = 8192


def draw_segments(key, part):
    key = jax.random.fold_in(key, 11)
    opening_key, closing_key = jax.random.split(key)
    opening = jax.random.randint(opening_key, (GROUPS, 1), 1, TOK_DEV, dtype=jnp.int32)
    closing = jax.random.randint(closing_key, (GROUPS, 1), SEQ - TOK_DEV + 1, SEQ, dtype=jnp.int32)
    places = jnp.arange(SEQ, dtype=jnp.int32)[None, :]
    return (places >= opening).astype(jnp.int32) + (places >= closing).astype(jnp.int32)


def with_spikes(drawn, stream_key, source, target, blocks, factor):
    owner, partner = [(jnp.arange(drawn.shape[position]) // (drawn.shape[position] // blocks)).reshape([-1 if axis == position else 1 for axis in range(drawn.ndim)]) for position in (source, target)]
    chosen = jax.random.permutation(stream_key, blocks)[partner]
    strong = (owner == chosen) | (owner == (partner + blocks // 2) % blocks)
    return jnp.where(strong, factor * drawn, drawn)


def block_scale(stream_key, dims, shards, smallest, largest):
    loudness = 1.0
    for position, parts in shards:
        steps = jax.random.uniform(jax.random.fold_in(jax.random.fold_in(stream_key, 6), position), (parts,), jnp.float32, smallest / len(shards), largest / len(shards))
        loudness = loudness * jnp.repeat(jnp.exp(steps), dims[position] // parts).reshape((-1,) + (1,) * (len(dims) - 1 - position))
    return loudness


def normal_values(key, extent, deviation, most, pieces=(), kind=jnp.bfloat16):
    entries = jax.random.normal(key, extent, jnp.float32) * deviation
    if len(pieces) > 0:
        entries = block_scale(key, extent, pieces, -0.22, 0.18) * entries
    return jnp.clip(entries, min=-most, max=most).astype(kind)


def heavy_noise(stream_key, dims, spread, most, cuts, heavy, held_as=jnp.bfloat16):
    entries = spread * jax.random.normal(stream_key, dims, jnp.float32)
    if cuts:
        entries = entries * block_scale(stream_key, dims, cuts, -0.22, 0.18)
    return jnp.clip(with_spikes(entries, jax.random.fold_in(stream_key, 3), *heavy), -most, most).astype(held_as)


def setup_inputs(seed: int = 0) -> dict:
    key_list = jax.random.split(jax.random.key(seed), 13)
    return {
        "inputs": heavy_noise(key_list[0], (TOKENS, MODEL_WIDTH), 1.0, 6.0, ((0, 32),), (0, 1, 32, 2.75)),
        "segments": draw_segments(jax.random.fold_in(key_list[12], 71), 0),
        "cotangent": normal_values(key_list[2], (TOKENS, MODEL_WIDTH), 1.0, 6.0, ((0, 32),)),
        "norm_gain_rows": jnp.clip(1.0 + 0.1 * jax.random.normal(key_list[3], (2, MODEL_WIDTH), jnp.float32), 0.5, 1.5).astype(jnp.bfloat16),
        "query_key_value_weight": normal_values(key_list[4], (MODEL_WIDTH, QUERY_KEY_VALUE), MODEL_WIDTH ** -0.5, 0.1875, ((0, 32),)),
        "output_weight": normal_values(key_list[5], (QUERY_WIDTH, MODEL_WIDTH), (QUERY_WIDTH // 64) ** -0.5, 1.5, ((0, 32),)),
        "gate_up_weight": normal_values(key_list[6], (MODEL_WIDTH, 2 * FF), MODEL_WIDTH ** -0.5, 0.1875, ((0, 32),)),
        "down_weight": normal_values(key_list[7], (FF, MODEL_WIDTH), FF ** -0.5, 0.078125, ((0, 32),)),
        "adapter_query_down": normal_values(key_list[8], (2, MODEL_WIDTH, ADAPTER_RANK), MODEL_WIDTH ** -0.5, 0.1875, ((1, 32),)),
        "adapter_query_lift": normal_values(key_list[9], (2, ADAPTER_RANK, QUERY_KEY_VALUE), (4 * ADAPTER_RANK) ** -0.5, 0.1875, ((1, 32),)),
        "adapter_output_down": normal_values(key_list[10], (2, QUERY_WIDTH, ADAPTER_RANK), (QUERY_WIDTH // 64) ** -0.5, 1.5, ((1, 32),)),
        "adapter_output_lift": normal_values(key_list[11], (2, ADAPTER_RANK, MODEL_WIDTH), (4 * ADAPTER_RANK) ** -0.5, 0.1875, ((1, 32),)),
    }


EPS = 1e-06
NEG = -1e+30
ROPE_BASE = 10000.0

@jax.custom_vjp
def low(v):
    return lax.optimization_barrier(v.astype(jnp.bfloat16)).astype(jnp.float32)

@jax.custom_vjp
def low_back(v):
    return v

def low_keep(v):
    return (low(v), None)

def low_pass(kept, grad):
    return (grad,)

def back_keep(v):
    return (v, None)

def back_low(kept, grad):
    return (low(grad),)
low.defvjp(low_keep, low_pass)
low_back.defvjp(back_keep, back_low)

def matmul(left_side, right_side):
    return jnp.dot(left_side, right_side, precision=lax.Precision.HIGHEST)

def norm_rows(values, gain_row):
    return values * lax.rsqrt(lax.optimization_barrier(jnp.mean(values * values, axis=-1, keepdims=True)) + EPS) * gain_row

def rotate(values, cosine_table, sine_table):
    halfway = values.shape[-1] // 2
    first_half = values[..., :halfway]
    second_half = values[..., halfway:]
    return jnp.concatenate([first_half * cosine_table - second_half * sine_table, second_half * cosine_table + first_half * sine_table], axis=-1)

def angles_of(segrow):
    places = jnp.arange(segrow.shape[0], dtype=jnp.int32)
    previous = jnp.concatenate([segrow[:1] - 1, segrow[:-1]])
    starts = lax.cummax(jnp.where(segrow != previous, places, 0), axis=0)
    offsets = (places - starts).astype(jnp.float32)
    frequency = jnp.exp(jnp.arange(HD // 2, dtype=jnp.float32) * (-2.0 * math.log(ROPE_BASE) / HD))
    turned = offsets[:, None] * frequency[None, :]
    return (jnp.cos(turned), jnp.sin(turned))

def attend(queries, key_rows, value_rows, segrow):
    length = key_rows.shape[0]
    block_rows = math.gcd(length, 512)
    places = jnp.arange(length, dtype=jnp.int32)

    def one_block(number):
        first_row = number * block_rows
        query_block = lax.dynamic_slice_in_dim(queries, first_row, block_rows, 1)
        query_places = first_row + jnp.arange(block_rows, dtype=jnp.int32)
        query_segs = lax.dynamic_slice_in_dim(segrow, first_row, block_rows, 0)
        scores = low_back(jnp.einsum('hqd,kd->hqk', query_block, key_rows, precision=lax.Precision.HIGHEST))
        allowed = (query_segs[:, None] == segrow[None, :]) & (places[None, :] <= query_places[:, None])
        scores = jnp.where(allowed[None], scores, NEG)
        weights = low(jax.nn.softmax(scores, axis=-1))
        return jnp.einsum('hqk,kd->hqd', weights, value_rows, precision=lax.Precision.HIGHEST)
    blocks = lax.map(jax.checkpoint(one_block), jnp.arange(length // block_rows, dtype=jnp.int32))
    return jnp.transpose(blocks, (1, 0, 2, 3)).reshape(queries.shape[0], length, queries.shape[2])

def one_loop(residual, loop_index, tables, segrow, gain_rows, query_key_value_weight, output_weight, gate_up_weight, down_weight, qkv_in, qkv_up, out_in, out_up):
    cosine_table, sine_table = tables
    length = residual.shape[0]
    normed = low(norm_rows(residual, gain_rows[0]))
    low_rank = low(low_back(matmul(normed, qkv_in[loop_index])))
    joined = low_back(matmul(normed, query_key_value_weight) + matmul(low_rank, qkv_up[loop_index]))
    query_heads = joined[:, :QUERY_WIDTH].reshape(length, H, HD).transpose(1, 0, 2)
    queries = low(rotate(query_heads, cosine_table, sine_table) * HD ** (-0.5))
    key_rows = low(rotate(joined[:, QUERY_WIDTH:QUERY_WIDTH + HD], cosine_table, sine_table))
    value_rows = low(joined[:, QUERY_WIDTH + HD:])
    mixed_out = attend(queries, key_rows, value_rows, segrow)
    mixed_out = low(low_back(mixed_out.transpose(1, 0, 2).reshape(length, QUERY_WIDTH)))
    side_rank = low(low_back(matmul(mixed_out, out_in[loop_index])))
    middle = residual + low_back(matmul(mixed_out, output_weight) + matmul(side_rank, out_up[loop_index]))
    normed_ff = low(norm_rows(middle, gain_rows[1]))
    gate_up = low_back(matmul(normed_ff, gate_up_weight))
    hidden = low(jax.nn.gelu(gate_up[:, :FF], approximate=True) * gate_up[:, FF:])
    return middle + low_back(matmul(hidden, down_weight))

def forward(residual, segrow, *weights):
    tables = angles_of(segrow)
    for loop_index in range(2):
        residual = one_loop(residual, loop_index, tables, segrow, *weights)
    return residual

def reference(inputs, segments, cotangent, norm_gain_rows, query_key_value_weight, output_weight, gate_up_weight, down_weight, adapter_query_down, adapter_query_lift, adapter_output_down, adapter_output_lift):
    parameters = tuple((weight_matrix.astype(jnp.float32) for weight_matrix in (norm_gain_rows, query_key_value_weight, output_weight, gate_up_weight, down_weight, adapter_query_down, adapter_query_lift, adapter_output_down, adapter_output_lift)))
    residuals = inputs.astype(jnp.float32).reshape(GROUPS, SEQ, MODEL_WIDTH)
    cotangents = cotangent.astype(jnp.float32).reshape(GROUPS, SEQ, MODEL_WIDTH)

    def group_step(totals, scan_item):
        residual, segrow, cot_rows = scan_item

        def run(residual_in, *weights):
            return forward(residual_in, segrow, *weights)
        result_rows, pullback = jax.vjp(run, residual, *parameters)
        gradients = pullback(cot_rows)
        totals = tuple((running + gradient for running, gradient in zip(totals, gradients[1:])))
        return (totals, (result_rows, gradients[0]))
    zero_sums = tuple((jnp.zeros_like(weight_matrix) for weight_matrix in parameters))
    totals, outputs = lax.scan(group_step, zero_sums, (residuals, segments, cotangents))
    results, input_grads = outputs
    return (results.reshape(TOKENS, MODEL_WIDTH).astype(jnp.bfloat16), input_grads.reshape(TOKENS, MODEL_WIDTH), totals[0], totals[1], totals[2], totals[3], totals[4], totals[5], totals[6], totals[7], totals[8])
```

```python
import math

import jax
import jax.numpy as jnp
from jax import lax
from jax.sharding import PartitionSpec as P

H = 4
HD = 256
EPS = 1e-06
NEG = -1e30
ROPE_BASE = 10000.0
AXES = ("fsdp", "blk")
BF = jnp.bfloat16
F32 = jnp.float32


def matmul(left_side, right_side):
    return jnp.dot(left_side, right_side, preferred_element_type=F32)


def matmul_nt(left_side, right_side):
    return lax.dot_general(
        left_side, right_side, (((1,), (1,)), ((), ())), preferred_element_type=F32
    )


def matmul_tn(left_side, right_side):
    return lax.dot_general(
        left_side, right_side, (((0,), (0,)), ((), ())), preferred_element_type=F32
    )


def rounded(values):
    return values.astype(BF)


class Grid:
    def __init__(self, mesh):
        self.fsdp = mesh.shape["fsdp"]
        self.blk = mesh.shape["blk"]
        self.sizes = {"y": self.fsdp // 2, "x": 2, "p": self.blk // 4, "h": 2, "c": 2}
        self.devices = self.fsdp * self.blk
        self.groups = self.devices // 4

    def place(self, name):
        f = lax.axis_index("fsdp")
        b = lax.axis_index("blk")
        return {"y": f // 2, "x": f % 2, "p": b // 4, "h": (b // 2) % 2, "c": b % 2}[name]

    def permute(self, values, shifts):
        pairs = []
        for f in range(self.fsdp):
            for b in range(self.blk):
                at = {"y": f // 2, "x": f % 2, "p": b // 4, "h": (b // 2) % 2, "c": b % 2}
                for name, shift in shifts.items():
                    at[name] = (at[name] + shift) % self.sizes[name]
                pairs.append(
                    (
                        f * self.blk + b,
                        (at["y"] * 2 + at["x"]) * self.blk + at["p"] * 4 + at["h"] * 2 + at["c"],
                    )
                )
        return lax.ppermute(values, AXES, pairs)

    def gather(self, values, name, axis):
        size = self.sizes[name]
        if size == 1:
            return jnp.expand_dims(values, axis)
        place = self.place(name)
        if size == 2:
            other = self.permute(values, {name: 1})
            first = place == 0
            return jnp.stack(
                [jnp.where(first, values, other), jnp.where(first, other, values)], axis=axis
            )
        parts = [values] + [self.permute(values, {name: shift}) for shift in range(1, size)]
        stacked = jnp.stack(parts, axis=axis)
        order = (place - jnp.arange(size)) % size
        return jnp.take(stacked, order, axis=axis)

    def scatter(self, values, name, axis):
        size = self.sizes[name]
        place = self.place(name)
        total = lax.dynamic_index_in_dim(values, place, axis, keepdims=False).astype(F32)
        for shift in range(1, size):
            sent = lax.dynamic_index_in_dim(values, (place + shift) % size, axis, keepdims=False)
            total = total + self.permute(sent.astype(BF), {name: shift}).astype(F32)
        return total

    def gather_all(self, values, turn, with_core):
        out = self.gather(values, "p", 0)
        out = self.gather(out, "h", 1)
        if turn:
            out = self.gather(out, "y", 0)
            out = self.gather(out, "x", 1)
        else:
            out = self.gather(out, "x", 0)
            out = self.gather(out, "y", 0)
        if with_core:
            out = self.gather(out, "c", 4)
        return out

    def gather_groups(self, values, turn):
        out = self.gather(values, "p", 0)
        if turn:
            out = self.gather(out, "y", 0)
            out = self.gather(out, "x", 1)
        else:
            out = self.gather(out, "x", 0)
            out = self.gather(out, "y", 0)
        return out.reshape(self.groups * values.shape[0], values.shape[1])

    def scatter_groups(self, values, turn):
        sizes = self.sizes
        out = values.reshape(
            sizes["y"], 2, sizes["p"], values.shape[0] // self.groups, values.shape[1]
        )
        if turn:
            out = self.scatter(out, "y", 0)
            out = self.scatter(out, "x", 0)
        else:
            out = self.scatter(out, "x", 1)
            out = self.scatter(out, "y", 0)
        return self.scatter(out, "p", 0)

    def scatter_all(self, values, turn):
        sizes = self.sizes
        out = values.reshape((sizes["y"], 2, sizes["p"], 2, 2) + values.shape[1:])
        out = self.scatter(out, "c", 4)
        if turn:
            out = self.scatter(out, "y", 0)
            out = self.scatter(out, "x", 0)
        else:
            out = self.scatter(out, "x", 1)
            out = self.scatter(out, "y", 0)
        out = self.scatter(out, "h", 1)
        return self.scatter(out, "p", 0)

    def tokens_in(self, rows):
        both = jnp.concatenate([rows, self.permute(rows, {"h": 1})], axis=0)
        return jnp.concatenate([both, self.permute(both, {"c": 1})], axis=0)

    def tokens_out(self, sums):
        count = sums.shape[0] // 4
        both = sums[: 2 * count] + self.permute(rounded(sums[2 * count :]), {"c": 1}).astype(F32)
        return both[:count] + self.permute(rounded(both[count:]), {"h": 1}).astype(F32)


def pad_rows(values, rows, axis):
    if values.shape[axis] == rows:
        return values
    widths = [(0, 0)] * values.ndim
    widths[axis] = (0, rows - values.shape[axis])
    return jnp.pad(values, widths)


def up8(rows):
    return -(-rows // 8) * 8


def pack(parts):
    axis = parts[0].ndim - 2
    return jnp.concatenate([pad_rows(part, up8(part.shape[axis]), axis) for part in parts], axis=axis)


def unpack(packed, counts):
    out = []
    at = 0
    for count in counts:
        piece = packed[:, at : at + count]
        out.append(piece.reshape(packed.shape[0] * count, packed.shape[2]))
        at += up8(count)
    return out


def unpack_own(packed, counts):
    out = []
    at = 0
    for count in counts:
        out.append(packed[at : at + count])
        at += up8(count)
    return out


def norm_rows(values, gain_row):
    return values * lax.rsqrt(jnp.mean(values * values, axis=-1, keepdims=True) + EPS) * gain_row


def norm_back(values, gain_row, grad):
    inverse = lax.rsqrt(jnp.mean(values * values, axis=-1, keepdims=True) + EPS)
    weighted = grad * gain_row
    inner = jnp.mean(weighted * values, axis=-1, keepdims=True)
    gain_grad = jnp.sum(grad * values * inverse, axis=0)
    return inverse * weighted - values * (inverse * inverse * inverse) * inner, gain_grad


def rotate(values, cosine_table, sine_table):
    halfway = values.shape[-1] // 2
    first_half = values[..., :halfway]
    second_half = values[..., halfway:]
    return jnp.concatenate(
        [
            first_half * cosine_table - second_half * sine_table,
            second_half * cosine_table + first_half * sine_table,
        ],
        axis=-1,
    )


def activate(gate, up):
    return jax.nn.gelu(gate, approximate=True) * up


def per_device(
    grid,
    inputs,
    segments,
    cotangent,
    norm_gain_rows,
    query_key_value_weight,
    output_weight,
    gate_up_weight,
    down_weight,
    adapter_query_down,
    adapter_query_lift,
    adapter_output_down,
    adapter_output_lift,
):
    tokens = inputs.shape[0]
    width = inputs.shape[1]
    groups = grid.groups
    gain_cols = norm_gain_rows.shape[1]
    qkv_rows = query_key_value_weight.shape[0]
    out_rows = output_weight.shape[0]
    qd_rows = adapter_query_down.shape[1]
    ql_rows = adapter_query_lift.shape[1]
    od_rows = adapter_output_down.shape[1]
    ol_rows = adapter_output_lift.shape[1]
    rank = adapter_query_down.shape[2]
    hidden_block = down_weight.shape[0]

    gains_part = jnp.pad(norm_gain_rows, ((0, 0), (0, rank - gain_cols)))
    packed_qkv = pack([query_key_value_weight, adapter_query_lift[0], adapter_query_lift[1]])
    packed_narrow = pack(
        [
            adapter_query_down[0],
            adapter_query_down[1],
            adapter_output_down[0],
            adapter_output_down[1],
            gains_part,
        ]
    )
    packed_out = pack([output_weight, adapter_output_lift[0], adapter_output_lift[1]])

    def whole(packed, turn):
        return grid.gather_all(packed, turn, True).reshape((grid.devices,) + packed.shape)

    all_qkv = whole(packed_qkv, False)
    all_narrow = whole(packed_narrow, True)
    all_out = whole(packed_out, True)
    qkv_counts = [qkv_rows, ql_rows, ql_rows]
    out_counts = [out_rows, ol_rows, ol_rows]
    narrow_counts = [qd_rows, qd_rows, od_rows, od_rows]
    w_qkv, ql_0, ql_1 = unpack(all_qkv, qkv_counts)
    qd_0, qd_1, od_0, od_1 = unpack(all_narrow, narrow_counts)
    w_out, ol_0, ol_1 = unpack(all_out, out_counts)
    gains = (
        all_narrow[:, -8:-6, :gain_cols].transpose(1, 0, 2).reshape(2, width).astype(F32)
    )
    adapters = ((qd_0, ql_0, od_0, ol_0), (qd_1, ql_1, od_1, ol_1))

    place_h = grid.place("h")
    place_c = grid.place("c")
    quarter = place_h * 2 + place_c
    cut = (
        gate_up_weight.reshape(qkv_rows, 2, groups, 4, hidden_block)
        .transpose(3, 1, 0, 2, 4)
        .reshape(2, 2, 2, qkv_rows, groups * hidden_block)
    )

    def cut_for(h, c):
        part = lax.dynamic_index_in_dim(cut, h, 0, keepdims=False)
        return lax.dynamic_index_in_dim(part, c, 0, keepdims=False)

    own = cut_for(place_h, place_c)
    from_c = grid.permute(cut_for(place_h, 1 - place_c), {"c": 1})
    from_h = grid.permute(cut_for(1 - place_h, place_c), {"h": 1})
    from_hc = grid.permute(cut_for(1 - place_h, 1 - place_c), {"h": 1, "c": 1})
    relative = jnp.stack([own, from_c, from_h, from_hc])
    pieces = jnp.stack(
        [
            lax.dynamic_index_in_dim(relative, quarter ^ index, 0, keepdims=False)
            for index in range(4)
        ],
        axis=1,
    )
    pieces = pieces.reshape(2, 4 * qkv_rows, groups * hidden_block)
    w_gate = grid.gather_groups(pieces[0], False)
    w_up = grid.gather_groups(pieces[1], True)
    half_cols = (width // 256) * 128 + 128
    w_down = jnp.concatenate(
        [
            grid.gather_groups(down_weight[:, :half_cols], False),
            grid.gather_groups(down_weight[:, half_cols:], True),
        ],
        axis=1,
    )

    segrow = segments[0]
    seq_len = segrow.shape[0]
    position = lax.axis_index("blk")
    places = position * tokens + jnp.arange(tokens, dtype=jnp.int32)
    own_segs = lax.dynamic_slice_in_dim(segrow, position * tokens, tokens, 0)
    below_one = jnp.sum((segrow < 1).astype(jnp.int32))
    below_two = jnp.sum((segrow < 2).astype(jnp.int32))
    starts = jnp.where(own_segs == 0, 0, jnp.where(own_segs == 1, below_one, below_two))
    offsets = (places - starts).astype(F32)
    frequency = jnp.exp(jnp.arange(HD // 2, dtype=F32) * (-2.0 * math.log(ROPE_BASE) / HD))
    turned = offsets[:, None] * frequency[None, :]
    cosine_table = jnp.cos(turned)
    sine_table = jnp.sin(turned)
    width_q = H * HD
    row_places = jnp.tile(places, H)
    row_segs = jnp.tile(own_segs, H)
    key_places = jnp.arange(seq_len, dtype=jnp.int32)
    allowed = (row_segs[:, None] == segrow[None, :]) & (key_places[None, :] <= row_places[:, None])

    def forward_loop(residual, loop):
        qd, ql, od, ol = adapters[loop]
        normed_b = rounded(norm_rows(residual, gains[0]))
        low_rank_b = rounded(matmul(normed_b, qd))
        joined = matmul(normed_b, w_qkv) + matmul(low_rank_b, ql)
        query_heads = joined[:, :width_q].reshape(tokens, H, HD).transpose(1, 0, 2)
        queries = rounded(rotate(query_heads, cosine_table, sine_table) * HD ** (-0.5)).reshape(
            H * tokens, HD
        )
        key_rows = rounded(rotate(joined[:, width_q : width_q + HD], cosine_table, sine_table))
        value_rows = rounded(joined[:, width_q + HD :])
        both = lax.all_gather(
            jnp.concatenate([key_rows, value_rows], axis=1), "blk", axis=0, tiled=True
        )
        keys, values = both[:, :HD], both[:, HD:]
        scores = matmul_nt(queries, keys)
        top = jnp.max(jnp.where(allowed, scores, NEG), axis=1, keepdims=True)
        probabilities = jnp.where(allowed, jnp.exp(scores - top), 0.0)
        total = jnp.sum(probabilities, axis=1, keepdims=True)
        mixed_rows = matmul(rounded(probabilities), values) / total
        log_total = top + jnp.log(total)
        mixed_b = rounded(
            mixed_rows.reshape(H, tokens, HD).transpose(1, 0, 2).reshape(tokens, width_q)
        )
        side_b = rounded(matmul(mixed_b, od))
        middle = residual + (matmul(mixed_b, w_out) + matmul(side_b, ol))
        normed_ff_b = rounded(norm_rows(middle, gains[1]))
        ff_in = grid.tokens_in(normed_ff_b)
        gate = matmul(ff_in, w_gate)
        up = matmul(ff_in, w_up)
        hidden_b = rounded(activate(gate, up))
        following = middle + grid.tokens_out(matmul(hidden_b, w_down))
        cache = (
            residual, normed_b, low_rank_b, queries, keys, values, mixed_rows, log_total,
            mixed_b, side_b, middle, ff_in, rounded(gate), rounded(up), hidden_b,
        )
        return following, cache

    def backward_loop(cache, grad_result, loop):
        (
            residual, normed_b, low_rank_b, queries, keys, values, mixed_rows, log_total,
            mixed_b, side_b, middle, ff_in, gate_b, up_b, hidden_b,
        ) = cache
        qd, ql, od, ol = adapters[loop]
        ff_grad = grid.tokens_in(rounded(grad_result))
        grad_hidden = matmul_nt(ff_grad, w_down)
        unused, pullback = jax.vjp(activate, gate_b.astype(F32), up_b.astype(F32))
        grad_gate, grad_up = pullback(grad_hidden)
        grad_gate_b = rounded(grad_gate)
        grad_up_b = rounded(grad_up)
        d_down = matmul_tn(hidden_b, ff_grad)
        grad_normed_ff = grid.tokens_out(
            matmul_nt(grad_gate_b, w_gate) + matmul_nt(grad_up_b, w_up)
        )
        d_gate = matmul_tn(ff_in, grad_gate_b)
        d_up = matmul_tn(ff_in, grad_up_b)
        grad_middle_norm, gain_grad_ff = norm_back(middle, gains[1], grad_normed_ff)
        grad_middle = grad_result + grad_middle_norm
        grad_branch_b = rounded(grad_middle)
        grad_side_b = rounded(matmul_nt(grad_branch_b, ol))
        grad_mixed_b = rounded(matmul_nt(grad_branch_b, w_out) + matmul_nt(grad_side_b, od))
        d_out = matmul_tn(mixed_b, grad_branch_b)
        d_ol = matmul_tn(side_b, grad_branch_b)
        d_od = matmul_tn(mixed_b, grad_side_b)
        grad_rows = grad_mixed_b.reshape(tokens, H, HD).transpose(1, 0, 2).reshape(H * tokens, HD)
        delta = jnp.sum(grad_rows.astype(F32) * mixed_rows, axis=1, keepdims=True)
        scores = matmul_nt(queries, keys)
        probabilities = jnp.where(allowed, jnp.exp(scores - log_total), 0.0)
        grad_probs = matmul_nt(grad_rows, values)
        grad_scores = rounded(probabilities * (grad_probs - delta))
        grad_q = matmul(grad_scores, keys)
        grad_k_all = matmul_tn(grad_scores, queries)
        grad_v_all = matmul_tn(rounded(probabilities), grad_rows)
        grad_kv = lax.psum_scatter(
            jnp.concatenate([rounded(grad_k_all), rounded(grad_v_all)], axis=1),
            "blk",
            scatter_dimension=0,
            tiled=True,
        ).astype(F32)
        grad_query_heads = rotate(
            grad_q.reshape(H, tokens, HD), cosine_table, -sine_table
        ) * HD ** (-0.5)
        grad_joined_b = rounded(
            jnp.concatenate(
                [
                    grad_query_heads.transpose(1, 0, 2).reshape(tokens, width_q),
                    rotate(grad_kv[:, :HD], cosine_table, -sine_table),
                    grad_kv[:, HD:],
                ],
                axis=1,
            )
        )
        grad_low_rank_b = rounded(matmul_nt(grad_joined_b, ql))
        grad_normed = matmul_nt(grad_joined_b, w_qkv) + matmul_nt(grad_low_rank_b, qd)
        grad_state_norm, gain_grad_attn = norm_back(residual, gains[0], grad_normed)
        shared = (
            jnp.stack([gain_grad_attn, gain_grad_ff]),
            matmul_tn(normed_b, grad_joined_b),
            d_out,
            d_gate,
            d_up,
            d_down,
        )
        single = (
            matmul_tn(normed_b, grad_low_rank_b),
            matmul_tn(low_rank_b, grad_joined_b),
            d_od,
            d_ol,
        )
        return grad_middle + grad_state_norm, shared, single

    residual_zero = inputs.astype(F32)
    residual_one, cache_one = forward_loop(residual_zero, 0)
    result, cache_two = forward_loop(residual_one, 1)
    grad_one, shared_two, single_two = backward_loop(cache_two, cotangent.astype(F32), 1)
    grad_inputs, shared_one, single_one = backward_loop(cache_one, grad_one, 0)
    g_gains, g_qkv, g_out, g_gate, g_up, g_down = [
        first + second for first, second in zip(shared_two, shared_one)
    ]

    def blocks(values):
        return values.reshape(grid.devices, values.shape[0] // grid.devices, values.shape[1])

    d_down = jnp.concatenate(
        [
            grid.scatter_groups(g_down[:, :half_cols], False),
            grid.scatter_groups(g_down[:, half_cols:], True),
        ],
        axis=1,
    )
    d_pieces = jnp.stack(
        [grid.scatter_groups(g_gate, False), grid.scatter_groups(g_up, True)]
    ).reshape(2, 4, qkv_rows, groups * hidden_block)
    d_pieces = rounded(d_pieces)

    def member(index):
        return lax.dynamic_index_in_dim(d_pieces, index, 1, keepdims=False)

    back = jnp.stack(
        [
            member(quarter),
            grid.permute(member(quarter ^ 1), {"c": 1}),
            grid.permute(member(quarter ^ 2), {"h": 1}),
            grid.permute(member(quarter ^ 3), {"h": 1, "c": 1}),
        ]
    )
    back = jnp.stack(
        [lax.dynamic_index_in_dim(back, quarter ^ index, 0, keepdims=False) for index in range(4)]
    )
    d_gate_up = (
        back.reshape(4, 2, qkv_rows, groups, hidden_block)
        .transpose(2, 1, 3, 0, 4)
        .reshape(qkv_rows, 8 * groups * hidden_block)
        .astype(F32)
    )

    got_out = grid.scatter_all(
        pack([blocks(g_out), blocks(single_one[3]), blocks(single_two[3])]), True
    )
    d_out, d_ol_0, d_ol_1 = unpack_own(got_out, out_counts)
    gain_blocks = jnp.pad(
        g_gains.reshape(2, grid.devices, gain_cols).transpose(1, 0, 2),
        ((0, 0), (0, 0), (0, rank - gain_cols)),
    )
    got_narrow = grid.scatter_all(
        pack(
            [
                blocks(single_one[0]),
                blocks(single_two[0]),
                blocks(single_one[2]),
                blocks(single_two[2]),
                gain_blocks,
            ]
        ),
        True,
    )
    d_qd_0, d_qd_1, d_od_0, d_od_1 = unpack_own(got_narrow, narrow_counts)
    d_gains = got_narrow[-8:-6, :gain_cols]
    got_qkv = grid.scatter_all(
        pack([blocks(g_qkv), blocks(single_one[1]), blocks(single_two[1])]), False
    )
    d_qkv, d_ql_0, d_ql_1 = unpack_own(got_qkv, qkv_counts)
    return (
        rounded(result),
        grad_inputs,
        d_gains,
        d_qkv,
        d_out,
        d_gate_up,
        d_down,
        jnp.stack([d_qd_0, d_qd_1]),
        jnp.stack([d_ql_0, d_ql_1]),
        jnp.stack([d_od_0, d_od_1]),
        jnp.stack([d_ol_0, d_ol_1]),
    )


def solution(mesh):
    grid = Grid(mesh)
    rows = P(AXES, None)
    deep = P(None, AXES, None)
    in_specs = (
        rows, P("fsdp", None), rows, P(None, AXES), rows, rows, rows, rows, deep, deep, deep, deep,
    )
    out_specs = (
        rows, rows, P(None, AXES), rows, rows, rows, rows, deep, deep, deep, deep,
    )

    def run(*arguments):
        return per_device(grid, *arguments)

    return jax.shard_map(
        run, mesh=mesh, in_specs=in_specs, out_specs=out_specs, check_vma=False
    )
```

```python
import functools
import itertools
import math

import jax
import jax.numpy as jnp
from jax import lax
from jax.experimental import pallas as pl
from jax.experimental.pallas import tpu as pltpu
from jax.sharding import PartitionSpec as P

H = 4
HD = 256
EPS = 1e-06
NEG = -1e30
ROPE_BASE = 10000.0
AXES = ("fsdp", "blk")
BF = jnp.bfloat16
F32 = jnp.float32


def matmul(left_side, right_side):
    return jnp.dot(left_side, right_side, preferred_element_type=F32)


def matmul_nt(left_side, right_side):
    return lax.dot_general(
        left_side, right_side, (((1,), (1,)), ((), ())), preferred_element_type=F32
    )


def matmul_tn(left_side, right_side):
    return lax.dot_general(
        left_side, right_side, (((0,), (0,)), ((), ())), preferred_element_type=F32
    )


def rounded(values):
    return values.astype(BF)


NAMES = ("y", "x", "p", "h", "c")


class Grid:
    def __init__(self, mesh):
        self.fsdp = mesh.shape["fsdp"]
        self.blk = mesh.shape["blk"]
        self.sizes = {"y": self.fsdp // 2, "x": 2, "p": self.blk // 4, "h": 2, "c": 2}
        self.devices = self.fsdp * self.blk
        self.groups = self.devices // 4

    def places(self):
        f = lax.axis_index("fsdp")
        b = lax.axis_index("blk")
        return {"y": f // 2, "x": f % 2, "p": b // 4, "h": (b // 2) % 2, "c": b % 2}

    def coordinates(self):
        places = self.places()
        return jnp.stack([places[name] for name in NAMES]).astype(jnp.int32)

    def permute(self, values, masks):
        pairs = []
        for f in range(self.fsdp):
            for b in range(self.blk):
                at = {"y": f // 2, "x": f % 2, "p": b // 4, "h": (b // 2) % 2, "c": b % 2}
                for name, mask in masks.items():
                    at[name] = at[name] ^ mask
                pairs.append(
                    (
                        f * self.blk + b,
                        (at["y"] * 2 + at["x"]) * self.blk + at["p"] * 4 + at["h"] * 2 + at["c"],
                    )
                )
        return lax.ppermute(values, AXES, pairs)

    def parts(self, values, name):
        return [values] + [
            self.permute(values, {name: mask}) for mask in range(1, self.sizes[name])
        ]

    def order(self, names):
        out = []
        stride = 1
        for name in names:
            out.append((NAMES.index(name), stride))
            stride *= self.sizes[name]
        return tuple(out)

    def blocks_of(self, names):
        out = []
        for y in range(self.sizes["y"]):
            for x in range(2):
                for p in range(self.sizes["p"]):
                    for h in range(2 if "h" in names else 1):
                        for c in range(2 if "c" in names else 1):
                            out.append((y, x, p, h, c))
        return tuple(out)

    def tokens_in(self, rows):
        other = self.permute(rows, {"h": 1})
        return [rows, other, self.permute(rows, {"c": 1}), self.permute(other, {"c": 1})]

    def extent(self, names):
        return tuple(self.sizes[name] for name in names)


def up8(rows):
    return -(-rows // 8) * 8


TILE = 256
INNER = math.sqrt(2.0 / math.pi)
CUBIC = 0.044715


def chunk_of(rows):
    return min(rows, 256)


LIGHT = pl.CostEstimate(flops=0, bytes_accessed=0, transcendentals=0)


def full(extent):
    return pl.BlockSpec(extent, lambda j: tuple([0] * len(extent)))


ANY = pl.BlockSpec(memory_space=pl.ANY)


def tied(body, operands, ties):
    if not ties:
        return body

    def run(*refs):
        body(*refs[:operands], *refs[operands + len(ties) :])

    return run


def kernel_call(body, grid, in_specs, out_specs, out_shape, scratch, ties=()):
    return pl.pallas_call(
        tied(body, len(in_specs), ties),
        grid=grid,
        in_specs=in_specs + [ANY] * len(ties),
        out_specs=out_specs,
        out_shape=out_shape,
        scratch_shapes=scratch,
        cost_estimate=LIGHT,
        compiler_params=pltpu.CompilerParams(
            dimension_semantics=("arbitrary",), vmem_limit_bytes=48 * 1024 * 1024
        ),
    )


def whole_call(body, out_shape, coordinates, operands, ties=(), scratch=()):
    count = len(operands)
    specs = [pl.BlockSpec(memory_space=pltpu.VMEM)] * count
    if coordinates is not None:
        operands = [coordinates, *operands]
        specs = [pl.BlockSpec(memory_space=pltpu.SMEM)] + specs
    return pl.pallas_call(
        tied(body, len(specs), ties),
        out_shape=out_shape,
        in_specs=specs + [ANY] * len(ties),
        scratch_shapes=list(scratch),
        cost_estimate=LIGHT,
        compiler_params=pltpu.CompilerParams(vmem_limit_bytes=48 * 1024 * 1024),
    )(*operands, *ties)


def left_columns(width):
    return (width // 256) * 128 + 128


def add_rows(start, size, value, own_ref, other_ref):
    half = own_ref.shape[0]
    if start < half:
        own_ref[start : start + size] += value
    else:
        other_ref[start - half : start - half + size] += value


CHUNKS = 4


def send_rows(other_ref, sent_refs):
    count = sent_refs[0].shape[0]
    for number, sent_ref in enumerate(sent_refs):
        sent_ref[...] = rounded(other_ref[number * count : (number + 1) * count])


def sent_chunks(rows, width):
    count = rows // 2 // CHUNKS
    return [full((count, width))] * CHUNKS, [shape(count, width)] * CHUNKS


def ff_forward_body(
    x0_ref, x1_ref, x2_ref, x3_ref, wg_ref, wu_ref, wd_ref, own_ref, g_ref, u_ref, *sent_refs
):
    *sent_refs, other_ref = sent_refs
    size = x0_ref.shape[0]

    @pl.when(pl.program_id(0) == 0)
    def _():
        own_ref[...] = jnp.zeros_like(own_ref)
        other_ref[...] = jnp.zeros_like(other_ref)

    wg, wu, wd = wg_ref[...], wu_ref[...], wd_ref[...]
    for number, x_ref in enumerate((x0_ref, x1_ref, x2_ref, x3_ref)):
        start = number * size
        part = slice(start, start + size)
        x = x_ref[...]
        gate = matmul(x, wg)
        up = matmul(x, wu)
        g_ref[part] = rounded(gate)
        u_ref[part] = rounded(up)
        bent = jnp.tanh(INNER * (gate + CUBIC * (gate * gate * gate)))
        hidden = rounded(0.5 * gate * (1.0 + bent) * up)
        add_rows(start, size, matmul(hidden, wd), own_ref, other_ref)

    @pl.when(pl.program_id(0) == pl.num_programs(0) - 1)
    def _():
        send_rows(other_ref, sent_refs)


def ff_forward(blocks, w_gate, w_up, w_down, ties=()):
    size, width = blocks[0].shape
    rows = 4 * size
    wide = w_gate.shape[1]
    column = pl.BlockSpec((rows, TILE), lambda j: (0, j))
    return kernel_call(
        ff_forward_body,
        (wide // TILE,),
        [full((size, width))] * 4
        + [
            pl.BlockSpec((width, TILE), lambda j: (0, j)),
            pl.BlockSpec((width, TILE), lambda j: (0, j)),
            pl.BlockSpec((TILE, width), lambda j: (j, 0)),
        ],
        [full((rows // 2, width)), column, column] + sent_chunks(rows, width)[0],
        [
            jax.ShapeDtypeStruct((rows // 2, width), F32),
            jax.ShapeDtypeStruct((rows, wide), BF),
            jax.ShapeDtypeStruct((rows, wide), BF),
        ]
        + sent_chunks(rows, width)[1],
        [pltpu.VMEM((rows // 2, width), F32)],
        ties,
    )(*blocks, w_gate, w_up, w_down, *ties)


def ff_backward_body(with_old, *refs):
    block_refs = refs[:4]
    g_ref, u_ref, wg_ref, wu_ref, wd_ref = refs[4:9]
    old_refs = refs[9:11] if with_old else None
    (
        own_ref, dg_ref, du_ref, dl_ref, dr_ref, *sent_refs, hidden_ref, other_ref, gg_ref,
    ) = refs[11 if with_old else 9 :]
    size = block_refs[0].shape[0]
    rows = 4 * size

    @pl.when(pl.program_id(0) == 0)
    def _():
        own_ref[...] = jnp.zeros_like(own_ref)
        other_ref[...] = jnp.zeros_like(other_ref)
        for number, block_ref in enumerate(block_refs):
            gg_ref[number * size : (number + 1) * size] = block_ref[...]

    wg, wu, wd = wg_ref[...], wu_ref[...], wd_ref[...]
    for start in range(0, rows, size):
        part = slice(start, start + size)
        grad = matmul_nt(gg_ref[part], wd)
        gate = g_ref[part].astype(F32)
        up = u_ref[part].astype(F32)
        square = gate * gate
        bent = jnp.tanh(INNER * (gate + CUBIC * (square * gate)))
        half = 0.5 * (1.0 + bent)
        gelu = gate * half
        slope = half + (0.5 * INNER) * gate * (1.0 - bent * bent) * (1.0 + (3.0 * CUBIC) * square)
        hidden_ref[part] = rounded(gelu * up)
        grad_gate = rounded(grad * up * slope)
        grad_up = rounded(grad * gelu)
        dg_ref[part] = grad_gate
        du_ref[part] = grad_up
        add_rows(
            start, size, matmul_nt(grad_gate, wg) + matmul_nt(grad_up, wu), own_ref, other_ref
        )
    total = matmul_tn(hidden_ref[...], gg_ref[...])
    left = dl_ref.shape[1]
    for number, (out_ref, part) in enumerate(((dl_ref, total[:, :left]), (dr_ref, total[:, left:]))):
        if old_refs is not None:
            part = part + old_refs[number][...].astype(F32)
        out_ref[...] = rounded(part)

    @pl.when(pl.program_id(0) == pl.num_programs(0) - 1)
    def _():
        send_rows(other_ref, sent_refs)


def ff_backward(blocks, gate, up, w_gate, w_up, w_down, old, ties=()):
    size, width = blocks[0].shape
    rows = 4 * size
    wide = w_gate.shape[1]
    left = left_columns(width)
    column = pl.BlockSpec((rows, TILE), lambda j: (0, j))
    halves = [pl.BlockSpec((TILE, cols), lambda j: (j, 0)) for cols in (left, width - left)]
    in_specs = [full((size, width))] * 4 + [
        column,
        column,
        pl.BlockSpec((width, TILE), lambda j: (0, j)),
        pl.BlockSpec((width, TILE), lambda j: (0, j)),
        pl.BlockSpec((TILE, width), lambda j: (j, 0)),
    ]
    operands = [*blocks, gate, up, w_gate, w_up, w_down]
    if old is not None:
        in_specs += halves
        operands += list(old)
    return kernel_call(
        functools.partial(ff_backward_body, old is not None),
        (wide // TILE,),
        in_specs,
        [full((rows // 2, width)), column, column] + halves + sent_chunks(rows, width)[0],
        [
            jax.ShapeDtypeStruct((rows // 2, width), F32),
            jax.ShapeDtypeStruct((rows, wide), BF),
            jax.ShapeDtypeStruct((rows, wide), BF),
            jax.ShapeDtypeStruct((wide, left), BF),
            jax.ShapeDtypeStruct((wide, width - left), BF),
        ]
        + sent_chunks(rows, width)[1],
        [
            pltpu.VMEM((rows, TILE), BF),
            pltpu.VMEM((rows // 2, width), F32),
            pltpu.VMEM((rows, width), BF),
        ],
        ties,
    )(*operands, *ties)


def ff_weights_body(with_old, *refs):
    x_refs = refs[:4]
    dg_ref, du_ref = refs[4:6]
    old_refs = refs[6:8] if with_old else (None, None)
    wg_ref, wu_ref, turned_ref = refs[8 if with_old else 6 :]
    size = x_refs[0].shape[0]

    @pl.when(pl.program_id(0) == 0)
    def _():
        for number, x_ref in enumerate(x_refs):
            turned_ref[:, number * size : (number + 1) * size] = x_ref[...].T

    for grad_ref, old_ref, out_ref in (
        (dg_ref, old_refs[0], wg_ref),
        (du_ref, old_refs[1], wu_ref),
    ):
        total = matmul(turned_ref[...], grad_ref[...])
        if old_ref is not None:
            total = total + old_ref[...].astype(F32)
        out_ref[...] = rounded(total)


def ff_weights(blocks, grad_gate, grad_up, old, ties=()):
    size, width = blocks[0].shape
    rows = 4 * size
    wide = grad_gate.shape[1]
    column = pl.BlockSpec((rows, TILE), lambda j: (0, j))
    block = pl.BlockSpec((width, TILE), lambda j: (0, j))
    operands = [*blocks, grad_gate, grad_up] + (list(old) if old is not None else [])
    return kernel_call(
        functools.partial(ff_weights_body, old is not None),
        (wide // TILE,),
        [full((size, width))] * 4
        + [column, column]
        + ([block, block] if old is not None else []),
        [block, block],
        [jax.ShapeDtypeStruct((width, wide), BF)] * 2,
        [pltpu.VMEM((width, rows), BF)],
        ties,
    )(*operands, *ties)


def stack_body(plan, *refs):
    out_at = sum(count for count, pick, columns in plan)
    at = 0
    for count, pick, columns in plan:
        group = refs[at : at + count]
        at += count
        for column in columns:
            out_ref = refs[out_at]
            out_at += 1
            for index, ref in enumerate(group):
                place = () if pick is None else (pick,)
                value = ref[place + (Ellipsis, column)]
                if count == 1:
                    out_ref[...] = value
                else:
                    out_ref[index] = value


def stack(items, ties=()):
    plan = []
    outs = []
    operands = []
    for parts, pick, widths in items:
        extent = parts[0].shape if pick is None else parts[0].shape[1:]
        widths = widths or [extent[-1]]
        if len(parts) > 1:
            extent = (len(parts),) + extent
        columns = []
        start = 0
        for columns_wide in widths:
            columns.append(slice(start, start + columns_wide))
            start += columns_wide
            outs.append(jax.ShapeDtypeStruct(extent[:-1] + (columns_wide,), parts[0].dtype))
        plan.append((len(parts), pick, columns))
        operands += parts
    return whole_call(functools.partial(stack_body, plan), outs, None, operands, ties)


def fold_body(plan, coords_ref, *refs):
    at = 0
    out_at = sum(count for item in plan for count in item["counts"])
    for item in plan:
        names, stage, size = item["names"], item["stage"], item["size"]
        outs = refs[out_at : out_at + size]
        out_at += size
        position = names.index(stage)
        own = coords_ref[NAMES.index(stage)]
        rest = [range(extent) for number, extent in enumerate(item["extent"]) if number != position]
        column = 0
        for count in item["counts"]:
            group = refs[at : at + count]
            at += count
            rows, cols = group[0].shape[-2:]
            for mask in range(size):
                for index in itertools.product(*rest):
                    source = index[:position] + (own ^ mask,) + index[position:]
                    if count == 1:
                        value = group[0][source]
                    else:
                        value = group[0][source].astype(F32)
                        for other in group[1:]:
                            value = value + other[source].astype(F32)
                        value = rounded(value)
                    out = outs[mask]
                    out[index + (slice(0, rows), slice(column, column + cols))] = value
                    if rows < out.shape[-2]:
                        out[index + (slice(rows, None), slice(column, column + cols))] = jnp.zeros(
                            (out.shape[-2] - rows, cols), out.dtype
                        )
            column += cols


def fold(grid, coordinates, items, ties=()):
    plan = []
    outs = []
    operands = []
    for names, stage, groups in items:
        rows = max(group[0].shape[-2] for group in groups)
        cols = sum(group[0].shape[-1] for group in groups)
        left = tuple(name for name in names if name != stage)
        size = grid.sizes[stage]
        plan.append(
            {
                "names": names,
                "stage": stage,
                "size": size,
                "extent": grid.extent(names),
                "counts": [len(group) for group in groups],
            }
        )
        outs += [jax.ShapeDtypeStruct(grid.extent(left) + (rows, cols), BF)] * size
        for group in groups:
            operands += [
                value.reshape(grid.extent(names) + value.shape[-2:]) for value in group
            ]
    results = whole_call(
        functools.partial(fold_body, plan), outs, coordinates, operands, ties
    )
    folded = []
    at = 0
    for names, stage, groups in items:
        size = grid.sizes[stage]
        kept = [results[at]] + [
            grid.permute(results[at + mask], {stage: mask}) for mask in range(1, size)
        ]
        folded.append((tuple(name for name in names if name != stage), kept))
        at += size
    return folded


def pair_body(own_ref, *refs):
    came_refs, (own_out, sent_out) = refs[:-2], refs[-2:]
    count = own_out.shape[0]
    step = came_refs[0].shape[0]
    for number, came_ref in enumerate(came_refs):
        start = number * step
        total = own_ref[start : start + step] + came_ref[...].astype(F32)
        if start < count:
            own_out[start : start + step] = total
        else:
            sent_out[start - count : start - count + step] = rounded(total)


def tokens_out(grid, own, sent, ties=()):
    came = [grid.permute(part, {"c": 1}) for part in sent]
    count, width = own.shape[0] // 2, own.shape[1]
    own, sent = whole_call(
        pair_body, [shape(count, width, F32), shape(count, width)], None, [own, *came], ties
    )
    return own, grid.permute(sent, {"h": 1})


def fetch(coords_ref, refs, order, block, place):
    index = 0
    for number, stride in order[:-1]:
        index = index + (coords_ref[number] ^ block[number]) * stride
    last = order[-1][0]
    side = coords_ref[last] ^ block[last]
    value = refs[-1][(index,) + place]
    for number in range(len(refs) - 1):
        value = jnp.where(side == number, refs[number][(index,) + place], value)
    return value


def quarter_of(coords_ref):
    return coords_ref[3] * 2 + coords_ref[4]


def cut_body(groups, block, block_up, coords_ref, w_ref, *refs):
    out_refs, held_ref = refs[:-1], refs[-1]
    own = quarter_of(coords_ref)
    held_ref[...] = jnp.zeros_like(held_ref)
    for quarter in range(4):
        slot = own ^ quarter
        for kind in range(2):
            for group in range(groups):
                at = kind * groups * 4 * block + (group * 4 + quarter) * block
                held_ref[slot, kind, :, group * block_up : group * block_up + block] = w_ref[
                    :, at : at + block
                ]
    for mask, out_ref in enumerate(out_refs):
        out_ref[...] = held_ref[mask]


def pick_of(own, refs, quarter):
    value = refs[3]
    for mask in range(3):
        value = jnp.where(own == quarter ^ mask, refs[mask], value)
    return value


def pieces_body(coords_ref, p0_ref, p1_ref, p2_ref, p3_ref, out_ref):
    own = quarter_of(coords_ref)
    rows = p0_ref.shape[1]
    for kind in range(2):
        refs = [ref[kind] for ref in (p0_ref, p1_ref, p2_ref, p3_ref)]
        for quarter in range(4):
            out_ref[kind, quarter * rows : (quarter + 1) * rows] = pick_of(own, refs, quarter)


def split_body(count, coords_ref, *refs):
    own = quarter_of(coords_ref)
    outs = refs[2 * count :]
    rows = outs[0].shape[1]
    for kind in range(2):
        total = refs[kind * count][...].astype(F32)
        for ref in refs[kind * count + 1 : (kind + 1) * count]:
            total = total + ref[...].astype(F32)
        total = rounded(total)
        for mask, out_ref in enumerate(outs):
            value = total[3 * rows :]
            for quarter in range(3):
                value = jnp.where(
                    own == quarter ^ mask, total[quarter * rows : (quarter + 1) * rows], value
                )
            out_ref[kind] = value


def join_body(groups, block, block_up, coords_ref, p0_ref, p1_ref, p2_ref, p3_ref, out_ref):
    own = quarter_of(coords_ref)
    for kind in range(2):
        refs = [ref[kind] for ref in (p0_ref, p1_ref, p2_ref, p3_ref)]
        for quarter in range(4):
            piece = pick_of(own, refs, quarter).astype(F32)
            for group in range(groups):
                at = kind * groups * 4 * block + (group * 4 + quarter) * block
                out_ref[:, at : at + block] = piece[
                    :, group * block_up : group * block_up + block
                ]


def order_body(blocks, orders, coords_ref, *refs):
    out_ref = refs[-1]
    count = (len(refs) - 1) // len(orders)
    at = 0
    for group, order in enumerate(orders):
        group_refs = refs[group * count : (group + 1) * count]
        rows, cols = group_refs[0].shape[1:]
        for number, block in enumerate(blocks):
            out_ref[number * rows : (number + 1) * rows, at : at + cols] = fetch(
                coords_ref, group_refs, order, block, (slice(None), slice(None))
            )
        at += cols


def in_order(grid, coordinates, *columns, ties=()):
    blocks = grid.blocks_of("pxy")
    orders = []
    flat = []
    count = max(len(parts) for parts, names in columns)
    for parts, names in columns:
        parts = [part.reshape((-1,) + part.shape[-2:]) for part in parts]
        order = grid.order(names)
        if len(parts) < count:
            parts = [jnp.concatenate(parts)]
            parts += parts * (count - 1)
            order = order + ((order[-1][0], -1),)
        flat += parts
        orders.append(order)
    rows = flat[0].shape[1]
    cols = sum(parts[0].shape[-1] for parts, names in columns)
    return whole_call(
        functools.partial(order_body, blocks, tuple(orders)),
        jax.ShapeDtypeStruct((grid.groups * rows, cols), flat[0].dtype),
        coordinates,
        flat,
        ties,
    )


def spread_body(sizes, coords_ref, normed_ref, low_ref, mixed_ref, side_ref, *refs):
    own_ref, sent_ref, held_ref = refs
    devices, qkv, joined, lift, lift_at, out, mixed, last, last_at = sizes
    held_ref[...] = jnp.zeros_like(held_ref)
    second = devices // 2 * joined
    for number in range(devices):
        core, place = number % 2, number // 2
        at = place * joined
        held_ref[core, :, at : at + qkv] = normed_ref[:, number * qkv : (number + 1) * qkv]
        at = at + lift_at
        held_ref[core, :, at : at + lift] = low_ref[:, number * lift : (number + 1) * lift]
        at = second + place * mixed
        held_ref[core, :, at : at + out] = mixed_ref[:, number * out : (number + 1) * out]
        at = at + last_at
        held_ref[core, :, at : at + last] = side_ref[:, number * last : (number + 1) * last]
    own_ref[...] = held_ref[coords_ref[4]]
    sent_ref[...] = held_ref[1 - coords_ref[4]]


def unpack_first_body(blocks, order, sizes, count, coords_ref, *refs):
    chunks = [refs[at : at + count] for at in range(0, len(refs) - 4, count)]
    w_ref, lift_ref, down_ref, gain_ref = refs[-4:]
    rows, rows_up, lift_rows, gain_cols = sizes
    gain_ref[...] = jnp.zeros_like(gain_ref)
    main = slice(0, rows)
    lift = slice(rows_up, rows_up + lift_rows)
    every = slice(None)
    for number, block in enumerate(blocks):
        place = slice(number * rows, (number + 1) * rows)
        lift_place = slice(number * lift_rows, (number + 1) * lift_rows)
        at = 0
        for chunk in chunks[:-1]:
            columns = slice(at, at + chunk[0].shape[-1])
            w_ref[place, columns] = fetch(coords_ref, chunk, order, block, (main, every))
            lift_ref[lift_place, columns] = fetch(coords_ref, chunk, order, block, (lift, every))
            at = columns.stop
        down_ref[place, :] = fetch(coords_ref, chunks[-1], order, block, (main, every))
        gain_ref[0:2, number * gain_cols : (number + 1) * gain_cols] = fetch(
            coords_ref,
            chunks[-1],
            order,
            block,
            (slice(rows_up, rows_up + 2), slice(0, gain_cols)),
        ).astype(F32)


def unpack_second_body(blocks, order, sizes, count, coords_ref, *refs):
    chunks = [refs[at : at + count] for at in range(0, len(refs) - 5, count)]
    out_ref, lift0_ref, lift1_ref, down_ref, late_ref = refs[-5:]
    rows, rows_up, lift_rows, lift_up, late_rows, late_up = sizes
    every = slice(None)
    main = slice(0, rows)
    fold_cols = chunks[-1][0].shape[-1]
    for number, block in enumerate(blocks):

        def get(chunk, start, size):
            return fetch(coords_ref, chunk, order, block, (slice(start, start + size), every))

        place = slice(number * rows, (number + 1) * rows)
        lift_place = slice(number * lift_rows, (number + 1) * lift_rows)
        at = 0
        for chunk in chunks[:-2]:
            columns = slice(at, at + chunk[0].shape[-1])
            out_ref[place, columns] = get(chunk, 0, rows)
            lift0_ref[lift_place, columns] = get(chunk, rows_up, lift_rows)
            lift1_ref[lift_place, columns] = get(chunk, rows_up + lift_up, lift_rows)
            at = columns.stop
        down_ref[place, :] = get(chunks[-2], 0, rows)
        late_place = slice(number * late_rows, (number + 1) * late_rows)
        for part in range(late_ref.shape[1] // fold_cols):
            late_ref[late_place, part * fold_cols : (part + 1) * fold_cols] = get(
                chunks[-1], part * late_up, late_rows
            )


def rotate(values, cosine_table, sine_table):
    halfway = values.shape[-1] // 2
    first_half = values[..., :halfway]
    second_half = values[..., halfway:]
    return jnp.concatenate(
        [
            first_half * cosine_table - second_half * sine_table,
            second_half * cosine_table + first_half * sine_table,
        ],
        axis=-1,
    )


def inverse_size(values):
    return lax.rsqrt(jnp.mean(values * values, axis=-1, keepdims=True) + EPS)


def norm_back(values, gain_row, grad):
    inverse = inverse_size(values)
    weighted = grad * gain_row
    inner = jnp.mean(weighted * values, axis=-1, keepdims=True)
    gain_grad = jnp.sum(grad * values * inverse, axis=0, keepdims=True)
    return inverse * weighted - values * (inverse * inverse * inverse) * inner, gain_grad


def shape(rows, cols, kind=BF):
    return jax.ShapeDtypeStruct((rows, cols), kind)


def pack_body(
    sizes, wq_ref, qd_ref, ql_ref, gain_ref, wo_ref, od_ref, ol_ref, first_ref, second_ref
):
    qkv_up, ql_up, out_up, ol_up = sizes
    for ref in (first_ref, second_ref):
        ref[...] = jnp.zeros_like(ref)
    rows, cols = wq_ref.shape
    lift_rows = ql_ref.shape[1]
    rank = qd_ref.shape[2]
    first_ref[:rows, :cols] = wq_ref[...]
    first_ref[qkv_up : qkv_up + lift_rows, :cols] = ql_ref[0]
    for loop in range(2):
        at = cols + loop * rank
        first_ref[:rows, at : at + rank] = qd_ref[loop]
    first_ref[qkv_up : qkv_up + 2, cols : cols + gain_ref.shape[1]] = gain_ref[...]
    rows, width = wo_ref.shape
    last_rows = ol_ref.shape[1]
    second_ref[:rows, :width] = wo_ref[...]
    for loop in range(2):
        at = out_up + loop * ol_up
        second_ref[at : at + last_rows, :width] = ol_ref[loop]
        at = width + loop * rank
        second_ref[:rows, at : at + rank] = od_ref[loop]
    for part in range(cols // rank):
        second_ref[part * ql_up : part * ql_up + lift_rows, width + 2 * rank :] = ql_ref[
            1, :, part * rank : (part + 1) * rank
        ]


def halves_body(w_ref, left_ref, right_ref):
    rows = w_ref.shape[0]
    left = left_ref.shape[1]
    for ref in (left_ref, right_ref):
        ref[...] = jnp.zeros_like(ref)
    left_ref[:rows] = w_ref[:, :left]
    right_ref[:rows] = w_ref[:, left:]


def project_kv_body(first_loop, addends, *refs):
    add_refs = refs[:addends]
    gain_ref, qd_ref, w_ref, ql_ref, cos_ref, sin_ref = refs[addends : addends + 6]
    kv_ref, normed_ref, low_ref, residual_ref = refs[addends + 6 :]
    rank = low_ref.shape[1]
    width_q = w_ref.shape[1] - 2 * HD
    values = add_refs[0][...].astype(F32)
    for ref in add_refs[1:]:
        values = values + ref[...].astype(F32)
    residual_ref[...] = values
    normed = rounded(values * inverse_size(values) * gain_ref[0:1])
    normed_ref[...] = normed
    down = qd_ref[:, :rank] if first_loop else qd_ref[:, rank:]
    low = rounded(matmul(normed, down))
    low_ref[...] = low
    kv = matmul(normed, w_ref[:, width_q:]) + matmul(low, ql_ref[:, width_q:])
    kv_ref[:, :HD] = rounded(rotate(kv[:, :HD], cos_ref[...], sin_ref[...]))
    kv_ref[:, HD:] = rounded(kv[:, HD:])


def project_q_body(normed_ref, low_ref, w_ref, ql_ref, cos_ref, sin_ref, q_ref):
    for head in range(H):
        at = slice(head * HD, (head + 1) * HD)
        part = matmul(normed_ref[...], w_ref[:, at]) + matmul(low_ref[...], ql_ref[:, at])
        q_ref[:, at] = rounded(rotate(part, cos_ref[...], sin_ref[...]) * HD ** (-0.5))


def mask_of(segs_ref, places_ref, row_ref):
    seq_len = row_ref.shape[1]
    key_places = lax.broadcasted_iota(jnp.int32, (segs_ref.shape[0], seq_len), 1)
    allowed = (segs_ref[...] == row_ref[...]) & (key_places <= places_ref[...])
    return jnp.where(allowed, 0.0, NEG)


def attend_body(q_ref, kv_ref, segs_ref, places_ref, row_ref, mixed_ref, log_ref):
    mask = mask_of(segs_ref, places_ref, row_ref)
    for head in range(H):
        at = slice(head * HD, (head + 1) * HD)
        scores = matmul_nt(q_ref[:, at], kv_ref[:, :HD]) + mask
        top = jnp.max(scores, axis=1, keepdims=True)
        probabilities = jnp.exp(scores - top)
        total = jnp.sum(probabilities, axis=1, keepdims=True)
        mixed_ref[:, at] = rounded(matmul(rounded(probabilities), kv_ref[:, HD:]) / total)
        log_ref[head] = top + jnp.log(total)


def attend_back_body(
    q_ref, kv_ref, segs_ref, places_ref, row_ref, log_ref, grad_ref, cos_ref, sin_ref,
    coords_ref, own_ref, sent_ref, gq_ref, keys_ref, values_ref,
):
    mask = mask_of(segs_ref, places_ref, row_ref)
    size = own_ref.shape[1]
    for head in range(H):
        at = slice(head * HD, (head + 1) * HD)
        queries = q_ref[:, at]
        grad = grad_ref[:, at]
        probabilities = jnp.exp(matmul_nt(queries, kv_ref[:, :HD]) + mask - log_ref[head])
        grad_probs = matmul_nt(grad, kv_ref[:, HD:])
        weighted = probabilities * grad_probs
        delta = jnp.sum(weighted, axis=1, keepdims=True)
        grad_scores = rounded(weighted - probabilities * delta)
        grad_q = matmul(grad_scores, kv_ref[:, :HD])
        gq_ref[:, at] = rounded(rotate(grad_q, cos_ref[...], -sin_ref[...]) * HD ** (-0.5))
        key_term = matmul_tn(grad_scores, queries)
        value_term = matmul_tn(rounded(probabilities), grad)
        if head == 0:
            keys_ref[...] = key_term
            values_ref[...] = value_term
        else:
            keys_ref[...] += key_term
            values_ref[...] += value_term
    core = coords_ref[4]
    for number in range(own_ref.shape[0]):
        for out_ref, which in ((own_ref, core), (sent_ref, 1 - core)):
            place = pl.ds(pl.multiple_of((2 * number + which) * size, size), size)
            out_ref[number, :, :HD] = rounded(keys_ref[place, :])
            out_ref[number, :, HD:] = rounded(values_ref[place, :])


def leave_body(
    first_loop, mixed_ref, od_ref, w_ref, ol_ref, residual_ref, gain_ref,
    side_ref, middle_ref, normed_ref,
):
    rank = side_ref.shape[1]
    down = od_ref[:, :rank] if first_loop else od_ref[:, rank:]
    side = rounded(matmul(mixed_ref[...], down))
    side_ref[...] = side
    middle = residual_ref[...] + (matmul(mixed_ref[...], w_ref[...]) + matmul(side, ol_ref[...]))
    middle_ref[...] = middle
    normed_ref[...] = rounded(middle * inverse_size(middle) * gain_ref[1:2])


def enter_back_body(
    first_loop, own_ref, other_ref, result_ref, middle_ref, gain_ref, w_ref, ol_ref, od_ref,
    grad_ref, branch_ref, side_ref, mixed_ref, gain_grad_ref,
):
    rank = side_ref.shape[1]
    grad_normed = own_ref[...] + other_ref[...].astype(F32)
    back, gain_grad = norm_back(middle_ref[...], gain_ref[1:2], grad_normed)
    gain_grad_ref[...] = jnp.broadcast_to(gain_grad, gain_grad_ref.shape)
    grad = result_ref[...].astype(F32) + back
    grad_ref[...] = grad
    branch = rounded(grad)
    branch_ref[...] = branch
    side = rounded(matmul_nt(branch, ol_ref[...]))
    side_ref[...] = side
    down = od_ref[:, :rank] if first_loop else od_ref[:, rank:]
    mixed_ref[...] = rounded(matmul_nt(branch, w_ref[...]) + matmul_nt(side, down))


def rope_back_body(count, *refs):
    gq_ref, ql_ref, cos_ref, sin_ref, out_ref, low_ref = refs[count:]
    width_q = gq_ref.shape[1]
    kv = refs[0][...].astype(F32)
    for ref in refs[1:count]:
        kv = kv + ref[...].astype(F32)
    keys = rounded(rotate(kv[:, :HD], cos_ref[...], -sin_ref[...]))
    values = rounded(kv[:, HD:])
    out_ref[:, :HD] = keys
    out_ref[:, HD:] = values
    low_ref[...] = rounded(
        matmul_nt(gq_ref[...], ql_ref[:, :width_q])
        + matmul_nt(keys, ql_ref[:, width_q : width_q + HD])
        + matmul_nt(values, ql_ref[:, width_q + HD :])
    )


def leave_back_body(
    first_loop, kv_ref, gq_ref, low_ref, w_ref, qd_ref, residual_ref, gain_ref, grad_ref,
    other_gain_ref, *refs,
):
    out_ref, out_b_ref, gain_grad_ref = refs[-3:]
    rank = low_ref.shape[1]
    width_q = gq_ref.shape[1]
    down = qd_ref[:, :rank] if first_loop else qd_ref[:, rank:]
    grad_normed = (
        matmul_nt(gq_ref[...], w_ref[:, :width_q])
        + matmul_nt(kv_ref[...], w_ref[:, width_q:])
        + matmul_nt(low_ref[...], down)
    )
    back, gain_grad = norm_back(residual_ref[...], gain_ref[0:1], grad_normed)
    gain_grad_ref[0:1] = gain_grad
    gain_grad_ref[1:2] = other_gain_ref[1:2]
    if len(refs) > 3:
        gain_grad_ref[0:2] += refs[0][0:2]
    grad = grad_ref[...] + back
    out_ref[...] = grad
    out_b_ref[...] = rounded(grad)


def late_body(sizes, coords_ref, kv_ref, qd_ref, *refs):
    count, rows, gain_cols = sizes
    gain_refs, out_ref = refs[:-1], refs[-1]
    kv_cols = kv_ref.shape[2]
    out_ref[:, :, :kv_cols] = kv_ref[...]
    out_ref[:, :, kv_cols:] = qd_ref[...]
    for row in range(2):
        gains = rounded(gain_refs[0][row : row + 1] + gain_refs[1][row : row + 1])
        for number in range(count):
            at = 2 * number * gain_cols
            value = jnp.where(
                coords_ref[4] == 0,
                gains[:, at : at + gain_cols],
                gains[:, at + gain_cols : at + 2 * gain_cols],
            )
            out_ref[number, rows + row : rows + row + 1, kv_cols : kv_cols + gain_cols] = value


def down_body(count, *refs):
    out_ref = refs[-1]
    at = 0
    for group in range(2):
        value = refs[group * count][...].astype(F32)
        for ref in refs[group * count + 1 : (group + 1) * count]:
            value = value + ref[...].astype(F32)
        out_ref[:, at : at + value.shape[1]] = value[: out_ref.shape[0]]
        at += value.shape[1]


def result_body(middle_ref, own_ref, other_ref, out_ref):
    out_ref[...] = rounded(middle_ref[...] + (own_ref[...] + other_ref[...].astype(F32)))


def finish_body(count, sizes, *refs):
    rows, rows_up, lift_rows, lift_up, out_rows, out_up, last_rows, last_up, gain_cols = sizes
    totals = []
    for group in range(3):
        value = refs[group * count][...].astype(F32)
        for ref in refs[group * count + 1 : (group + 1) * count]:
            value = value + ref[...].astype(F32)
        totals.append(value)
    outs, queries, late = totals
    gains_ref, qkv_ref, out_ref, qd_ref, ql_ref, od_ref, ol_ref = refs[3 * count :]
    width = out_ref.shape[1]
    rank = qd_ref.shape[2]
    half = queries.shape[1] - rank
    rest = qkv_ref.shape[1] - half
    gains_ref[...] = late[rows : rows + 2, rest : rest + gain_cols]
    qkv_ref[:, :half] = queries[:rows, :half]
    qkv_ref[:, half:] = late[:rows, :rest]
    out_ref[...] = outs[:out_rows, :width]
    qd_ref[0] = late[:rows, rest:]
    qd_ref[1] = queries[:rows, half:]
    for loop in range(2):
        at = rows_up + loop * lift_up
        ql_ref[loop, :, :half] = queries[at : at + lift_rows, :half]
        ql_ref[loop, :, half:] = late[at : at + lift_rows, :rest]
        at = width + loop * rank
        od_ref[loop] = outs[:out_rows, at : at + rank]
        at = out_up + loop * last_up
        ol_ref[loop] = outs[at : at + last_rows, :width]


def outer_body(columns, rights, olds, own_ref, came_ref, *refs):
    out_refs = refs[2 * rights + olds :]
    own, came = own_ref[:, columns], came_ref[:, columns]
    for number in range(rights):
        right_ref, right_came_ref = refs[2 * number], refs[2 * number + 1]
        out_ref = out_refs[number]
        cols = out_ref.shape[1]
        step = 512 if cols % 512 == 0 else 384 if cols % 384 == 0 else cols
        for start in range(0, cols, step):
            part = slice(start, start + step)
            total = matmul_tn(own, right_ref[:, part]) + matmul_tn(came, right_came_ref[:, part])
            if number < olds:
                total = total + refs[2 * rights + number][:, part].astype(F32)
            out_ref[:, part] = rounded(total)


def outer(left, columns, rights, olds=(), ties=()):
    rows = columns.stop - columns.start
    return whole_call(
        functools.partial(outer_body, columns, len(rights), len(olds)),
        [shape(rows, right[0].shape[1]) for right in rights],
        None,
        [*left, *[value for right in rights for value in right], *olds],
        ties,
    )


def per_device(
    grid,
    inputs,
    segments,
    cotangent,
    norm_gain_rows,
    query_key_value_weight,
    output_weight,
    gate_up_weight,
    down_weight,
    adapter_query_down,
    adapter_query_lift,
    adapter_output_down,
    adapter_output_lift,
):
    tokens = inputs.shape[0]
    width = inputs.shape[1]
    groups = grid.groups
    gain_cols = norm_gain_rows.shape[1]
    qkv_rows = query_key_value_weight.shape[0]
    out_rows = output_weight.shape[0]
    ql_rows = adapter_query_lift.shape[1]
    ol_rows = adapter_output_lift.shape[1]
    rank = adapter_query_down.shape[2]
    hidden_block = down_weight.shape[0]
    width_q = H * HD

    qkv_up, ql_up = up8(qkv_rows), up8(ql_rows)
    out_up, ol_up = up8(out_rows), up8(ol_rows)
    wide = -(-groups * hidden_block // TILE) * TILE
    block_up = wide // groups
    qkv_cols = query_key_value_weight.shape[1]
    left_cols = left_columns(width)
    coordinates = grid.coordinates()
    straight = ("p", "h", "x", "y", "c")
    turned = ("p", "h", "y", "x", "c")

    def flat(parts):
        return [part.reshape((-1,) + part.shape[-2:]) for part in parts]

    def parts(values, name):
        return grid.parts(values, name)

    segrow = segments[0]
    seq_len = segrow.shape[0]
    position = lax.axis_index("blk")
    places = position * tokens + jnp.arange(tokens, dtype=jnp.int32)
    own_segs = lax.dynamic_slice_in_dim(segrow, position * tokens, tokens, 0)
    below_one = jnp.sum((segrow < 1).astype(jnp.int32))
    below_two = jnp.sum((segrow < 2).astype(jnp.int32))
    starts = jnp.where(own_segs == 0, 0, jnp.where(own_segs == 1, below_one, below_two))
    offsets = (places - starts).astype(F32)
    frequency = jnp.exp(jnp.arange(HD // 2, dtype=F32) * (-2.0 * math.log(ROPE_BASE) / HD))
    angles = offsets[:, None] * frequency[None, :]
    tables = [jnp.cos(angles), jnp.sin(angles)]
    masks = [own_segs[:, None], places[:, None], segments]

    second_rows = max(out_up + 2 * ol_up, qkv_cols // rank * ql_up)
    first, second = whole_call(
        functools.partial(pack_body, (qkv_up, ql_up, out_up, ol_up)),
        [shape(qkv_up + ql_up, qkv_cols + 2 * rank), shape(second_rows, width + 3 * rank)],
        None,
        [
            query_key_value_weight, adapter_query_down, adapter_query_lift, norm_gain_rows,
            output_weight, adapter_output_down, adapter_output_lift,
        ],
    )
    first, second = stack([(parts(first, "p"), None, None), (parts(second, "p"), None, None)])
    cut = whole_call(
        functools.partial(cut_body, groups, hidden_block, block_up),
        [jax.ShapeDtypeStruct((2, qkv_rows, wide), BF)] * 4,
        coordinates,
        [gate_up_weight],
        [first],
        [pltpu.VMEM((4, 2, qkv_rows, wide), BF)],
    )
    down_left, down_right = whole_call(
        halves_body,
        [shape(block_up, left_cols), shape(block_up, width - left_cols)],
        None,
        [down_weight],
        [cut[0]],
    )
    first, second = stack(
        [(parts(first, "h"), None, None), (parts(second, "h"), None, None)], [down_left]
    )
    gate_up = whole_call(
        pieces_body,
        jax.ShapeDtypeStruct((2, 4 * qkv_rows, wide), BF),
        coordinates,
        [
            cut[0],
            grid.permute(cut[1], {"c": 1}),
            grid.permute(cut[2], {"h": 1}),
            grid.permute(cut[3], {"h": 1, "c": 1}),
        ],
        [first],
    )
    first, second = stack(
        [(parts(first, "x"), None, None), (parts(second, "y"), None, None)], [gate_up]
    )
    gate_up = parts(gate_up, "p")
    first_chunks = [qkv_cols // 3] * 3 + [2 * rank]
    second_chunks = [width - left_cols, left_cols, 2 * rank, rank]
    chunks = stack(
        [
            (parts(first, "y"), None, first_chunks),
            (parts(second, "x"), None, second_chunks),
        ]
    )
    chunks = [flat(parts(chunk, "c")) for chunk in chunks]
    first = [part for chunk in chunks[:4] for part in chunk]
    second = [part for chunk in chunks[4:] for part in chunk]
    gate, up, down_left, down_right = stack(
        [
            (gate_up, 0, None),
            (gate_up, 1, None),
            ([down_left], None, None),
            ([down_right], None, None),
        ],
        [chunks[0][0]],
    )
    gate, up = parts(gate, "x"), parts(up, "y")
    down_left, down_right = parts(down_left, "p"), parts(down_right, "p")
    w_qkv, ql_0, qd, gains = whole_call(
        functools.partial(
            unpack_first_body,
            grid.blocks_of(straight),
            grid.order(straight),
            (qkv_rows, qkv_up, ql_rows, gain_cols),
            2,
        ),
        [shape(width, qkv_cols), shape(rank, qkv_cols), shape(width, 2 * rank), shape(8, width, F32)],
        coordinates,
        first,
        [gate[0]],
    )
    lifts_in = [ql_0, None]

    def project_kv(addends, loop):
        own_kv, normed_b, low_rank_b, residual = whole_call(
            functools.partial(project_kv_body, loop == 0, len(addends)),
            [
                shape(tokens, 2 * HD), shape(tokens, width), shape(tokens, rank),
                shape(tokens, width, F32),
            ],
            None,
            [*addends, gains, qd, w_qkv, lifts_in[loop], *tables],
        )
        both = lax.all_gather(own_kv, "blk", axis=0, tiled=True)
        return own_kv, normed_b, low_rank_b, residual, both

    def project_q(projected, loop, ties=()):
        return whole_call(
            project_q_body,
            shape(tokens, width_q),
            None,
            [projected[1], projected[2], w_qkv, lifts_in[loop], *tables],
            ties,
        )

    def attend(queries, both, ties=()):
        return whole_call(
            attend_body,
            [shape(tokens, width_q), jax.ShapeDtypeStruct((H, tokens, 1), F32)],
            None,
            [queries, both, *masks],
            ties,
        )

    projected_one = project_kv([inputs], 0)
    queries_one = project_q(projected_one, 0)
    gate, up = stack([(gate, None, None), (up, None, None)], [queries_one])
    gate, up = parts(gate, "y"), parts(up, "x")
    w_out, ol_0, ol_1, od, ql_1 = whole_call(
        functools.partial(
            unpack_second_body,
            grid.blocks_of(straight),
            grid.order(turned),
            (out_rows, out_up, ol_rows, ol_up, ql_rows, ql_up),
            2,
        ),
        [
            shape(width_q, width), shape(rank, width), shape(rank, width),
            shape(width_q, 2 * rank), shape(rank, qkv_cols),
        ],
        coordinates,
        second,
        [gate[0]],
    )
    attended_one = attend(queries_one, projected_one[4], [w_out])
    down_left, down_right = stack(
        [(down_left, None, None), (down_right, None, None)], [attended_one[0]]
    )
    down_left, down_right = parts(down_left, "x"), parts(down_right, "y")
    lifts_in[1] = ql_1
    lifts_out = (ol_0, ol_1)

    def leave(loop, mixed_b, residual):
        return whole_call(
            functools.partial(leave_body, loop == 0),
            [shape(tokens, rank), shape(tokens, width, F32), shape(tokens, width)],
            None,
            [mixed_b, od, w_out, lifts_out[loop], residual, gains],
        )

    left_one = leave(0, attended_one[0], projected_one[3])
    ff_in_one = grid.tokens_in(left_one[2])
    down_left, down_right = stack(
        [(down_left, None, None), (down_right, None, None)], [left_one[2]]
    )
    down_left, down_right = parts(down_left, "y"), parts(down_right, "x")
    w_gate = in_order(grid, coordinates, (gate, ("p", "x", "y")))
    w_up = in_order(grid, coordinates, (up, ("p", "y", "x")))
    w_down = in_order(
        grid, coordinates, (down_left, ("p", "x", "y")), (down_right, ("p", "y", "x"))
    )

    qkv_block = qkv_up + 2 * ql_up
    out_block = out_up + 2 * ol_up

    cotangent_in = grid.tokens_in(cotangent)

    def feed_forward(loop, projected, queries, attended, left, ff_in, ties=()):
        own_kv, normed_b, low_rank_b, residual, both = projected
        mixed_b, log_total = attended
        side_b, middle, unused = left
        ff_own, gate_b, up_b, *ff_sent = ff_forward(ff_in, w_gate, w_up, w_down)
        own, other = tokens_out(grid, ff_own, ff_sent, ties)
        spread_own, spread_sent = whole_call(
            functools.partial(
                spread_body,
                (
                    grid.devices, qkv_rows, qkv_block, ql_rows, qkv_up + loop * ql_up,
                    out_rows, out_block, ol_rows, out_up + loop * ol_up,
                ),
            ),
            [shape(tokens, grid.devices // 2 * (qkv_block + out_block))] * 2,
            coordinates,
            [normed_b, low_rank_b, mixed_b, side_b],
            [gate_b],
            [pltpu.VMEM((2, tokens, grid.devices // 2 * (qkv_block + out_block)), BF)],
        )
        cache = (
            residual, (spread_own, grid.permute(spread_sent, {"c": 1})), queries, both, log_total,
            middle, ff_in, gate_b, up_b,
        )
        return [middle, own, other], cache

    addends, cache_one = feed_forward(
        0, projected_one, queries_one, attended_one, left_one, ff_in_one, [cotangent_in[1]]
    )
    projected_two = project_kv(addends, 1)
    queries_two = project_q(projected_two, 1)
    attended_two = attend(queries_two, projected_two[4])
    left_two = leave(1, attended_two[0], projected_two[3])
    addends, cache_two = feed_forward(
        1, projected_two, queries_two, attended_two, left_two, grid.tokens_in(left_two[2])
    )
    result = whole_call(result_body, shape(tokens, width), None, addends)

    group_names = ("y", "x", "p")
    names = ("y", "x", "p", "h")
    half = grid.devices // 2
    joined_columns = slice(0, half * qkv_block)
    mixed_columns = slice(half * qkv_block, half * (qkv_block + out_block))

    def step(stages, ties=()):
        return fold(
            grid, coordinates, [(item[0], stage, [item[1]]) for item, stage in stages], ties
        )

    def with_core(values):
        return values, grid.permute(values, {"c": 1})

    def backward_loop(cache, grad_result, blocks_in, loop, old):
        (
            residual, spreads, queries, both, log_total, middle, ff_in, gate_b, up_b,
        ) = cache
        last = old is not None
        ql, ol = lifts_in[loop], lifts_out[loop]

        def before(name):
            return old[name] if last else None

        def grouped(values):
            return values.reshape(groups, values.shape[0] // groups, values.shape[1])

        own, grad_gate_b, grad_up_b, *down = ff_backward(
            blocks_in, gate_b, up_b, w_gate, w_up, w_down, before("down")
        )
        down, sent = down[:2], down[2:]
        ties = [] if last else [result]
        if last:
            down = fold(
                grid,
                coordinates,
                [
                    (group_names, "x", [[grouped(down[0])]]),
                    (group_names, "y", [[grouped(down[1])]]),
                ],
            )
            ties = [down[0][1][0]]
        own, other = tokens_out(grid, own, sent, ties)
        d_gate, d_up = ff_weights(
            ff_in,
            grad_gate_b,
            grad_up_b,
            (old["gate"], old["up"]) if last else None,
            [own],
        )
        ties = [d_gate]
        if last:
            d_gate, d_up = fold(
                grid,
                coordinates,
                [
                    (group_names, "x", [[grouped(d_gate)]]),
                    (group_names, "y", [[grouped(d_up)]]),
                ],
            )
        grad_middle, grad_branch_b, grad_side_b, grad_mixed_b, gain_grad_ff = whole_call(
            functools.partial(enter_back_body, loop == 0),
            [
                shape(tokens, width, F32), shape(tokens, width), shape(tokens, rank),
                shape(tokens, width_q), shape(8, width, F32),
            ],
            None,
            [own, other, grad_result, middle, gains, w_out, ol, od],
            ties,
        )
        ties = []
        if last:
            down = fold(
                grid,
                coordinates,
                [(down[0][0], "y", [down[0][1]]), (down[1][0], "x", [down[1][1]])],
                [grad_mixed_b, d_gate[1][0]],
            )
            ties = [down[0][1][0]]
        kv_own, kv_sent, grad_queries_b = pl.pallas_call(
            tied(attend_back_body, 10, ties),
            out_shape=[jax.ShapeDtypeStruct((grid.blk // 2, tokens, 2 * HD), BF)] * 2
            + [shape(tokens, width_q)],
            in_specs=[pl.BlockSpec(memory_space=pltpu.VMEM)] * 9
            + [pl.BlockSpec(memory_space=pltpu.SMEM)]
            + [ANY] * len(ties),
            scratch_shapes=[pltpu.VMEM((seq_len, HD), F32)] * 2,
            cost_estimate=LIGHT,
            compiler_params=pltpu.CompilerParams(vmem_limit_bytes=48 * 1024 * 1024),
        )(queries, both, *masks, log_total, grad_mixed_b, *tables, coordinates, *ties)
        grad_kv = (("p", "h"), [kv_own, grid.permute(kv_sent, {"c": 1})])
        (grad_kv,) = step([(grad_kv, "h")])
        (grad_kv,) = step([(grad_kv, "p")])
        branch, side = with_core(grad_branch_b), with_core(grad_side_b)
        d_out, d_od = outer(
            spreads, mixed_columns, [branch, side], [old["out"]] if last else [], [grad_kv[1][0]]
        )
        (d_queries,) = outer(
            spreads,
            joined_columns,
            [with_core(grad_queries_b)],
            [old["queries"]] if last else [],
            [d_out],
        )
        sums = {"out": d_out, "od": d_od, "queries": d_queries}
        ties = [] if last else [d_queries, cache_one[1][1]]
        if last:
            sums["out"], sums["queries"] = fold(
                grid,
                coordinates,
                [
                    (names, "x", [[blocks(value)] for value in (d_out, d_od, old["od"])]),
                    (names, "y", [[blocks(value)] for value in (d_queries, old["qd"])]),
                ],
            )
            sums["gate"], sums["up"], down[0], down[1] = fold(
                grid,
                coordinates,
                [
                    (d_gate[0], "y", [d_gate[1]]),
                    (d_up[0], "x", [d_up[1]]),
                    (down[0][0], "p", [down[0][1]]),
                    (down[1][0], "p", [down[1][1]]),
                ],
                [sums["out"][1][0]],
            )
            ties = [sums["gate"][1][0]]
        else:
            sums["gate"], sums["up"] = d_gate, d_up
        sums["down"] = down
        grad_kv_b, grad_low_rank_b = whole_call(
            functools.partial(rope_back_body, len(grad_kv[1])),
            [shape(tokens, 2 * HD), shape(tokens, rank)],
            None,
            [*grad_kv[1], grad_queries_b, ql, *tables],
            ties,
        )
        sums["kv"], sums["qd"] = outer(
            spreads,
            joined_columns,
            [with_core(grad_kv_b), with_core(grad_low_rank_b)],
            [old["kv"]] if last else [],
        )
        following, following_b, gain_grads = whole_call(
            functools.partial(leave_back_body, loop == 0),
            [shape(tokens, width, F32), shape(tokens, width), shape(8, width, F32)],
            None,
            [
                grad_kv_b, grad_queries_b, grad_low_rank_b, w_qkv, qd, residual, gains,
                grad_middle, gain_grad_ff,
            ]
            + ([old["gains"]] if last else []),
        )
        sums["gains"] = gain_grads
        return following, following_b, sums

    def blocks(values):
        return values.reshape(half, values.shape[0] // half, values.shape[1])

    grad_one, grad_one_b, sums_two = backward_loop(cache_two, cotangent, cotangent_in, 1, None)
    grad_inputs, unused, sums = backward_loop(
        cache_one, grad_one, grid.tokens_in(grad_one_b), 0, sums_two
    )

    late = whole_call(
        functools.partial(late_body, (half, qkv_rows, gain_cols)),
        jax.ShapeDtypeStruct((half, qkv_block, 2 * HD + rank), BF),
        coordinates,
        [blocks(sums["kv"]), blocks(sums["qd"]), *with_core(sums["gains"])],
    )
    (late,) = step([((names, [late]), "x")])
    d_down = whole_call(
        functools.partial(down_body, len(sums["down"][0][1])),
        shape(hidden_block, width, F32),
        None,
        sums["down"][0][1] + sums["down"][1][1],
        [late[1][0]],
    )
    gate, up = step([(sums["gate"], "p"), (sums["up"], "p")], [d_down])
    outs, queries = step([(sums["out"], "y"), (sums["queries"], "x")], [gate[1][0]])
    (late,) = step([(late, "y")], [outs[1][0]])
    split = whole_call(
        functools.partial(split_body, len(gate[1])),
        [jax.ShapeDtypeStruct((2, qkv_rows, wide), BF)] * 4,
        coordinates,
        gate[1] + up[1],
        [late[1][0]],
    )
    back = [
        split[0],
        grid.permute(split[1], {"c": 1}),
        grid.permute(split[2], {"h": 1}),
        grid.permute(split[3], {"h": 1, "c": 1}),
    ]
    outs, queries, late = step([(outs, "h"), (queries, "h"), (late, "h")], [split[0]])
    outs, queries, late = step([(outs, "p"), (queries, "p"), (late, "p")])
    d_gate_up = whole_call(
        functools.partial(join_body, groups, hidden_block, block_up),
        shape(qkv_rows, 8 * groups * hidden_block, F32),
        coordinates,
        back,
        [late[1][0]],
    )
    last = [outs[1], queries[1], late[1]]
    d_gains, d_qkv, d_out, d_qd, d_ql, d_od, d_ol = whole_call(
        functools.partial(
            finish_body,
            len(outs[1]),
            (
                qkv_rows, qkv_up, ql_rows, ql_up, out_rows, out_up, ol_rows, ol_up, gain_cols,
            ),
        ),
        [
            shape(2, gain_cols, F32),
            shape(qkv_rows, qkv_cols, F32),
            shape(out_rows, width, F32),
            jax.ShapeDtypeStruct(adapter_query_down.shape, F32),
            jax.ShapeDtypeStruct(adapter_query_lift.shape, F32),
            jax.ShapeDtypeStruct(adapter_output_down.shape, F32),
            jax.ShapeDtypeStruct(adapter_output_lift.shape, F32),
        ],
        None,
        [value for values in last for value in values],
    )
    return (
        result, grad_inputs, d_gains, d_qkv, d_out, d_gate_up, d_down, d_qd, d_ql, d_od, d_ol,
    )


def solution(mesh):
    grid = Grid(mesh)
    rows = P(AXES, None)
    deep = P(None, AXES, None)
    in_specs = (
        rows, P("fsdp", None), rows, P(None, AXES), rows, rows, rows, rows, deep, deep, deep, deep,
    )
    out_specs = (
        rows, rows, P(None, AXES), rows, rows, rows, rows, deep, deep, deep, deep,
    )

    def run(*arguments):
        return per_device(grid, *arguments)

    return jax.shard_map(
        run, mesh=mesh, in_specs=in_specs, out_specs=out_specs, check_vma=False
    )
```

```python
import functools
import itertools
import math

import jax
import jax.numpy as jnp
from jax import lax
from jax.experimental import pallas as pl
from jax.experimental.pallas import tpu as pltpu
from jax.sharding import PartitionSpec as P

H = 4
HD = 256
EPS = 1e-06
NEG = -1e30
ROPE_BASE = 10000.0
AXES = ("fsdp", "blk")
BF = jnp.bfloat16
F32 = jnp.float32


def matmul(left_side, right_side):
    return jnp.dot(left_side, right_side, preferred_element_type=F32)


def matmul_nt(left_side, right_side):
    return lax.dot_general(
        left_side, right_side, (((1,), (1,)), ((), ())), preferred_element_type=F32
    )


def matmul_tn(left_side, right_side):
    return lax.dot_general(
        left_side, right_side, (((0,), (0,)), ((), ())), preferred_element_type=F32
    )


def rounded(values):
    return values.astype(BF)


NAMES = ("y", "x", "p", "h", "c")


class Grid:
    def __init__(self, mesh):
        self.fsdp = mesh.shape["fsdp"]
        self.blk = mesh.shape["blk"]
        self.sizes = {"y": self.fsdp // 2, "x": 2, "p": self.blk // 4, "h": 2, "c": 2}
        self.devices = self.fsdp * self.blk
        self.groups = self.devices // 4

    def places(self):
        f = lax.axis_index("fsdp")
        b = lax.axis_index("blk")
        return {"y": f // 2, "x": f % 2, "p": b // 4, "h": (b // 2) % 2, "c": b % 2}

    def coordinates(self):
        places = self.places()
        return jnp.stack([places[name] for name in NAMES]).astype(jnp.int32)

    def permute(self, values, masks):
        pairs = []
        for f in range(self.fsdp):
            for b in range(self.blk):
                at = {"y": f // 2, "x": f % 2, "p": b // 4, "h": (b // 2) % 2, "c": b % 2}
                for name, mask in masks.items():
                    at[name] = at[name] ^ mask
                pairs.append(
                    (
                        f * self.blk + b,
                        (at["y"] * 2 + at["x"]) * self.blk + at["p"] * 4 + at["h"] * 2 + at["c"],
                    )
                )
        return lax.ppermute(values, AXES, pairs)

    def parts(self, values, name):
        return [values] + [
            self.permute(values, {name: mask}) for mask in range(1, self.sizes[name])
        ]

    def order(self, names):
        out = []
        stride = 1
        for name in names:
            out.append((NAMES.index(name), stride))
            stride *= self.sizes[name]
        return tuple(out)

    def blocks_of(self, names):
        out = []
        for y in range(self.sizes["y"]):
            for x in range(2):
                for p in range(self.sizes["p"]):
                    for h in range(2 if "h" in names else 1):
                        for c in range(2 if "c" in names else 1):
                            out.append((y, x, p, h, c))
        return tuple(out)

    def tokens_in(self, rows):
        other = self.permute(rows, {"h": 1})
        return [rows, other, self.permute(rows, {"c": 1}), self.permute(other, {"c": 1})]

    def extent(self, names):
        return tuple(self.sizes[name] for name in names)


def up8(rows):
    return -(-rows // 8) * 8


TILE = 256
INNER = math.sqrt(2.0 / math.pi)
CUBIC = 0.044715


def chunk_of(rows):
    return min(rows, 256)


LIGHT = pl.CostEstimate(flops=0, bytes_accessed=0, transcendentals=0)


def full(extent):
    return pl.BlockSpec(extent, lambda j: tuple([0] * len(extent)))


ANY = pl.BlockSpec(memory_space=pl.ANY)


def tied(body, operands, ties):
    if not ties:
        return body

    def run(*refs):
        body(*refs[:operands], *refs[operands + len(ties) :])

    return run


def kernel_call(body, grid, in_specs, out_specs, out_shape, scratch, ties=()):
    return pl.pallas_call(
        tied(body, len(in_specs), ties),
        grid=grid,
        in_specs=in_specs + [ANY] * len(ties),
        out_specs=out_specs,
        out_shape=out_shape,
        scratch_shapes=scratch,
        cost_estimate=LIGHT,
        compiler_params=pltpu.CompilerParams(
            dimension_semantics=("arbitrary",), vmem_limit_bytes=48 * 1024 * 1024
        ),
    )


def whole_call(body, out_shape, coordinates, operands, ties=(), scratch=()):
    count = len(operands)
    specs = [pl.BlockSpec(memory_space=pltpu.VMEM)] * count
    if coordinates is not None:
        operands = [coordinates, *operands]
        specs = [pl.BlockSpec(memory_space=pltpu.SMEM)] + specs
    return pl.pallas_call(
        tied(body, len(specs), ties),
        out_shape=out_shape,
        in_specs=specs + [ANY] * len(ties),
        scratch_shapes=list(scratch),
        cost_estimate=LIGHT,
        compiler_params=pltpu.CompilerParams(vmem_limit_bytes=48 * 1024 * 1024),
    )(*operands, *ties)


def left_columns(width):
    return (width // 256) * 128 + 128


def add_rows(start, size, value, own_ref, other_ref):
    half = own_ref.shape[0]
    if start < half:
        own_ref[start : start + size] += value
    else:
        other_ref[start - half : start - half + size] += value


CHUNKS = 4


def send_rows(other_ref, sent_refs):
    count = sent_refs[0].shape[0]
    for number, sent_ref in enumerate(sent_refs):
        sent_ref[...] = rounded(other_ref[number * count : (number + 1) * count])


def sent_chunks(rows, width):
    count = rows // 2 // CHUNKS
    return [full((count, width))] * CHUNKS, [shape(count, width)] * CHUNKS


def ff_forward_body(
    x0_ref, x1_ref, x2_ref, x3_ref, wg_ref, wu_ref, wd_ref, own_ref, g_ref, u_ref, *sent_refs
):
    *sent_refs, other_ref = sent_refs
    size = x0_ref.shape[0]

    @pl.when(pl.program_id(0) == 0)
    def _():
        own_ref[...] = jnp.zeros_like(own_ref)
        other_ref[...] = jnp.zeros_like(other_ref)

    wg, wu, wd = wg_ref[...], wu_ref[...], wd_ref[...]
    for number, x_ref in enumerate((x0_ref, x1_ref, x2_ref, x3_ref)):
        start = number * size
        part = slice(start, start + size)
        x = x_ref[...]
        gate = matmul(x, wg)
        up = matmul(x, wu)
        g_ref[part] = rounded(gate)
        u_ref[part] = rounded(up)
        bent = jnp.tanh(INNER * (gate + CUBIC * (gate * gate * gate)))
        hidden = rounded(0.5 * gate * (1.0 + bent) * up)
        add_rows(start, size, matmul(hidden, wd), own_ref, other_ref)

    @pl.when(pl.program_id(0) == pl.num_programs(0) - 1)
    def _():
        send_rows(other_ref, sent_refs)


def ff_forward(blocks, w_gate, w_up, w_down, ties=()):
    size, width = blocks[0].shape
    rows = 4 * size
    wide = w_gate.shape[1]
    column = pl.BlockSpec((rows, TILE), lambda j: (0, j))
    return kernel_call(
        ff_forward_body,
        (wide // TILE,),
        [full((size, width))] * 4
        + [
            pl.BlockSpec((width, TILE), lambda j: (0, j)),
            pl.BlockSpec((width, TILE), lambda j: (0, j)),
            pl.BlockSpec((TILE, width), lambda j: (j, 0)),
        ],
        [full((rows // 2, width)), column, column] + sent_chunks(rows, width)[0],
        [
            jax.ShapeDtypeStruct((rows // 2, width), F32),
            jax.ShapeDtypeStruct((rows, wide), BF),
            jax.ShapeDtypeStruct((rows, wide), BF),
        ]
        + sent_chunks(rows, width)[1],
        [pltpu.VMEM((rows // 2, width), F32)],
        ties,
    )(*blocks, w_gate, w_up, w_down, *ties)


def ff_backward_body(with_old, *refs):
    block_refs = refs[:4]
    g_ref, u_ref, wg_ref, wu_ref, wd_ref = refs[4:9]
    old_refs = refs[9:11] if with_old else None
    (
        own_ref, dg_ref, du_ref, dl_ref, dr_ref, *sent_refs, hidden_ref, other_ref, gg_ref,
    ) = refs[11 if with_old else 9 :]
    size = block_refs[0].shape[0]
    rows = 4 * size

    @pl.when(pl.program_id(0) == 0)
    def _():
        own_ref[...] = jnp.zeros_like(own_ref)
        other_ref[...] = jnp.zeros_like(other_ref)
        for number, block_ref in enumerate(block_refs):
            gg_ref[number * size : (number + 1) * size] = block_ref[...]

    wg, wu, wd = wg_ref[...], wu_ref[...], wd_ref[...]
    for start in range(0, rows, size):
        part = slice(start, start + size)
        grad = matmul_nt(gg_ref[part], wd)
        gate = g_ref[part].astype(F32)
        up = u_ref[part].astype(F32)
        square = gate * gate
        bent = jnp.tanh(INNER * (gate + CUBIC * (square * gate)))
        half = 0.5 * (1.0 + bent)
        gelu = gate * half
        slope = half + (0.5 * INNER) * gate * (1.0 - bent * bent) * (1.0 + (3.0 * CUBIC) * square)
        hidden_ref[part] = rounded(gelu * up)
        grad_gate = rounded(grad * up * slope)
        grad_up = rounded(grad * gelu)
        dg_ref[part] = grad_gate
        du_ref[part] = grad_up
        add_rows(
            start, size, matmul_nt(grad_gate, wg) + matmul_nt(grad_up, wu), own_ref, other_ref
        )
    total = matmul_tn(hidden_ref[...], gg_ref[...])
    left = dl_ref.shape[1]
    for number, (out_ref, part) in enumerate(((dl_ref, total[:, :left]), (dr_ref, total[:, left:]))):
        if old_refs is not None:
            part = part + old_refs[number][...].astype(F32)
        out_ref[...] = rounded(part)

    @pl.when(pl.program_id(0) == pl.num_programs(0) - 1)
    def _():
        send_rows(other_ref, sent_refs)


def ff_backward(blocks, gate, up, w_gate, w_up, w_down, old, ties=()):
    size, width = blocks[0].shape
    rows = 4 * size
    wide = w_gate.shape[1]
    left = left_columns(width)
    column = pl.BlockSpec((rows, TILE), lambda j: (0, j))
    halves = [pl.BlockSpec((TILE, cols), lambda j: (j, 0)) for cols in (left, width - left)]
    in_specs = [full((size, width))] * 4 + [
        column,
        column,
        pl.BlockSpec((width, TILE), lambda j: (0, j)),
        pl.BlockSpec((width, TILE), lambda j: (0, j)),
        pl.BlockSpec((TILE, width), lambda j: (j, 0)),
    ]
    operands = [*blocks, gate, up, w_gate, w_up, w_down]
    if old is not None:
        in_specs += halves
        operands += list(old)
    return kernel_call(
        functools.partial(ff_backward_body, old is not None),
        (wide // TILE,),
        in_specs,
        [full((rows // 2, width)), column, column] + halves + sent_chunks(rows, width)[0],
        [
            jax.ShapeDtypeStruct((rows // 2, width), F32),
            jax.ShapeDtypeStruct((rows, wide), BF),
            jax.ShapeDtypeStruct((rows, wide), BF),
            jax.ShapeDtypeStruct((wide, left), BF),
            jax.ShapeDtypeStruct((wide, width - left), BF),
        ]
        + sent_chunks(rows, width)[1],
        [
            pltpu.VMEM((rows, TILE), BF),
            pltpu.VMEM((rows // 2, width), F32),
            pltpu.VMEM((rows, width), BF),
        ],
        ties,
    )(*operands, *ties)


def ff_weights_body(split, with_old, *refs):
    if split:
        (extent, stages), coords_ref, refs = split, refs[0], refs[1:]
    x_refs = refs[:4]
    dg_ref, du_ref = refs[4:6]
    old_refs = refs[6:8] if with_old else (None, None)
    refs = refs[8 if with_old else 6 :]
    outs, turned_ref = refs[: 4 if split else 2], refs[4 if split else 2]
    size = x_refs[0].shape[0]

    @pl.when(pl.program_id(0) == 0)
    def _():
        for number, x_ref in enumerate(x_refs):
            turned_ref[:, number * size : (number + 1) * size] = x_ref[...].T

    for kind, grad_ref in enumerate((dg_ref, du_ref)):
        total = matmul(turned_ref[...], grad_ref[...])
        if with_old:
            total = total + old_refs[kind][...].astype(F32)
        total = rounded(total)
        if not split:
            outs[kind][...] = total
            continue
        held_ref = refs[5]
        rows = held_ref.shape[-2]
        for number, index in enumerate(itertools.product(*[range(count) for count in extent])):
            held_ref[index] = total[number * rows : (number + 1) * rows]
        name, position = stages[kind]
        rest = [range(count) for number, count in enumerate(extent) if number != position]
        for side in range(2):
            for index in itertools.product(*rest):
                source = index[:position] + (coords_ref[name] ^ side,) + index[position:]
                outs[2 * kind + side][index] = held_ref[source]


def ff_weights(grid, coordinates, blocks, grad_gate, grad_up, old, stages=None, ties=()):
    size, width = blocks[0].shape
    rows = 4 * size
    wide = grad_gate.shape[1]
    column = pl.BlockSpec((rows, TILE), lambda j: (0, j))
    block = pl.BlockSpec((width, TILE), lambda j: (0, j))
    in_specs = [full((size, width))] * 4 + [column, column]
    operands = [*blocks, grad_gate, grad_up]
    scratch = [pltpu.VMEM((width, rows), BF)]
    if old is not None:
        in_specs += [block, block]
        operands += list(old)
    if stages is None:
        split = None
        outs = [jax.ShapeDtypeStruct((width, wide), BF)] * 2
        out_specs = [block, block]
    else:
        names = ("y", "x", "p")
        extent = grid.extent(names)
        split = (extent, [(NAMES.index(stage), names.index(stage)) for stage in stages])
        piece = width // grid.groups
        in_specs = [pl.BlockSpec(memory_space=pltpu.SMEM)] + in_specs
        operands = [coordinates] + operands
        scratch.append(pltpu.VMEM(extent + (piece, TILE), BF))
        outs = []
        out_specs = []
        for stage in stages:
            left = grid.extent([name for name in names if name != stage])
            for side in range(2):
                outs.append(jax.ShapeDtypeStruct(left + (piece, wide), BF))
                out_specs.append(
                    pl.BlockSpec(left + (piece, TILE), lambda j: (0,) * (len(left) + 1) + (j,))
                )
    return kernel_call(
        functools.partial(ff_weights_body, split, old is not None),
        (wide // TILE,),
        in_specs,
        out_specs,
        outs,
        scratch,
        ties,
    )(*operands, *ties)


def stack_body(plan, *refs):
    out_at = sum(count for count, pick, columns in plan)
    at = 0
    for count, pick, columns in plan:
        group = refs[at : at + count]
        at += count
        for column in columns:
            out_ref = refs[out_at]
            out_at += 1
            for index, ref in enumerate(group):
                place = () if pick is None else (pick,)
                value = ref[place + (Ellipsis, column)]
                if count == 1:
                    out_ref[...] = value
                else:
                    out_ref[index] = value


def stack(items, ties=()):
    plan = []
    outs = []
    operands = []
    for parts, pick, widths in items:
        extent = parts[0].shape if pick is None else parts[0].shape[1:]
        widths = widths or [extent[-1]]
        if len(parts) > 1:
            extent = (len(parts),) + extent
        columns = []
        start = 0
        for columns_wide in widths:
            columns.append(slice(start, start + columns_wide))
            start += columns_wide
            outs.append(jax.ShapeDtypeStruct(extent[:-1] + (columns_wide,), parts[0].dtype))
        plan.append((len(parts), pick, columns))
        operands += parts
    return whole_call(functools.partial(stack_body, plan), outs, None, operands, ties)


def fold_body(plan, coords_ref, *refs):
    at = 0
    out_at = sum(count for item in plan for count in item["counts"])
    for item in plan:
        names, stage, size = item["names"], item["stage"], item["size"]
        outs = refs[out_at : out_at + size]
        out_at += size
        position = names.index(stage)
        own = coords_ref[NAMES.index(stage)]
        rest = [range(extent) for number, extent in enumerate(item["extent"]) if number != position]
        column = 0
        for count in item["counts"]:
            group = refs[at : at + count]
            at += count
            rows, cols = group[0].shape[-2:]
            for mask in range(size):
                for index in itertools.product(*rest):
                    source = index[:position] + (own ^ mask,) + index[position:]
                    if count == 1:
                        value = group[0][source]
                    else:
                        value = group[0][source].astype(F32)
                        for other in group[1:]:
                            value = value + other[source].astype(F32)
                        value = rounded(value)
                    out = outs[mask]
                    out[index + (slice(0, rows), slice(column, column + cols))] = value
                    if rows < out.shape[-2]:
                        out[index + (slice(rows, None), slice(column, column + cols))] = jnp.zeros(
                            (out.shape[-2] - rows, cols), out.dtype
                        )
            column += cols


def fold(grid, coordinates, items, ties=()):
    plan = []
    outs = []
    operands = []
    for names, stage, groups in items:
        rows = max(group[0].shape[-2] for group in groups)
        cols = sum(group[0].shape[-1] for group in groups)
        left = tuple(name for name in names if name != stage)
        size = grid.sizes[stage]
        plan.append(
            {
                "names": names,
                "stage": stage,
                "size": size,
                "extent": grid.extent(names),
                "counts": [len(group) for group in groups],
            }
        )
        outs += [jax.ShapeDtypeStruct(grid.extent(left) + (rows, cols), BF)] * size
        for group in groups:
            operands += [
                value.reshape(grid.extent(names) + value.shape[-2:]) for value in group
            ]
    results = whole_call(
        functools.partial(fold_body, plan), outs, coordinates, operands, ties
    )
    folded = []
    at = 0
    for names, stage, groups in items:
        size = grid.sizes[stage]
        kept = [results[at]] + [
            grid.permute(results[at + mask], {stage: mask}) for mask in range(1, size)
        ]
        folded.append((tuple(name for name in names if name != stage), kept))
        at += size
    return folded


def pair_body(own_ref, *refs):
    came_refs, (own_out, sent_out) = refs[:-2], refs[-2:]
    count = own_out.shape[0]
    step = came_refs[0].shape[0]
    for number, came_ref in enumerate(came_refs):
        start = number * step
        total = own_ref[start : start + step] + came_ref[...].astype(F32)
        if start < count:
            own_out[start : start + step] = total
        else:
            sent_out[start - count : start - count + step] = rounded(total)


def tokens_out(grid, own, sent, ties=()):
    came = [grid.permute(part, {"c": 1}) for part in sent]
    count, width = own.shape[0] // 2, own.shape[1]
    own, sent = whole_call(
        pair_body, [shape(count, width, F32), shape(count, width)], None, [own, *came], ties
    )
    return own, grid.permute(sent, {"h": 1})


def fetch(coords_ref, refs, order, block, place):
    index = 0
    for number, stride in order[:-1]:
        index = index + (coords_ref[number] ^ block[number]) * stride
    last = order[-1][0]
    side = coords_ref[last] ^ block[last]
    value = refs[-1][(index,) + place]
    for number in range(len(refs) - 1):
        value = jnp.where(side == number, refs[number][(index,) + place], value)
    return value


def quarter_of(coords_ref):
    return coords_ref[3] * 2 + coords_ref[4]


def cut_body(groups, block, block_up, coords_ref, w_ref, *refs):
    out_refs, held_ref = refs[:-1], refs[-1]
    own = quarter_of(coords_ref)
    held_ref[...] = jnp.zeros_like(held_ref)
    for quarter in range(4):
        slot = own ^ quarter
        for kind in range(2):
            for group in range(groups):
                at = kind * groups * 4 * block + (group * 4 + quarter) * block
                held_ref[slot, kind, :, group * block_up : group * block_up + block] = w_ref[
                    :, at : at + block
                ]
    for mask, out_ref in enumerate(out_refs):
        out_ref[...] = held_ref[mask]


def pick_of(own, refs, quarter):
    value = refs[3]
    for mask in range(3):
        value = jnp.where(own == quarter ^ mask, refs[mask], value)
    return value


def pieces_body(coords_ref, p0_ref, p1_ref, p2_ref, p3_ref, out_ref):
    own = quarter_of(coords_ref)
    rows = p0_ref.shape[1]
    for kind in range(2):
        refs = [ref[kind] for ref in (p0_ref, p1_ref, p2_ref, p3_ref)]
        for quarter in range(4):
            out_ref[kind, quarter * rows : (quarter + 1) * rows] = pick_of(own, refs, quarter)


def split_body(count, coords_ref, *refs):
    own = quarter_of(coords_ref)
    outs = refs[2 * count :]
    rows = outs[0].shape[1]
    for kind in range(2):
        total = refs[kind * count][...].astype(F32)
        for ref in refs[kind * count + 1 : (kind + 1) * count]:
            total = total + ref[...].astype(F32)
        total = rounded(total)
        for mask, out_ref in enumerate(outs):
            value = total[3 * rows :]
            for quarter in range(3):
                value = jnp.where(
                    own == quarter ^ mask, total[quarter * rows : (quarter + 1) * rows], value
                )
            out_ref[kind] = value


def join_body(groups, block, block_up, coords_ref, p0_ref, p1_ref, p2_ref, p3_ref, out_ref):
    own = quarter_of(coords_ref)
    for kind in range(2):
        refs = [ref[kind] for ref in (p0_ref, p1_ref, p2_ref, p3_ref)]
        for quarter in range(4):
            piece = pick_of(own, refs, quarter).astype(F32)
            for group in range(groups):
                at = kind * groups * 4 * block + (group * 4 + quarter) * block
                out_ref[:, at : at + block] = piece[
                    :, group * block_up : group * block_up + block
                ]


def order_body(blocks, orders, coords_ref, *refs):
    out_ref = refs[-1]
    count = (len(refs) - 1) // len(orders)
    at = 0
    for group, order in enumerate(orders):
        group_refs = refs[group * count : (group + 1) * count]
        rows, cols = group_refs[0].shape[1:]
        for number, block in enumerate(blocks):
            out_ref[number * rows : (number + 1) * rows, at : at + cols] = fetch(
                coords_ref, group_refs, order, block, (slice(None), slice(None))
            )
        at += cols


def in_order(grid, coordinates, *columns, ties=()):
    blocks = grid.blocks_of("pxy")
    orders = []
    flat = []
    count = max(len(parts) for parts, names in columns)
    for parts, names in columns:
        parts = [part.reshape((-1,) + part.shape[-2:]) for part in parts]
        order = grid.order(names)
        if len(parts) < count:
            parts = [jnp.concatenate(parts)]
            parts += parts * (count - 1)
            order = order + ((order[-1][0], -1),)
        flat += parts
        orders.append(order)
    rows = flat[0].shape[1]
    cols = sum(parts[0].shape[-1] for parts, names in columns)
    return whole_call(
        functools.partial(order_body, blocks, tuple(orders)),
        jax.ShapeDtypeStruct((grid.groups * rows, cols), flat[0].dtype),
        coordinates,
        flat,
        ties,
    )


def spread_body(sizes, coords_ref, normed_ref, low_ref, mixed_ref, side_ref, *refs):
    own_ref, sent_ref, held_ref = refs
    devices, qkv, joined, lift, lift_at, out, mixed, last, last_at = sizes
    held_ref[...] = jnp.zeros_like(held_ref)
    second = devices // 2 * joined
    for number in range(devices):
        core, place = number % 2, number // 2
        at = place * joined
        held_ref[core, :, at : at + qkv] = normed_ref[:, number * qkv : (number + 1) * qkv]
        at = at + lift_at
        held_ref[core, :, at : at + lift] = low_ref[:, number * lift : (number + 1) * lift]
        at = second + place * mixed
        held_ref[core, :, at : at + out] = mixed_ref[:, number * out : (number + 1) * out]
        at = at + last_at
        held_ref[core, :, at : at + last] = side_ref[:, number * last : (number + 1) * last]
    own_ref[...] = held_ref[coords_ref[4]]
    sent_ref[...] = held_ref[1 - coords_ref[4]]


def unpack_first_body(blocks, order, sizes, count, coords_ref, *refs):
    chunks = [refs[at : at + count] for at in range(0, len(refs) - 4, count)]
    w_ref, lift_ref, down_ref, gain_ref = refs[-4:]
    rows, rows_up, lift_rows, gain_cols = sizes
    gain_ref[...] = jnp.zeros_like(gain_ref)
    main = slice(0, rows)
    lift = slice(rows_up, rows_up + lift_rows)
    every = slice(None)
    for number, block in enumerate(blocks):
        place = slice(number * rows, (number + 1) * rows)
        lift_place = slice(number * lift_rows, (number + 1) * lift_rows)
        at = 0
        for chunk in chunks[:-1]:
            columns = slice(at, at + chunk[0].shape[-1])
            w_ref[place, columns] = fetch(coords_ref, chunk, order, block, (main, every))
            lift_ref[lift_place, columns] = fetch(coords_ref, chunk, order, block, (lift, every))
            at = columns.stop
        down_ref[place, :] = fetch(coords_ref, chunks[-1], order, block, (main, every))
        gain_ref[0:2, number * gain_cols : (number + 1) * gain_cols] = fetch(
            coords_ref,
            chunks[-1],
            order,
            block,
            (slice(rows_up, rows_up + 2), slice(0, gain_cols)),
        ).astype(F32)


def unpack_second_body(blocks, order, sizes, count, coords_ref, *refs):
    chunks = [refs[at : at + count] for at in range(0, len(refs) - 5, count)]
    out_ref, lift0_ref, lift1_ref, down_ref, late_ref = refs[-5:]
    rows, rows_up, lift_rows, lift_up, late_rows, late_up = sizes
    every = slice(None)
    main = slice(0, rows)
    fold_cols = chunks[-1][0].shape[-1]
    for number, block in enumerate(blocks):

        def get(chunk, start, size):
            return fetch(coords_ref, chunk, order, block, (slice(start, start + size), every))

        place = slice(number * rows, (number + 1) * rows)
        lift_place = slice(number * lift_rows, (number + 1) * lift_rows)
        at = 0
        for chunk in chunks[:-2]:
            columns = slice(at, at + chunk[0].shape[-1])
            out_ref[place, columns] = get(chunk, 0, rows)
            lift0_ref[lift_place, columns] = get(chunk, rows_up, lift_rows)
            lift1_ref[lift_place, columns] = get(chunk, rows_up + lift_up, lift_rows)
            at = columns.stop
        down_ref[place, :] = get(chunks[-2], 0, rows)
        late_place = slice(number * late_rows, (number + 1) * late_rows)
        for part in range(late_ref.shape[1] // fold_cols):
            late_ref[late_place, part * fold_cols : (part + 1) * fold_cols] = get(
                chunks[-1], part * late_up, late_rows
            )


def rotate(values, cosine_table, sine_table):
    halfway = values.shape[-1] // 2
    first_half = values[..., :halfway]
    second_half = values[..., halfway:]
    return jnp.concatenate(
        [
            first_half * cosine_table - second_half * sine_table,
            second_half * cosine_table + first_half * sine_table,
        ],
        axis=-1,
    )


def inverse_size(values):
    return lax.rsqrt(jnp.mean(values * values, axis=-1, keepdims=True) + EPS)


def norm_back(values, gain_row, grad):
    inverse = inverse_size(values)
    weighted = grad * gain_row
    inner = jnp.mean(weighted * values, axis=-1, keepdims=True)
    gain_grad = jnp.sum(grad * values * inverse, axis=0, keepdims=True)
    return inverse * weighted - values * (inverse * inverse * inverse) * inner, gain_grad


def shape(rows, cols, kind=BF):
    return jax.ShapeDtypeStruct((rows, cols), kind)


def pack_body(
    sizes, wq_ref, qd_ref, ql_ref, gain_ref, wo_ref, od_ref, ol_ref, first_ref, second_ref
):
    qkv_up, ql_up, out_up, ol_up = sizes
    for ref in (first_ref, second_ref):
        ref[...] = jnp.zeros_like(ref)
    rows, cols = wq_ref.shape
    lift_rows = ql_ref.shape[1]
    rank = qd_ref.shape[2]
    first_ref[:rows, :cols] = wq_ref[...]
    first_ref[qkv_up : qkv_up + lift_rows, :cols] = ql_ref[0]
    for loop in range(2):
        at = cols + loop * rank
        first_ref[:rows, at : at + rank] = qd_ref[loop]
    first_ref[qkv_up : qkv_up + 2, cols : cols + gain_ref.shape[1]] = gain_ref[...]
    rows, width = wo_ref.shape
    last_rows = ol_ref.shape[1]
    second_ref[:rows, :width] = wo_ref[...]
    for loop in range(2):
        at = out_up + loop * ol_up
        second_ref[at : at + last_rows, :width] = ol_ref[loop]
        at = width + loop * rank
        second_ref[:rows, at : at + rank] = od_ref[loop]
    for part in range(cols // rank):
        second_ref[part * ql_up : part * ql_up + lift_rows, width + 2 * rank :] = ql_ref[
            1, :, part * rank : (part + 1) * rank
        ]


def halves_body(w_ref, left_ref, right_ref):
    rows = w_ref.shape[0]
    left = left_ref.shape[1]
    for ref in (left_ref, right_ref):
        ref[...] = jnp.zeros_like(ref)
    left_ref[:rows] = w_ref[:, :left]
    right_ref[:rows] = w_ref[:, left:]


def project_kv_body(first_loop, addends, *refs):
    add_refs = refs[:addends]
    gain_ref, qd_ref, w_ref, ql_ref, cos_ref, sin_ref = refs[addends : addends + 6]
    kv_ref, normed_ref, low_ref, residual_ref = refs[addends + 6 :]
    rank = low_ref.shape[1]
    width_q = w_ref.shape[1] - 2 * HD
    values = add_refs[0][...].astype(F32)
    for ref in add_refs[1:]:
        values = values + ref[...].astype(F32)
    residual_ref[...] = values
    normed = rounded(values * inverse_size(values) * gain_ref[0:1])
    normed_ref[...] = normed
    down = qd_ref[:, :rank] if first_loop else qd_ref[:, rank:]
    low = rounded(matmul(normed, down))
    low_ref[...] = low
    kv = matmul(normed, w_ref[:, width_q:]) + matmul(low, ql_ref[:, width_q:])
    kv_ref[:, :HD] = rounded(rotate(kv[:, :HD], cos_ref[...], sin_ref[...]))
    kv_ref[:, HD:] = rounded(kv[:, HD:])


def project_q_body(normed_ref, low_ref, w_ref, ql_ref, cos_ref, sin_ref, q_ref):
    for head in range(H):
        at = slice(head * HD, (head + 1) * HD)
        part = matmul(normed_ref[...], w_ref[:, at]) + matmul(low_ref[...], ql_ref[:, at])
        q_ref[:, at] = rounded(rotate(part, cos_ref[...], sin_ref[...]) * HD ** (-0.5))


def mask_of(segs_ref, places_ref, row_ref):
    seq_len = row_ref.shape[1]
    key_places = lax.broadcasted_iota(jnp.int32, (segs_ref.shape[0], seq_len), 1)
    allowed = (segs_ref[...] == row_ref[...]) & (key_places <= places_ref[...])
    return jnp.where(allowed, 0.0, NEG)


def attend_body(q_ref, kv_ref, segs_ref, places_ref, row_ref, mixed_ref, log_ref):
    mask = mask_of(segs_ref, places_ref, row_ref)
    for head in range(H):
        at = slice(head * HD, (head + 1) * HD)
        scores = matmul_nt(q_ref[:, at], kv_ref[:, :HD]) + mask
        top = jnp.max(scores, axis=1, keepdims=True)
        probabilities = jnp.exp(scores - top)
        total = jnp.sum(probabilities, axis=1, keepdims=True)
        mixed_ref[:, at] = rounded(matmul(rounded(probabilities), kv_ref[:, HD:]) / total)
        log_ref[head] = top + jnp.log(total)


def attend_back_body(
    q_ref, kv_ref, segs_ref, places_ref, row_ref, log_ref, grad_ref, cos_ref, sin_ref,
    coords_ref, own_ref, sent_ref, gq_ref, keys_ref, values_ref,
):
    mask = mask_of(segs_ref, places_ref, row_ref)
    size = own_ref.shape[1]
    for head in range(H):
        at = slice(head * HD, (head + 1) * HD)
        queries = q_ref[:, at]
        grad = grad_ref[:, at]
        probabilities = jnp.exp(matmul_nt(queries, kv_ref[:, :HD]) + mask - log_ref[head])
        grad_probs = matmul_nt(grad, kv_ref[:, HD:])
        weighted = probabilities * grad_probs
        delta = jnp.sum(weighted, axis=1, keepdims=True)
        grad_scores = rounded(weighted - probabilities * delta)
        grad_q = matmul(grad_scores, kv_ref[:, :HD])
        gq_ref[:, at] = rounded(rotate(grad_q, cos_ref[...], -sin_ref[...]) * HD ** (-0.5))
        key_term = matmul_tn(grad_scores, queries)
        value_term = matmul_tn(rounded(probabilities), grad)
        if head == 0:
            keys_ref[...] = key_term
            values_ref[...] = value_term
        else:
            keys_ref[...] += key_term
            values_ref[...] += value_term
    core = coords_ref[4]
    for number in range(own_ref.shape[0]):
        for out_ref, which in ((own_ref, core), (sent_ref, 1 - core)):
            place = pl.ds(pl.multiple_of((2 * number + which) * size, size), size)
            out_ref[number, :, :HD] = rounded(keys_ref[place, :])
            out_ref[number, :, HD:] = rounded(values_ref[place, :])


def leave_body(
    first_loop, mixed_ref, od_ref, w_ref, ol_ref, residual_ref, gain_ref,
    side_ref, middle_ref, normed_ref,
):
    rank = side_ref.shape[1]
    down = od_ref[:, :rank] if first_loop else od_ref[:, rank:]
    side = rounded(matmul(mixed_ref[...], down))
    side_ref[...] = side
    middle = residual_ref[...] + (matmul(mixed_ref[...], w_ref[...]) + matmul(side, ol_ref[...]))
    middle_ref[...] = middle
    normed_ref[...] = rounded(middle * inverse_size(middle) * gain_ref[1:2])


def enter_back_body(
    first_loop, own_ref, other_ref, result_ref, middle_ref, gain_ref, w_ref, ol_ref, od_ref,
    grad_ref, branch_ref, side_ref, mixed_ref, gain_grad_ref,
):
    rank = side_ref.shape[1]
    grad_normed = own_ref[...] + other_ref[...].astype(F32)
    back, gain_grad = norm_back(middle_ref[...], gain_ref[1:2], grad_normed)
    gain_grad_ref[...] = jnp.broadcast_to(gain_grad, gain_grad_ref.shape)
    grad = result_ref[...].astype(F32) + back
    grad_ref[...] = grad
    branch = rounded(grad)
    branch_ref[...] = branch
    side = rounded(matmul_nt(branch, ol_ref[...]))
    side_ref[...] = side
    down = od_ref[:, :rank] if first_loop else od_ref[:, rank:]
    mixed_ref[...] = rounded(matmul_nt(branch, w_ref[...]) + matmul_nt(side, down))


def rope_back_body(count, *refs):
    gq_ref, ql_ref, cos_ref, sin_ref, out_ref, low_ref = refs[count:]
    width_q = gq_ref.shape[1]
    kv = refs[0][...].astype(F32)
    for ref in refs[1:count]:
        kv = kv + ref[...].astype(F32)
    keys = rounded(rotate(kv[:, :HD], cos_ref[...], -sin_ref[...]))
    values = rounded(kv[:, HD:])
    out_ref[:, :HD] = keys
    out_ref[:, HD:] = values
    low_ref[...] = rounded(
        matmul_nt(gq_ref[...], ql_ref[:, :width_q])
        + matmul_nt(keys, ql_ref[:, width_q : width_q + HD])
        + matmul_nt(values, ql_ref[:, width_q + HD :])
    )


def leave_back_body(
    first_loop, kv_ref, gq_ref, low_ref, w_ref, qd_ref, residual_ref, gain_ref, grad_ref,
    other_gain_ref, *refs,
):
    out_ref, out_b_ref, gain_grad_ref = refs[-3:]
    rank = low_ref.shape[1]
    width_q = gq_ref.shape[1]
    down = qd_ref[:, :rank] if first_loop else qd_ref[:, rank:]
    grad_normed = (
        matmul_nt(gq_ref[...], w_ref[:, :width_q])
        + matmul_nt(kv_ref[...], w_ref[:, width_q:])
        + matmul_nt(low_ref[...], down)
    )
    back, gain_grad = norm_back(residual_ref[...], gain_ref[0:1], grad_normed)
    gain_grad_ref[0:1] = gain_grad
    gain_grad_ref[1:2] = other_gain_ref[1:2]
    if len(refs) > 3:
        gain_grad_ref[0:2] += refs[0][0:2]
    grad = grad_ref[...] + back
    out_ref[...] = grad
    out_b_ref[...] = rounded(grad)


def late_body(sizes, coords_ref, kv_ref, qd_ref, *refs):
    count, rows, gain_cols = sizes
    gain_refs, out_ref = refs[:-1], refs[-1]
    kv_cols = kv_ref.shape[2]
    out_ref[:, :, :kv_cols] = kv_ref[...]
    out_ref[:, :, kv_cols:] = qd_ref[...]
    for row in range(2):
        gains = rounded(gain_refs[0][row : row + 1] + gain_refs[1][row : row + 1])
        for number in range(count):
            at = 2 * number * gain_cols
            value = jnp.where(
                coords_ref[4] == 0,
                gains[:, at : at + gain_cols],
                gains[:, at + gain_cols : at + 2 * gain_cols],
            )
            out_ref[number, rows + row : rows + row + 1, kv_cols : kv_cols + gain_cols] = value


def down_body(count, *refs):
    out_ref = refs[-1]
    at = 0
    for group in range(2):
        value = refs[group * count][...].astype(F32)
        for ref in refs[group * count + 1 : (group + 1) * count]:
            value = value + ref[...].astype(F32)
        out_ref[:, at : at + value.shape[1]] = value[: out_ref.shape[0]]
        at += value.shape[1]


def result_body(middle_ref, own_ref, other_ref, out_ref):
    out_ref[...] = rounded(middle_ref[...] + (own_ref[...] + other_ref[...].astype(F32)))


def finish_body(count, sizes, *refs):
    rows, rows_up, lift_rows, lift_up, out_rows, out_up, last_rows, last_up, gain_cols = sizes
    totals = []
    for group in range(3):
        value = refs[group * count][...].astype(F32)
        for ref in refs[group * count + 1 : (group + 1) * count]:
            value = value + ref[...].astype(F32)
        totals.append(value)
    outs, queries, late = totals
    gains_ref, qkv_ref, out_ref, qd_ref, ql_ref, od_ref, ol_ref = refs[3 * count :]
    width = out_ref.shape[1]
    rank = qd_ref.shape[2]
    half = queries.shape[1] - rank
    rest = qkv_ref.shape[1] - half
    gains_ref[...] = late[rows : rows + 2, rest : rest + gain_cols]
    qkv_ref[:, :half] = queries[:rows, :half]
    qkv_ref[:, half:] = late[:rows, :rest]
    out_ref[...] = outs[:out_rows, :width]
    qd_ref[0] = late[:rows, rest:]
    qd_ref[1] = queries[:rows, half:]
    for loop in range(2):
        at = rows_up + loop * lift_up
        ql_ref[loop, :, :half] = queries[at : at + lift_rows, :half]
        ql_ref[loop, :, half:] = late[at : at + lift_rows, :rest]
        at = width + loop * rank
        od_ref[loop] = outs[:out_rows, at : at + rank]
        at = out_up + loop * last_up
        ol_ref[loop] = outs[at : at + last_rows, :width]


def outer_body(columns, rights, olds, own_ref, came_ref, *refs):
    out_refs = refs[2 * rights + olds :]
    own, came = own_ref[:, columns], came_ref[:, columns]
    for number in range(rights):
        right_ref, right_came_ref = refs[2 * number], refs[2 * number + 1]
        out_ref = out_refs[number]
        cols = out_ref.shape[1]
        step = 512 if cols % 512 == 0 else 384 if cols % 384 == 0 else cols
        for start in range(0, cols, step):
            part = slice(start, start + step)
            total = matmul_tn(own, right_ref[:, part]) + matmul_tn(came, right_came_ref[:, part])
            if number < olds:
                total = total + refs[2 * rights + number][:, part].astype(F32)
            out_ref[:, part] = rounded(total)


def outer(left, columns, rights, olds=(), ties=()):
    rows = columns.stop - columns.start
    return whole_call(
        functools.partial(outer_body, columns, len(rights), len(olds)),
        [shape(rows, right[0].shape[1]) for right in rights],
        None,
        [*left, *[value for right in rights for value in right], *olds],
        ties,
    )


def per_device(
    grid,
    inputs,
    segments,
    cotangent,
    norm_gain_rows,
    query_key_value_weight,
    output_weight,
    gate_up_weight,
    down_weight,
    adapter_query_down,
    adapter_query_lift,
    adapter_output_down,
    adapter_output_lift,
):
    tokens = inputs.shape[0]
    width = inputs.shape[1]
    groups = grid.groups
    gain_cols = norm_gain_rows.shape[1]
    qkv_rows = query_key_value_weight.shape[0]
    out_rows = output_weight.shape[0]
    ql_rows = adapter_query_lift.shape[1]
    ol_rows = adapter_output_lift.shape[1]
    rank = adapter_query_down.shape[2]
    hidden_block = down_weight.shape[0]
    width_q = H * HD

    qkv_up, ql_up = up8(qkv_rows), up8(ql_rows)
    out_up, ol_up = up8(out_rows), up8(ol_rows)
    wide = -(-groups * hidden_block // TILE) * TILE
    block_up = wide // groups
    qkv_cols = query_key_value_weight.shape[1]
    left_cols = left_columns(width)
    coordinates = grid.coordinates()
    straight = ("p", "h", "x", "y", "c")
    turned = ("p", "h", "y", "x", "c")

    def flat(parts):
        return [part.reshape((-1,) + part.shape[-2:]) for part in parts]

    def parts(values, name):
        return grid.parts(values, name)

    segrow = segments[0]
    seq_len = segrow.shape[0]
    position = lax.axis_index("blk")
    places = position * tokens + jnp.arange(tokens, dtype=jnp.int32)
    own_segs = lax.dynamic_slice_in_dim(segrow, position * tokens, tokens, 0)
    below_one = jnp.sum((segrow < 1).astype(jnp.int32))
    below_two = jnp.sum((segrow < 2).astype(jnp.int32))
    starts = jnp.where(own_segs == 0, 0, jnp.where(own_segs == 1, below_one, below_two))
    offsets = (places - starts).astype(F32)
    frequency = jnp.exp(jnp.arange(HD // 2, dtype=F32) * (-2.0 * math.log(ROPE_BASE) / HD))
    angles = offsets[:, None] * frequency[None, :]
    tables = [jnp.cos(angles), jnp.sin(angles)]
    masks = [own_segs[:, None], places[:, None], segments]

    second_rows = max(out_up + 2 * ol_up, qkv_cols // rank * ql_up)
    first, second = whole_call(
        functools.partial(pack_body, (qkv_up, ql_up, out_up, ol_up)),
        [shape(qkv_up + ql_up, qkv_cols + 2 * rank), shape(second_rows, width + 3 * rank)],
        None,
        [
            query_key_value_weight, adapter_query_down, adapter_query_lift, norm_gain_rows,
            output_weight, adapter_output_down, adapter_output_lift,
        ],
    )
    first, second = stack([(parts(first, "p"), None, None), (parts(second, "p"), None, None)])
    cut = whole_call(
        functools.partial(cut_body, groups, hidden_block, block_up),
        [jax.ShapeDtypeStruct((2, qkv_rows, wide), BF)] * 4,
        coordinates,
        [gate_up_weight],
        [first],
        [pltpu.VMEM((4, 2, qkv_rows, wide), BF)],
    )
    down_left, down_right = whole_call(
        halves_body,
        [shape(block_up, left_cols), shape(block_up, width - left_cols)],
        None,
        [down_weight],
        [cut[0]],
    )
    first, second = stack(
        [(parts(first, "h"), None, None), (parts(second, "h"), None, None)], [down_left]
    )
    gate_up = whole_call(
        pieces_body,
        jax.ShapeDtypeStruct((2, 4 * qkv_rows, wide), BF),
        coordinates,
        [
            cut[0],
            grid.permute(cut[1], {"c": 1}),
            grid.permute(cut[2], {"h": 1}),
            grid.permute(cut[3], {"h": 1, "c": 1}),
        ],
        [first],
    )
    first, second = stack(
        [(parts(first, "x"), None, None), (parts(second, "y"), None, None)], [gate_up]
    )
    gate_up = parts(gate_up, "p")
    first_chunks = [qkv_cols // 3] * 3 + [2 * rank]
    second_chunks = [width - left_cols, left_cols, 2 * rank, rank]
    chunks = stack(
        [
            (parts(first, "y"), None, first_chunks),
            (parts(second, "x"), None, second_chunks),
        ]
    )
    chunks = [flat(parts(chunk, "c")) for chunk in chunks]
    first = [part for chunk in chunks[:4] for part in chunk]
    second = [part for chunk in chunks[4:] for part in chunk]
    gate, up, down_left, down_right = stack(
        [
            (gate_up, 0, None),
            (gate_up, 1, None),
            ([down_left], None, None),
            ([down_right], None, None),
        ],
        [chunks[0][0]],
    )
    gate, up = parts(gate, "x"), parts(up, "y")
    down_left, down_right = parts(down_left, "p"), parts(down_right, "p")
    w_qkv, ql_0, qd, gains = whole_call(
        functools.partial(
            unpack_first_body,
            grid.blocks_of(straight),
            grid.order(straight),
            (qkv_rows, qkv_up, ql_rows, gain_cols),
            2,
        ),
        [shape(width, qkv_cols), shape(rank, qkv_cols), shape(width, 2 * rank), shape(8, width, F32)],
        coordinates,
        first,
        [gate[0]],
    )
    lifts_in = [ql_0, None]

    def project_kv(addends, loop):
        own_kv, normed_b, low_rank_b, residual = whole_call(
            functools.partial(project_kv_body, loop == 0, len(addends)),
            [
                shape(tokens, 2 * HD), shape(tokens, width), shape(tokens, rank),
                shape(tokens, width, F32),
            ],
            None,
            [*addends, gains, qd, w_qkv, lifts_in[loop], *tables],
        )
        both = lax.all_gather(own_kv, "blk", axis=0, tiled=True)
        return own_kv, normed_b, low_rank_b, residual, both

    def project_q(projected, loop, ties=()):
        return whole_call(
            project_q_body,
            shape(tokens, width_q),
            None,
            [projected[1], projected[2], w_qkv, lifts_in[loop], *tables],
            ties,
        )

    def attend(queries, both, ties=()):
        return whole_call(
            attend_body,
            [shape(tokens, width_q), jax.ShapeDtypeStruct((H, tokens, 1), F32)],
            None,
            [queries, both, *masks],
            ties,
        )

    projected_one = project_kv([inputs], 0)
    queries_one = project_q(projected_one, 0)
    gate, up = stack([(gate, None, None), (up, None, None)], [queries_one])
    gate, up = parts(gate, "y"), parts(up, "x")
    w_out, ol_0, ol_1, od, ql_1 = whole_call(
        functools.partial(
            unpack_second_body,
            grid.blocks_of(straight),
            grid.order(turned),
            (out_rows, out_up, ol_rows, ol_up, ql_rows, ql_up),
            2,
        ),
        [
            shape(width_q, width), shape(rank, width), shape(rank, width),
            shape(width_q, 2 * rank), shape(rank, qkv_cols),
        ],
        coordinates,
        second,
        [gate[0]],
    )
    attended_one = attend(queries_one, projected_one[4], [w_out])
    down_left, down_right = stack(
        [(down_left, None, None), (down_right, None, None)], [attended_one[0]]
    )
    down_left, down_right = parts(down_left, "x"), parts(down_right, "y")
    lifts_in[1] = ql_1
    lifts_out = (ol_0, ol_1)

    def leave(loop, mixed_b, residual):
        return whole_call(
            functools.partial(leave_body, loop == 0),
            [shape(tokens, rank), shape(tokens, width, F32), shape(tokens, width)],
            None,
            [mixed_b, od, w_out, lifts_out[loop], residual, gains],
        )

    left_one = leave(0, attended_one[0], projected_one[3])
    ff_in_one = grid.tokens_in(left_one[2])
    down_left, down_right = stack(
        [(down_left, None, None), (down_right, None, None)], [left_one[2]]
    )
    down_left, down_right = parts(down_left, "y"), parts(down_right, "x")
    w_gate = in_order(grid, coordinates, (gate, ("p", "x", "y")))
    w_up = in_order(grid, coordinates, (up, ("p", "y", "x")))
    w_down = in_order(
        grid, coordinates, (down_left, ("p", "x", "y")), (down_right, ("p", "y", "x"))
    )

    qkv_block = qkv_up + 2 * ql_up
    out_block = out_up + 2 * ol_up

    cotangent_in = grid.tokens_in(cotangent)

    def feed_forward(loop, projected, queries, attended, left, ff_in, ties=()):
        own_kv, normed_b, low_rank_b, residual, both = projected
        mixed_b, log_total = attended
        side_b, middle, unused = left
        spread_own, spread_sent = whole_call(
            functools.partial(
                spread_body,
                (
                    grid.devices, qkv_rows, qkv_block, ql_rows, qkv_up + loop * ql_up,
                    out_rows, out_block, ol_rows, out_up + loop * ol_up,
                ),
            ),
            [shape(tokens, grid.devices // 2 * (qkv_block + out_block))] * 2,
            coordinates,
            [normed_b, low_rank_b, mixed_b, side_b],
            (),
            [pltpu.VMEM((2, tokens, grid.devices // 2 * (qkv_block + out_block)), BF)],
        )
        ff_own, gate_b, up_b, *ff_sent = ff_forward(
            ff_in, w_gate, w_up, w_down, [spread_sent]
        )
        own, other = tokens_out(grid, ff_own, ff_sent, ties)
        cache = (
            residual, (spread_own, grid.permute(spread_sent, {"c": 1})), queries, both, log_total,
            middle, ff_in, gate_b, up_b,
        )
        return [middle, own, other], cache

    addends, cache_one = feed_forward(
        0, projected_one, queries_one, attended_one, left_one, ff_in_one, [cotangent_in[1]]
    )
    projected_two = project_kv(addends, 1)
    queries_two = project_q(projected_two, 1)
    attended_two = attend(queries_two, projected_two[4])
    left_two = leave(1, attended_two[0], projected_two[3])
    addends, cache_two = feed_forward(
        1, projected_two, queries_two, attended_two, left_two, grid.tokens_in(left_two[2])
    )
    result = whole_call(result_body, shape(tokens, width), None, addends)

    group_names = ("y", "x", "p")
    names = ("y", "x", "p", "h")
    half = grid.devices // 2
    joined_columns = slice(0, half * qkv_block)
    mixed_columns = slice(half * qkv_block, half * (qkv_block + out_block))

    def step(stages, ties=()):
        return fold(
            grid, coordinates, [(item[0], stage, [item[1]]) for item, stage in stages], ties
        )

    y_size = grid.sizes["y"]

    def with_core(values):
        return values, grid.permute(values, {"c": 1})

    def backward_loop(cache, grad_result, blocks_in, loop, old):
        (
            residual, spreads, queries, both, log_total, middle, ff_in, gate_b, up_b,
        ) = cache
        last = old is not None
        ql, ol = lifts_in[loop], lifts_out[loop]

        def before(name):
            return old[name] if last else None

        def grouped(values):
            return values.reshape(groups, values.shape[0] // groups, values.shape[1])

        own, grad_gate_b, grad_up_b, *down = ff_backward(
            blocks_in, gate_b, up_b, w_gate, w_up, w_down, before("down")
        )
        down, sent = down[:2], down[2:]
        ties = [] if last else [result]
        if last:
            down = fold(
                grid,
                coordinates,
                [
                    (group_names, "x", [[grouped(down[0])]]),
                    (group_names, "y", [[grouped(down[1])]]),
                ],
            )
            ties = [down[0][1][0]]
        own, other = tokens_out(grid, own, sent, ties)
        pair = ff_weights(
            grid,
            coordinates,
            ff_in,
            grad_gate_b,
            grad_up_b,
            (old["gate"], old["up"]) if last else None,
            ("x", "y" if y_size == 2 else "x") if last else None,
            [own],
        )
        ties = [pair[0]]
        if last:
            d_gate = (("y", "p"), [pair[0], grid.permute(pair[1], {"x": 1})])
            if y_size == 2:
                d_up = (("x", "p"), [pair[2], grid.permute(pair[3], {"y": 1})])
            else:
                d_up = (("y", "p"), [pair[2], grid.permute(pair[3], {"x": 1})])
        else:
            d_gate, d_up = pair
        grad_middle, grad_branch_b, grad_side_b, grad_mixed_b, gain_grad_ff = whole_call(
            functools.partial(enter_back_body, loop == 0),
            [
                shape(tokens, width, F32), shape(tokens, width), shape(tokens, rank),
                shape(tokens, width_q), shape(8, width, F32),
            ],
            None,
            [own, other, grad_result, middle, gains, w_out, ol, od],
            ties,
        )
        ties = []
        if last:
            down = fold(
                grid,
                coordinates,
                [(down[0][0], "y", [down[0][1]]), (down[1][0], "x", [down[1][1]])],
                [grad_mixed_b],
            )
            ties = [down[0][1][0]]
        kv_own, kv_sent, grad_queries_b = pl.pallas_call(
            tied(attend_back_body, 10, ties),
            out_shape=[jax.ShapeDtypeStruct((grid.blk // 2, tokens, 2 * HD), BF)] * 2
            + [shape(tokens, width_q)],
            in_specs=[pl.BlockSpec(memory_space=pltpu.VMEM)] * 9
            + [pl.BlockSpec(memory_space=pltpu.SMEM)]
            + [ANY] * len(ties),
            scratch_shapes=[pltpu.VMEM((seq_len, HD), F32)] * 2,
            cost_estimate=LIGHT,
            compiler_params=pltpu.CompilerParams(vmem_limit_bytes=48 * 1024 * 1024),
        )(queries, both, *masks, log_total, grad_mixed_b, *tables, coordinates, *ties)
        grad_kv = (("p", "h"), [kv_own, grid.permute(kv_sent, {"c": 1})])
        (grad_kv,) = step([(grad_kv, "h")])
        (grad_kv,) = step([(grad_kv, "p")])
        branch, side = with_core(grad_branch_b), with_core(grad_side_b)
        d_out, d_od = outer(
            spreads, mixed_columns, [branch, side], [old["out"]] if last else [], [grad_kv[1][0]]
        )
        (d_queries,) = outer(
            spreads,
            joined_columns,
            [with_core(grad_queries_b)],
            [old["queries"]] if last else [],
            [d_out],
        )
        sums = {"out": d_out, "od": d_od, "queries": d_queries}
        ties = [] if last else [d_queries, cache_one[1][1]]
        if last:
            sums["out"], sums["queries"] = fold(
                grid,
                coordinates,
                [
                    (names, "x", [[blocks(value)] for value in (d_out, d_od, old["od"])]),
                    (names, "y", [[blocks(value)] for value in (d_queries, old["qd"])]),
                ],
            )
            sums["gate"], sums["up"], down[0], down[1] = fold(
                grid,
                coordinates,
                [
                    (d_gate[0], "y", [d_gate[1]]),
                    (d_up[0], d_up[0][0], [d_up[1]]),
                    (down[0][0], "p", [down[0][1]]),
                    (down[1][0], "p", [down[1][1]]),
                ],
                [sums["out"][1][0]],
            )
            ties = [sums["gate"][1][0]]
        else:
            sums["gate"], sums["up"] = d_gate, d_up
        sums["down"] = down
        grad_kv_b, grad_low_rank_b = whole_call(
            functools.partial(rope_back_body, len(grad_kv[1])),
            [shape(tokens, 2 * HD), shape(tokens, rank)],
            None,
            [*grad_kv[1], grad_queries_b, ql, *tables],
            ties,
        )
        sums["kv"], sums["qd"] = outer(
            spreads,
            joined_columns,
            [with_core(grad_kv_b), with_core(grad_low_rank_b)],
            [old["kv"]] if last else [],
        )
        following, following_b, gain_grads = whole_call(
            functools.partial(leave_back_body, loop == 0),
            [shape(tokens, width, F32), shape(tokens, width), shape(8, width, F32)],
            None,
            [
                grad_kv_b, grad_queries_b, grad_low_rank_b, w_qkv, qd, residual, gains,
                grad_middle, gain_grad_ff,
            ]
            + ([old["gains"]] if last else []),
        )
        sums["gains"] = gain_grads
        return following, following_b, sums

    def blocks(values):
        return values.reshape(half, values.shape[0] // half, values.shape[1])

    grad_one, grad_one_b, sums_two = backward_loop(cache_two, cotangent, cotangent_in, 1, None)
    grad_inputs, unused, sums = backward_loop(
        cache_one, grad_one, grid.tokens_in(grad_one_b), 0, sums_two
    )

    late = whole_call(
        functools.partial(late_body, (half, qkv_rows, gain_cols)),
        jax.ShapeDtypeStruct((half, qkv_block, 2 * HD + rank), BF),
        coordinates,
        [blocks(sums["kv"]), blocks(sums["qd"]), *with_core(sums["gains"])],
    )
    (late,) = step([((names, [late]), "x")])
    d_down = whole_call(
        functools.partial(down_body, len(sums["down"][0][1])),
        shape(hidden_block, width, F32),
        None,
        sums["down"][0][1] + sums["down"][1][1],
        [late[1][0]],
    )
    gate, up = step([(sums["gate"], "p"), (sums["up"], "p")], [d_down])
    outs, queries = step([(sums["out"], "y"), (sums["queries"], "x")], [gate[1][0]])
    (late,) = step([(late, "y")], [outs[1][0]])
    split = whole_call(
        functools.partial(split_body, len(gate[1])),
        [jax.ShapeDtypeStruct((2, qkv_rows, wide), BF)] * 4,
        coordinates,
        gate[1] + up[1],
        [late[1][0]],
    )
    back = [
        split[0],
        grid.permute(split[1], {"c": 1}),
        grid.permute(split[2], {"h": 1}),
        grid.permute(split[3], {"h": 1, "c": 1}),
    ]
    outs, queries, late = step([(outs, "h"), (queries, "h"), (late, "h")], [split[0]])
    outs, queries, late = step([(outs, "p"), (queries, "p"), (late, "p")])
    d_gate_up = whole_call(
        functools.partial(join_body, groups, hidden_block, block_up),
        shape(qkv_rows, 8 * groups * hidden_block, F32),
        coordinates,
        back,
        [late[1][0]],
    )
    last = [outs[1], queries[1], late[1]]
    d_gains, d_qkv, d_out, d_qd, d_ql, d_od, d_ol = whole_call(
        functools.partial(
            finish_body,
            len(outs[1]),
            (
                qkv_rows, qkv_up, ql_rows, ql_up, out_rows, out_up, ol_rows, ol_up, gain_cols,
            ),
        ),
        [
            shape(2, gain_cols, F32),
            shape(qkv_rows, qkv_cols, F32),
            shape(out_rows, width, F32),
            jax.ShapeDtypeStruct(adapter_query_down.shape, F32),
            jax.ShapeDtypeStruct(adapter_query_lift.shape, F32),
            jax.ShapeDtypeStruct(adapter_output_down.shape, F32),
            jax.ShapeDtypeStruct(adapter_output_lift.shape, F32),
        ],
        None,
        [value for values in last for value in values],
    )
    return (
        result, grad_inputs, d_gains, d_qkv, d_out, d_gate_up, d_down, d_qd, d_ql, d_od, d_ol,
    )


def solution(mesh):
    grid = Grid(mesh)
    rows = P(AXES, None)
    deep = P(None, AXES, None)
    in_specs = (
        rows, P("fsdp", None), rows, P(None, AXES), rows, rows, rows, rows, deep, deep, deep, deep,
    )
    out_specs = (
        rows, rows, P(None, AXES), rows, rows, rows, rows, deep, deep, deep, deep,
    )

    def run(*arguments):
        return per_device(grid, *arguments)

    return jax.shard_map(
        run, mesh=mesh, in_specs=in_specs, out_specs=out_specs, check_vma=False
    )
```

```python
import functools
import itertools
import math

import jax
import jax.numpy as jnp
from jax import lax
from jax.experimental import pallas as pl
from jax.experimental.pallas import tpu as pltpu
from jax.sharding import PartitionSpec as P

H = 4
HD = 256
EPS = 1e-06
NEG = -1e30
ROPE_BASE = 10000.0
AXES = ("fsdp", "blk")
BF = jnp.bfloat16
F32 = jnp.float32


def matmul(left_side, right_side):
    return jnp.dot(left_side, right_side, preferred_element_type=F32)


def matmul_nt(left_side, right_side):
    return lax.dot_general(
        left_side, right_side, (((1,), (1,)), ((), ())), preferred_element_type=F32
    )


def matmul_tn(left_side, right_side):
    return lax.dot_general(
        left_side, right_side, (((0,), (0,)), ((), ())), preferred_element_type=F32
    )


def rounded(values):
    return values.astype(BF)


NAMES = ("y", "x", "p", "h", "c")


class Grid:
    def __init__(self, mesh):
        self.fsdp = mesh.shape["fsdp"]
        self.blk = mesh.shape["blk"]
        self.sizes = {"y": self.fsdp // 2, "x": 2, "p": self.blk // 4, "h": 2, "c": 2}
        self.devices = self.fsdp * self.blk
        self.groups = self.devices // 4

    def places(self):
        f = lax.axis_index("fsdp")
        b = lax.axis_index("blk")
        return {"y": f // 2, "x": f % 2, "p": b // 4, "h": (b // 2) % 2, "c": b % 2}

    def coordinates(self):
        places = self.places()
        return jnp.stack([places[name] for name in NAMES]).astype(jnp.int32)

    def permute(self, values, masks):
        pairs = []
        for f in range(self.fsdp):
            for b in range(self.blk):
                at = {"y": f // 2, "x": f % 2, "p": b // 4, "h": (b // 2) % 2, "c": b % 2}
                for name, mask in masks.items():
                    at[name] = at[name] ^ mask
                pairs.append(
                    (
                        f * self.blk + b,
                        (at["y"] * 2 + at["x"]) * self.blk + at["p"] * 4 + at["h"] * 2 + at["c"],
                    )
                )
        return lax.ppermute(values, AXES, pairs)

    def parts(self, values, name):
        return [values] + [
            self.permute(values, {name: mask}) for mask in range(1, self.sizes[name])
        ]

    def order(self, names):
        out = []
        stride = 1
        for name in names:
            out.append((NAMES.index(name), stride))
            stride *= self.sizes[name]
        return tuple(out)

    def blocks_of(self, names):
        out = []
        for y in range(self.sizes["y"]):
            for x in range(2):
                for p in range(self.sizes["p"]):
                    for h in range(2 if "h" in names else 1):
                        for c in range(2 if "c" in names else 1):
                            out.append((y, x, p, h, c))
        return tuple(out)

    def tokens_in(self, rows, ties=()):
        other = self.permute(rows, {"h": 1})
        if ties:
            (other,) = stack([([other], None, None)], ties)
        return [rows, other, self.permute(rows, {"c": 1}), self.permute(other, {"c": 1})]

    def extent(self, names):
        return tuple(self.sizes[name] for name in names)


def up8(rows):
    return -(-rows // 8) * 8


TILE = 256
INNER = math.sqrt(2.0 / math.pi)
CUBIC = 0.044715


def chunk_of(rows):
    return min(rows, 256)


COST_FORWARD = 6
COST_BACKWARD = 0
COST_WEIGHTS = 4
COST_ATTEND = 4
COST_ATTEND_BACK = 10
COST_OUTER = 0
COST_LEAVE = 2
COST_ENTER = 2
LIGHT = pl.CostEstimate(flops=0, bytes_accessed=0, transcendentals=0)


def full(extent):
    return pl.BlockSpec(extent, lambda j: tuple([0] * len(extent)))


ANY = pl.BlockSpec(memory_space=pl.ANY)


def tied(body, operands, ties):
    if not ties:
        return body

    def run(*refs):
        body(*refs[:operands], *refs[operands + len(ties) :])

    return run


def kernel_call(body, grid, in_specs, out_specs, out_shape, scratch, ties=(), flops=0):
    return pl.pallas_call(
        tied(body, len(in_specs), ties),
        grid=grid,
        in_specs=in_specs + [ANY] * len(ties),
        out_specs=out_specs,
        out_shape=out_shape,
        scratch_shapes=scratch,
        cost_estimate=pl.CostEstimate(flops=flops, bytes_accessed=0, transcendentals=0),
        compiler_params=pltpu.CompilerParams(
            dimension_semantics=("arbitrary",), vmem_limit_bytes=48 * 1024 * 1024
        ),
    )


def whole_call(body, out_shape, coordinates, operands, ties=(), scratch=(), flops=0):
    count = len(operands)
    specs = [pl.BlockSpec(memory_space=pltpu.VMEM)] * count
    if coordinates is not None:
        operands = [coordinates, *operands]
        specs = [pl.BlockSpec(memory_space=pltpu.SMEM)] + specs
    return pl.pallas_call(
        tied(body, len(specs), ties),
        out_shape=out_shape,
        in_specs=specs + [ANY] * len(ties),
        scratch_shapes=list(scratch),
        cost_estimate=pl.CostEstimate(flops=flops, bytes_accessed=0, transcendentals=0),
        compiler_params=pltpu.CompilerParams(vmem_limit_bytes=48 * 1024 * 1024),
    )(*operands, *ties)


def left_columns(width):
    return (width // 256) * 128 + 128


def add_rows(start, size, value, own_ref, other_ref):
    half = own_ref.shape[0]
    if start < half:
        own_ref[start : start + size] += value
    else:
        other_ref[start - half : start - half + size] += value


CHUNKS = 4


def send_rows(other_ref, sent_refs):
    count = sent_refs[0].shape[0]
    for number, sent_ref in enumerate(sent_refs):
        sent_ref[...] = rounded(other_ref[number * count : (number + 1) * count])


def sent_chunks(rows, width):
    count = rows // 2 // CHUNKS
    return [full((count, width))] * CHUNKS, [shape(count, width)] * CHUNKS


def ff_forward_body(
    x0_ref, x1_ref, x2_ref, x3_ref, wg_ref, wu_ref, wd_ref, own_ref, g_ref, u_ref, *sent_refs
):
    *sent_refs, other_ref = sent_refs
    size = x0_ref.shape[0]

    @pl.when(pl.program_id(0) == 0)
    def _():
        own_ref[...] = jnp.zeros_like(own_ref)
        other_ref[...] = jnp.zeros_like(other_ref)

    wg, wu, wd = wg_ref[...], wu_ref[...], wd_ref[...]
    for number, x_ref in enumerate((x0_ref, x1_ref, x2_ref, x3_ref)):
        start = number * size
        part = slice(start, start + size)
        x = x_ref[...]
        gate = matmul(x, wg)
        up = matmul(x, wu)
        g_ref[part] = rounded(gate)
        u_ref[part] = rounded(up)
        bent = jnp.tanh(INNER * (gate + CUBIC * (gate * gate * gate)))
        hidden = rounded(0.5 * gate * (1.0 + bent) * up)
        add_rows(start, size, matmul(hidden, wd), own_ref, other_ref)

    @pl.when(pl.program_id(0) == pl.num_programs(0) - 1)
    def _():
        send_rows(other_ref, sent_refs)


def ff_forward(blocks, w_gate, w_up, w_down, ties=()):
    size, width = blocks[0].shape
    rows = 4 * size
    wide = w_gate.shape[1]
    column = pl.BlockSpec((rows, TILE), lambda j: (0, j))
    return kernel_call(
        ff_forward_body,
        (wide // TILE,),
        [full((size, width))] * 4
        + [
            pl.BlockSpec((width, TILE), lambda j: (0, j)),
            pl.BlockSpec((width, TILE), lambda j: (0, j)),
            pl.BlockSpec((TILE, width), lambda j: (j, 0)),
        ],
        [full((rows // 2, width)), column, column] + sent_chunks(rows, width)[0],
        [
            jax.ShapeDtypeStruct((rows // 2, width), F32),
            jax.ShapeDtypeStruct((rows, wide), BF),
            jax.ShapeDtypeStruct((rows, wide), BF),
        ]
        + sent_chunks(rows, width)[1],
        [pltpu.VMEM((rows // 2, width), F32)],
        ties,
        int(COST_FORWARD * rows * width * wide),
    )(*blocks, w_gate, w_up, w_down, *ties)


def ff_backward_body(with_old, *refs):
    block_refs = refs[:4]
    g_ref, u_ref, wg_ref, wu_ref, wd_ref = refs[4:9]
    old_refs = refs[9:11] if with_old else None
    (
        own_ref, dg_ref, du_ref, dl_ref, dr_ref, *sent_refs, hidden_ref, other_ref, gg_ref,
    ) = refs[11 if with_old else 9 :]
    size = block_refs[0].shape[0]
    rows = 4 * size

    @pl.when(pl.program_id(0) == 0)
    def _():
        own_ref[...] = jnp.zeros_like(own_ref)
        other_ref[...] = jnp.zeros_like(other_ref)
        for number, block_ref in enumerate(block_refs):
            gg_ref[number * size : (number + 1) * size] = block_ref[...]

    wg, wu, wd = wg_ref[...], wu_ref[...], wd_ref[...]
    for start in range(0, rows, size):
        part = slice(start, start + size)
        grad = matmul_nt(gg_ref[part], wd)
        gate = g_ref[part].astype(F32)
        up = u_ref[part].astype(F32)
        square = gate * gate
        bent = jnp.tanh(INNER * (gate + CUBIC * (square * gate)))
        half = 0.5 * (1.0 + bent)
        gelu = gate * half
        slope = half + (0.5 * INNER) * gate * (1.0 - bent * bent) * (1.0 + (3.0 * CUBIC) * square)
        hidden_ref[part] = rounded(gelu * up)
        grad_gate = rounded(grad * up * slope)
        grad_up = rounded(grad * gelu)
        dg_ref[part] = grad_gate
        du_ref[part] = grad_up
        add_rows(
            start, size, matmul_nt(grad_gate, wg) + matmul_nt(grad_up, wu), own_ref, other_ref
        )
    total = matmul_tn(hidden_ref[...], gg_ref[...])
    left = dl_ref.shape[1]
    for number, (out_ref, part) in enumerate(((dl_ref, total[:, :left]), (dr_ref, total[:, left:]))):
        if old_refs is not None:
            part = part + old_refs[number][...].astype(F32)
        out_ref[...] = rounded(part)

    @pl.when(pl.program_id(0) == pl.num_programs(0) - 1)
    def _():
        send_rows(other_ref, sent_refs)


def ff_backward(blocks, gate, up, w_gate, w_up, w_down, old, ties=()):
    size, width = blocks[0].shape
    rows = 4 * size
    wide = w_gate.shape[1]
    left = left_columns(width)
    column = pl.BlockSpec((rows, TILE), lambda j: (0, j))
    halves = [pl.BlockSpec((TILE, cols), lambda j: (j, 0)) for cols in (left, width - left)]
    in_specs = [full((size, width))] * 4 + [
        column,
        column,
        pl.BlockSpec((width, TILE), lambda j: (0, j)),
        pl.BlockSpec((width, TILE), lambda j: (0, j)),
        pl.BlockSpec((TILE, width), lambda j: (j, 0)),
    ]
    operands = [*blocks, gate, up, w_gate, w_up, w_down]
    if old is not None:
        in_specs += halves
        operands += list(old)
    return kernel_call(
        functools.partial(ff_backward_body, old is not None),
        (wide // TILE,),
        in_specs,
        [full((rows // 2, width)), column, column] + halves + sent_chunks(rows, width)[0],
        [
            jax.ShapeDtypeStruct((rows // 2, width), F32),
            jax.ShapeDtypeStruct((rows, wide), BF),
            jax.ShapeDtypeStruct((rows, wide), BF),
            jax.ShapeDtypeStruct((wide, left), BF),
            jax.ShapeDtypeStruct((wide, width - left), BF),
        ]
        + sent_chunks(rows, width)[1],
        [
            pltpu.VMEM((rows, TILE), BF),
            pltpu.VMEM((rows // 2, width), F32),
            pltpu.VMEM((rows, width), BF),
        ],
        ties,
        int(COST_BACKWARD * rows * width * wide),
    )(*operands, *ties)


def ff_weights_body(split, with_old, *refs):
    if split:
        (extent, stages), coords_ref, refs = split, refs[0], refs[1:]
    x_refs = refs[:4]
    dg_ref, du_ref = refs[4:6]
    old_refs = refs[6:8] if with_old else (None, None)
    refs = refs[8 if with_old else 6 :]
    outs, turned_ref = refs[: 4 if split else 2], refs[4 if split else 2]
    size = x_refs[0].shape[0]

    @pl.when(pl.program_id(0) == 0)
    def _():
        for number, x_ref in enumerate(x_refs):
            turned_ref[:, number * size : (number + 1) * size] = x_ref[...].T

    for kind, grad_ref in enumerate((dg_ref, du_ref)):
        total = matmul(turned_ref[...], grad_ref[...])
        if with_old:
            total = total + old_refs[kind][...].astype(F32)
        total = rounded(total)
        if not split:
            outs[kind][...] = total
            continue
        held_ref = refs[5]
        rows = held_ref.shape[-2]
        for number, index in enumerate(itertools.product(*[range(count) for count in extent])):
            held_ref[index] = total[number * rows : (number + 1) * rows]
        name, position = stages[kind]
        rest = [range(count) for number, count in enumerate(extent) if number != position]
        for side in range(2):
            for index in itertools.product(*rest):
                source = index[:position] + (coords_ref[name] ^ side,) + index[position:]
                outs[2 * kind + side][index] = held_ref[source]


def ff_weights(grid, coordinates, blocks, grad_gate, grad_up, old, stages=None, ties=()):
    size, width = blocks[0].shape
    rows = 4 * size
    wide = grad_gate.shape[1]
    column = pl.BlockSpec((rows, TILE), lambda j: (0, j))
    block = pl.BlockSpec((width, TILE), lambda j: (0, j))
    in_specs = [full((size, width))] * 4 + [column, column]
    operands = [*blocks, grad_gate, grad_up]
    scratch = [pltpu.VMEM((width, rows), BF)]
    if old is not None:
        in_specs += [block, block]
        operands += list(old)
    if stages is None:
        split = None
        outs = [jax.ShapeDtypeStruct((width, wide), BF)] * 2
        out_specs = [block, block]
    else:
        names = ("y", "x", "p")
        extent = grid.extent(names)
        split = (extent, [(NAMES.index(stage), names.index(stage)) for stage in stages])
        piece = width // grid.groups
        in_specs = [pl.BlockSpec(memory_space=pltpu.SMEM)] + in_specs
        operands = [coordinates] + operands
        scratch.append(pltpu.VMEM(extent + (piece, TILE), BF))
        outs = []
        out_specs = []
        for stage in stages:
            left = grid.extent([name for name in names if name != stage])
            for side in range(2):
                outs.append(jax.ShapeDtypeStruct(left + (piece, wide), BF))
                out_specs.append(
                    pl.BlockSpec(left + (piece, TILE), lambda j: (0,) * (len(left) + 1) + (j,))
                )
    return kernel_call(
        functools.partial(ff_weights_body, split, old is not None),
        (wide // TILE,),
        in_specs,
        out_specs,
        outs,
        scratch,
        ties,
        int(COST_WEIGHTS * rows * width * wide),
    )(*operands, *ties)


def stack_body(plan, *refs):
    out_at = sum(count for count, pick, columns in plan)
    at = 0
    for count, pick, columns in plan:
        group = refs[at : at + count]
        at += count
        for column in columns:
            out_ref = refs[out_at]
            out_at += 1
            for index, ref in enumerate(group):
                place = () if pick is None else (pick,)
                value = ref[place + (Ellipsis, column)]
                if count == 1:
                    out_ref[...] = value
                else:
                    out_ref[index] = value


def stack(items, ties=()):
    plan = []
    outs = []
    operands = []
    for parts, pick, widths in items:
        extent = parts[0].shape if pick is None else parts[0].shape[1:]
        widths = widths or [extent[-1]]
        if len(parts) > 1:
            extent = (len(parts),) + extent
        columns = []
        start = 0
        for columns_wide in widths:
            columns.append(slice(start, start + columns_wide))
            start += columns_wide
            outs.append(jax.ShapeDtypeStruct(extent[:-1] + (columns_wide,), parts[0].dtype))
        plan.append((len(parts), pick, columns))
        operands += parts
    return whole_call(functools.partial(stack_body, plan), outs, None, operands, ties)


def fold_body(plan, coords_ref, *refs):
    at = 0
    out_at = sum(count for item in plan for count in item["counts"])
    for item in plan:
        names, stage, size = item["names"], item["stage"], item["size"]
        outs = refs[out_at : out_at + size]
        out_at += size
        position = names.index(stage)
        own = coords_ref[NAMES.index(stage)]
        rest = [range(extent) for number, extent in enumerate(item["extent"]) if number != position]
        column = 0
        for count in item["counts"]:
            group = refs[at : at + count]
            at += count
            rows, cols = group[0].shape[-2:]
            for mask in range(size):
                for index in itertools.product(*rest):
                    source = index[:position] + (own ^ mask,) + index[position:]
                    if count == 1:
                        value = group[0][source]
                    else:
                        value = group[0][source].astype(F32)
                        for other in group[1:]:
                            value = value + other[source].astype(F32)
                        value = rounded(value)
                    out = outs[mask]
                    out[index + (slice(0, rows), slice(column, column + cols))] = value
                    if rows < out.shape[-2]:
                        out[index + (slice(rows, None), slice(column, column + cols))] = jnp.zeros(
                            (out.shape[-2] - rows, cols), out.dtype
                        )
            column += cols


def fold(grid, coordinates, items, ties=()):
    plan = []
    outs = []
    operands = []
    for names, stage, groups in items:
        rows = max(group[0].shape[-2] for group in groups)
        cols = sum(group[0].shape[-1] for group in groups)
        left = tuple(name for name in names if name != stage)
        size = grid.sizes[stage]
        plan.append(
            {
                "names": names,
                "stage": stage,
                "size": size,
                "extent": grid.extent(names),
                "counts": [len(group) for group in groups],
            }
        )
        outs += [jax.ShapeDtypeStruct(grid.extent(left) + (rows, cols), BF)] * size
        for group in groups:
            operands += [
                value.reshape(grid.extent(names) + value.shape[-2:]) for value in group
            ]
    results = whole_call(
        functools.partial(fold_body, plan), outs, coordinates, operands, ties
    )
    folded = []
    at = 0
    for names, stage, groups in items:
        size = grid.sizes[stage]
        kept = [results[at]] + [
            grid.permute(results[at + mask], {stage: mask}) for mask in range(1, size)
        ]
        folded.append((tuple(name for name in names if name != stage), kept))
        at += size
    return folded


def pair_body(own_ref, *refs):
    came_refs, (own_out, sent_out) = refs[:-2], refs[-2:]
    count = own_out.shape[0]
    step = came_refs[0].shape[0]
    for number, came_ref in enumerate(came_refs):
        start = number * step
        total = own_ref[start : start + step] + came_ref[...].astype(F32)
        if start < count:
            own_out[start : start + step] = total
        else:
            sent_out[start - count : start - count + step] = rounded(total)


def tokens_out(grid, own, sent, ties=()):
    came = [grid.permute(part, {"c": 1}) for part in sent]
    count, width = own.shape[0] // 2, own.shape[1]
    own, sent = whole_call(
        pair_body, [shape(count, width, F32), shape(count, width)], None, [own, *came], ties
    )
    return own, grid.permute(sent, {"h": 1})


def fetch(coords_ref, refs, order, block, place):
    index = 0
    for number, stride in order[:-1]:
        index = index + (coords_ref[number] ^ block[number]) * stride
    last = order[-1][0]
    side = coords_ref[last] ^ block[last]
    value = refs[-1][(index,) + place]
    for number in range(len(refs) - 1):
        value = jnp.where(side == number, refs[number][(index,) + place], value)
    return value


def quarter_of(coords_ref):
    return coords_ref[3] * 2 + coords_ref[4]


def cut_body(groups, block, block_up, coords_ref, w_ref, *refs):
    out_refs, held_ref = refs[:-1], refs[-1]
    own = quarter_of(coords_ref)
    held_ref[...] = jnp.zeros_like(held_ref)
    for quarter in range(4):
        slot = own ^ quarter
        for kind in range(2):
            for group in range(groups):
                at = kind * groups * 4 * block + (group * 4 + quarter) * block
                held_ref[slot, kind, :, group * block_up : group * block_up + block] = w_ref[
                    :, at : at + block
                ]
    for mask, out_ref in enumerate(out_refs):
        out_ref[...] = held_ref[mask]


def pick_of(own, refs, quarter):
    value = refs[3]
    for mask in range(3):
        value = jnp.where(own == quarter ^ mask, refs[mask], value)
    return value


def pieces_body(coords_ref, p0_ref, p1_ref, p2_ref, p3_ref, out_ref):
    own = quarter_of(coords_ref)
    rows = p0_ref.shape[1]
    for kind in range(2):
        refs = [ref[kind] for ref in (p0_ref, p1_ref, p2_ref, p3_ref)]
        for quarter in range(4):
            out_ref[kind, quarter * rows : (quarter + 1) * rows] = pick_of(own, refs, quarter)


def split_body(count, coords_ref, *refs):
    own = quarter_of(coords_ref)
    outs = refs[2 * count :]
    rows = outs[0].shape[1]
    for kind in range(2):
        total = refs[kind * count][...].astype(F32)
        for ref in refs[kind * count + 1 : (kind + 1) * count]:
            total = total + ref[...].astype(F32)
        total = rounded(total)
        for mask, out_ref in enumerate(outs):
            value = total[3 * rows :]
            for quarter in range(3):
                value = jnp.where(
                    own == quarter ^ mask, total[quarter * rows : (quarter + 1) * rows], value
                )
            out_ref[kind] = value


def join_body(groups, block, block_up, coords_ref, p0_ref, p1_ref, p2_ref, p3_ref, out_ref):
    own = quarter_of(coords_ref)
    for kind in range(2):
        refs = [ref[kind] for ref in (p0_ref, p1_ref, p2_ref, p3_ref)]
        for quarter in range(4):
            piece = pick_of(own, refs, quarter).astype(F32)
            for group in range(groups):
                at = kind * groups * 4 * block + (group * 4 + quarter) * block
                out_ref[:, at : at + block] = piece[
                    :, group * block_up : group * block_up + block
                ]


def order_body(blocks, orders, coords_ref, *refs):
    out_ref = refs[-1]
    count = (len(refs) - 1) // len(orders)
    at = 0
    for group, order in enumerate(orders):
        group_refs = refs[group * count : (group + 1) * count]
        rows, cols = group_refs[0].shape[1:]
        for number, block in enumerate(blocks):
            out_ref[number * rows : (number + 1) * rows, at : at + cols] = fetch(
                coords_ref, group_refs, order, block, (slice(None), slice(None))
            )
        at += cols


def in_order(grid, coordinates, *columns, ties=()):
    blocks = grid.blocks_of("pxy")
    orders = []
    flat = []
    count = max(len(parts) for parts, names in columns)
    for parts, names in columns:
        parts = [part.reshape((-1,) + part.shape[-2:]) for part in parts]
        order = grid.order(names)
        if len(parts) < count:
            parts = [jnp.concatenate(parts)]
            parts += parts * (count - 1)
            order = order + ((order[-1][0], -1),)
        flat += parts
        orders.append(order)
    rows = flat[0].shape[1]
    cols = sum(parts[0].shape[-1] for parts, names in columns)
    return whole_call(
        functools.partial(order_body, blocks, tuple(orders)),
        jax.ShapeDtypeStruct((grid.groups * rows, cols), flat[0].dtype),
        coordinates,
        flat,
        ties,
    )


def spread_body(sizes, coords_ref, normed_ref, low_ref, mixed_ref, side_ref, *refs):
    own_ref, sent_ref, held_ref = refs
    devices, qkv, joined, lift, lift_at, out, mixed, last, last_at = sizes
    held_ref[...] = jnp.zeros_like(held_ref)
    second = devices // 2 * joined
    for number in range(devices):
        core, place = number % 2, number // 2
        at = place * joined
        held_ref[core, :, at : at + qkv] = normed_ref[:, number * qkv : (number + 1) * qkv]
        at = at + lift_at
        held_ref[core, :, at : at + lift] = low_ref[:, number * lift : (number + 1) * lift]
        at = second + place * mixed
        held_ref[core, :, at : at + out] = mixed_ref[:, number * out : (number + 1) * out]
        at = at + last_at
        held_ref[core, :, at : at + last] = side_ref[:, number * last : (number + 1) * last]
    own_ref[...] = held_ref[coords_ref[4]]
    sent_ref[...] = held_ref[1 - coords_ref[4]]


def unpack_first_body(blocks, order, sizes, count, coords_ref, *refs):
    chunks = [refs[at : at + count] for at in range(0, len(refs) - 4, count)]
    w_ref, lift_ref, down_ref, gain_ref = refs[-4:]
    rows, rows_up, lift_rows, gain_cols = sizes
    gain_ref[...] = jnp.zeros_like(gain_ref)
    main = slice(0, rows)
    lift = slice(rows_up, rows_up + lift_rows)
    every = slice(None)
    for number, block in enumerate(blocks):
        place = slice(number * rows, (number + 1) * rows)
        lift_place = slice(number * lift_rows, (number + 1) * lift_rows)
        at = 0
        for chunk in chunks[:-1]:
            columns = slice(at, at + chunk[0].shape[-1])
            w_ref[place, columns] = fetch(coords_ref, chunk, order, block, (main, every))
            lift_ref[lift_place, columns] = fetch(coords_ref, chunk, order, block, (lift, every))
            at = columns.stop
        down_ref[place, :] = fetch(coords_ref, chunks[-1], order, block, (main, every))
        gain_ref[0:2, number * gain_cols : (number + 1) * gain_cols] = fetch(
            coords_ref,
            chunks[-1],
            order,
            block,
            (slice(rows_up, rows_up + 2), slice(0, gain_cols)),
        ).astype(F32)


def unpack_second_body(blocks, order, sizes, count, coords_ref, *refs):
    chunks = [refs[at : at + count] for at in range(0, len(refs) - 5, count)]
    out_ref, lift0_ref, lift1_ref, down_ref, late_ref = refs[-5:]
    rows, rows_up, lift_rows, lift_up, late_rows, late_up = sizes
    every = slice(None)
    main = slice(0, rows)
    fold_cols = chunks[-1][0].shape[-1]
    for number, block in enumerate(blocks):

        def get(chunk, start, size):
            return fetch(coords_ref, chunk, order, block, (slice(start, start + size), every))

        place = slice(number * rows, (number + 1) * rows)
        lift_place = slice(number * lift_rows, (number + 1) * lift_rows)
        at = 0
        for chunk in chunks[:-2]:
            columns = slice(at, at + chunk[0].shape[-1])
            out_ref[place, columns] = get(chunk, 0, rows)
            lift0_ref[lift_place, columns] = get(chunk, rows_up, lift_rows)
            lift1_ref[lift_place, columns] = get(chunk, rows_up + lift_up, lift_rows)
            at = columns.stop
        down_ref[place, :] = get(chunks[-2], 0, rows)
        late_place = slice(number * late_rows, (number + 1) * late_rows)
        for part in range(late_ref.shape[1] // fold_cols):
            late_ref[late_place, part * fold_cols : (part + 1) * fold_cols] = get(
                chunks[-1], part * late_up, late_rows
            )


def rotate(values, cosine_table, sine_table):
    halfway = values.shape[-1] // 2
    first_half = values[..., :halfway]
    second_half = values[..., halfway:]
    return jnp.concatenate(
        [
            first_half * cosine_table - second_half * sine_table,
            second_half * cosine_table + first_half * sine_table,
        ],
        axis=-1,
    )


def inverse_size(values):
    return lax.rsqrt(jnp.mean(values * values, axis=-1, keepdims=True) + EPS)


def norm_back(values, gain_row, grad):
    inverse = inverse_size(values)
    weighted = grad * gain_row
    inner = jnp.mean(weighted * values, axis=-1, keepdims=True)
    gain_grad = jnp.sum(grad * values * inverse, axis=0, keepdims=True)
    return inverse * weighted - values * (inverse * inverse * inverse) * inner, gain_grad


def shape(rows, cols, kind=BF):
    return jax.ShapeDtypeStruct((rows, cols), kind)


def pack_body(
    sizes, wq_ref, qd_ref, ql_ref, gain_ref, wo_ref, od_ref, ol_ref, first_ref, second_ref
):
    qkv_up, ql_up, out_up, ol_up = sizes
    for ref in (first_ref, second_ref):
        ref[...] = jnp.zeros_like(ref)
    rows, cols = wq_ref.shape
    lift_rows = ql_ref.shape[1]
    rank = qd_ref.shape[2]
    first_ref[:rows, :cols] = wq_ref[...]
    first_ref[qkv_up : qkv_up + lift_rows, :cols] = ql_ref[0]
    for loop in range(2):
        at = cols + loop * rank
        first_ref[:rows, at : at + rank] = qd_ref[loop]
    first_ref[qkv_up : qkv_up + 2, cols : cols + gain_ref.shape[1]] = gain_ref[...]
    rows, width = wo_ref.shape
    last_rows = ol_ref.shape[1]
    second_ref[:rows, :width] = wo_ref[...]
    for loop in range(2):
        at = out_up + loop * ol_up
        second_ref[at : at + last_rows, :width] = ol_ref[loop]
        at = width + loop * rank
        second_ref[:rows, at : at + rank] = od_ref[loop]
    for part in range(cols // rank):
        second_ref[part * ql_up : part * ql_up + lift_rows, width + 2 * rank :] = ql_ref[
            1, :, part * rank : (part + 1) * rank
        ]


def rows_body(w_ref, out_ref):
    out_ref[...] = jnp.zeros_like(out_ref)
    out_ref[: w_ref.shape[0]] = w_ref[...]


def project_kv_body(first_loop, addends, *refs):
    add_refs = refs[:addends]
    gain_ref, qd_ref, w_ref, ql_ref, cos_ref, sin_ref = refs[addends : addends + 6]
    kv_ref, normed_ref, low_ref, residual_ref = refs[addends + 6 :]
    rank = low_ref.shape[1]
    width_q = w_ref.shape[1] - 2 * HD
    values = add_refs[0][...].astype(F32)
    for ref in add_refs[1:]:
        values = values + ref[...].astype(F32)
    residual_ref[...] = values
    normed = rounded(values * inverse_size(values) * gain_ref[0:1])
    normed_ref[...] = normed
    down = qd_ref[:, :rank] if first_loop else qd_ref[:, rank:]
    low = rounded(matmul(normed, down))
    low_ref[...] = low
    kv = matmul(normed, w_ref[:, width_q:]) + matmul(low, ql_ref[:, width_q:])
    kv_ref[:, :HD] = rounded(rotate(kv[:, :HD], cos_ref[...], sin_ref[...]))
    kv_ref[:, HD:] = rounded(kv[:, HD:])


def project_q_body(normed_ref, low_ref, w_ref, ql_ref, cos_ref, sin_ref, q_ref):
    for head in range(H):
        at = slice(head * HD, (head + 1) * HD)
        part = matmul(normed_ref[...], w_ref[:, at]) + matmul(low_ref[...], ql_ref[:, at])
        q_ref[:, at] = rounded(rotate(part, cos_ref[...], sin_ref[...]) * HD ** (-0.5))


def mask_of(segs_ref, places_ref, row_ref):
    seq_len = row_ref.shape[1]
    key_places = lax.broadcasted_iota(jnp.int32, (segs_ref.shape[0], seq_len), 1)
    allowed = (segs_ref[...] == row_ref[...]) & (key_places <= places_ref[...])
    return jnp.where(allowed, 0.0, NEG)


def attend_body(entries, coords_ref, q_ref, segs_ref, places_ref, row_ref, *refs):
    mixed_ref, log_ref, kv_ref = refs[-3:]
    for (p_mask, h_mask, c_mask), number, index in entries:
        value = refs[number][...] if index is None else refs[number][index]
        size = value.shape[0]
        block = (coords_ref[2] ^ p_mask) * 4 + (coords_ref[3] ^ h_mask) * 2
        block = block + (coords_ref[4] ^ c_mask)
        kv_ref[pl.ds(pl.multiple_of(block * size, size), size), :] = value
    mask = mask_of(segs_ref, places_ref, row_ref)
    for head in range(H):
        at = slice(head * HD, (head + 1) * HD)
        scores = matmul_nt(q_ref[:, at], kv_ref[:, :HD]) + mask
        top = jnp.max(scores, axis=1, keepdims=True)
        probabilities = jnp.exp(scores - top)
        total = jnp.sum(probabilities, axis=1, keepdims=True)
        mixed_ref[:, at] = rounded(matmul(rounded(probabilities), kv_ref[:, HD:]) / total)
        log_ref[head] = top + jnp.log(total)


def attend_back_body(
    q_ref, kv_ref, segs_ref, places_ref, row_ref, log_ref, grad_ref, cos_ref, sin_ref,
    coords_ref, own_ref, sent_ref, gq_ref, keys_ref, values_ref,
):
    mask = mask_of(segs_ref, places_ref, row_ref)
    size = own_ref.shape[1]
    for head in range(H):
        at = slice(head * HD, (head + 1) * HD)
        queries = q_ref[:, at]
        grad = grad_ref[:, at]
        probabilities = jnp.exp(matmul_nt(queries, kv_ref[:, :HD]) + mask - log_ref[head])
        grad_probs = matmul_nt(grad, kv_ref[:, HD:])
        weighted = probabilities * grad_probs
        delta = jnp.sum(weighted, axis=1, keepdims=True)
        grad_scores = rounded(weighted - probabilities * delta)
        grad_q = matmul(grad_scores, kv_ref[:, :HD])
        gq_ref[:, at] = rounded(rotate(grad_q, cos_ref[...], -sin_ref[...]) * HD ** (-0.5))
        key_term = matmul_tn(grad_scores, queries)
        value_term = matmul_tn(rounded(probabilities), grad)
        if head == 0:
            keys_ref[...] = key_term
            values_ref[...] = value_term
        else:
            keys_ref[...] += key_term
            values_ref[...] += value_term
    core = coords_ref[4]
    for number in range(own_ref.shape[0]):
        for out_ref, which in ((own_ref, core), (sent_ref, 1 - core)):
            place = pl.ds(pl.multiple_of((2 * number + which) * size, size), size)
            out_ref[number, :, :HD] = rounded(keys_ref[place, :])
            out_ref[number, :, HD:] = rounded(values_ref[place, :])


def leave_body(
    first_loop, mixed_ref, od_ref, w_ref, ol_ref, residual_ref, gain_ref,
    side_ref, middle_ref, normed_ref,
):
    rank = side_ref.shape[1]
    down = od_ref[:, :rank] if first_loop else od_ref[:, rank:]
    side = rounded(matmul(mixed_ref[...], down))
    side_ref[...] = side
    middle = residual_ref[...] + (matmul(mixed_ref[...], w_ref[...]) + matmul(side, ol_ref[...]))
    middle_ref[...] = middle
    normed_ref[...] = rounded(middle * inverse_size(middle) * gain_ref[1:2])


def enter_back_body(
    first_loop, own_ref, other_ref, result_ref, middle_ref, gain_ref, w_ref, ol_ref, od_ref,
    grad_ref, branch_ref, side_ref, mixed_ref, gain_grad_ref,
):
    rank = side_ref.shape[1]
    grad_normed = own_ref[...] + other_ref[...].astype(F32)
    back, gain_grad = norm_back(middle_ref[...], gain_ref[1:2], grad_normed)
    gain_grad_ref[...] = jnp.broadcast_to(gain_grad, gain_grad_ref.shape)
    grad = result_ref[...].astype(F32) + back
    grad_ref[...] = grad
    branch = rounded(grad)
    branch_ref[...] = branch
    side = rounded(matmul_nt(branch, ol_ref[...]))
    side_ref[...] = side
    down = od_ref[:, :rank] if first_loop else od_ref[:, rank:]
    mixed_ref[...] = rounded(matmul_nt(branch, w_ref[...]) + matmul_nt(side, down))


def rope_back_body(count, *refs):
    gq_ref, ql_ref, cos_ref, sin_ref, out_ref, low_ref = refs[count:]
    width_q = gq_ref.shape[1]
    kv = refs[0][...].astype(F32)
    for ref in refs[1:count]:
        kv = kv + ref[...].astype(F32)
    keys = rounded(rotate(kv[:, :HD], cos_ref[...], -sin_ref[...]))
    values = rounded(kv[:, HD:])
    out_ref[:, :HD] = keys
    out_ref[:, HD:] = values
    low_ref[...] = rounded(
        matmul_nt(gq_ref[...], ql_ref[:, :width_q])
        + matmul_nt(keys, ql_ref[:, width_q : width_q + HD])
        + matmul_nt(values, ql_ref[:, width_q + HD :])
    )


def leave_back_body(
    first_loop, kv_ref, gq_ref, low_ref, w_ref, qd_ref, residual_ref, gain_ref, grad_ref,
    other_gain_ref, *refs,
):
    out_ref, out_b_ref, gain_grad_ref = refs[-3:]
    rank = low_ref.shape[1]
    width_q = gq_ref.shape[1]
    down = qd_ref[:, :rank] if first_loop else qd_ref[:, rank:]
    grad_normed = (
        matmul_nt(gq_ref[...], w_ref[:, :width_q])
        + matmul_nt(kv_ref[...], w_ref[:, width_q:])
        + matmul_nt(low_ref[...], down)
    )
    back, gain_grad = norm_back(residual_ref[...], gain_ref[0:1], grad_normed)
    gain_grad_ref[0:1] = gain_grad
    gain_grad_ref[1:2] = other_gain_ref[1:2]
    if len(refs) > 3:
        gain_grad_ref[0:2] += refs[0][0:2]
    grad = grad_ref[...] + back
    out_ref[...] = grad
    out_b_ref[...] = rounded(grad)


def late_body(sizes, coords_ref, kv_ref, qd_ref, *refs):
    count, rows, gain_cols = sizes
    gain_refs, out_ref = refs[:-1], refs[-1]
    kv_cols = kv_ref.shape[2]
    out_ref[:, :, :kv_cols] = kv_ref[...]
    out_ref[:, :, kv_cols:] = qd_ref[...]
    for row in range(2):
        gains = rounded(gain_refs[0][row : row + 1] + gain_refs[1][row : row + 1])
        for number in range(count):
            at = 2 * number * gain_cols
            value = jnp.where(
                coords_ref[4] == 0,
                gains[:, at : at + gain_cols],
                gains[:, at + gain_cols : at + 2 * gain_cols],
            )
            out_ref[number, rows + row : rows + row + 1, kv_cols : kv_cols + gain_cols] = value


def down_body(count, *refs):
    out_ref = refs[-1]
    at = 0
    for group in range(2):
        value = refs[group * count][...].astype(F32)
        for ref in refs[group * count + 1 : (group + 1) * count]:
            value = value + ref[...].astype(F32)
        out_ref[:, at : at + value.shape[1]] = value[: out_ref.shape[0]]
        at += value.shape[1]


def result_body(middle_ref, own_ref, other_ref, out_ref):
    out_ref[...] = rounded(middle_ref[...] + (own_ref[...] + other_ref[...].astype(F32)))


def finish_body(count, sizes, *refs):
    rows, rows_up, lift_rows, lift_up, out_rows, out_up, last_rows, last_up, gain_cols = sizes
    totals = []
    for group in range(3):
        value = refs[group * count][...].astype(F32)
        for ref in refs[group * count + 1 : (group + 1) * count]:
            value = value + ref[...].astype(F32)
        totals.append(value)
    outs, queries, late = totals
    gains_ref, qkv_ref, out_ref, qd_ref, ql_ref, od_ref, ol_ref = refs[3 * count :]
    width = out_ref.shape[1]
    rank = qd_ref.shape[2]
    half = queries.shape[1] - rank
    rest = qkv_ref.shape[1] - half
    gains_ref[...] = late[rows : rows + 2, rest : rest + gain_cols]
    qkv_ref[:, :half] = queries[:rows, :half]
    qkv_ref[:, half:] = late[:rows, :rest]
    out_ref[...] = outs[:out_rows, :width]
    qd_ref[0] = late[:rows, rest:]
    qd_ref[1] = queries[:rows, half:]
    for loop in range(2):
        at = rows_up + loop * lift_up
        ql_ref[loop, :, :half] = queries[at : at + lift_rows, :half]
        ql_ref[loop, :, half:] = late[at : at + lift_rows, :rest]
        at = width + loop * rank
        od_ref[loop] = outs[:out_rows, at : at + rank]
        at = out_up + loop * last_up
        ol_ref[loop] = outs[at : at + last_rows, :width]


def outer_body(columns, rights, olds, own_ref, came_ref, *refs):
    out_refs = refs[2 * rights + olds :]
    own, came = own_ref[:, columns], came_ref[:, columns]
    for number in range(rights):
        right_ref, right_came_ref = refs[2 * number], refs[2 * number + 1]
        out_ref = out_refs[number]
        cols = out_ref.shape[1]
        step = 512 if cols % 512 == 0 else 384 if cols % 384 == 0 else cols
        for start in range(0, cols, step):
            part = slice(start, start + step)
            total = matmul_tn(own, right_ref[:, part]) + matmul_tn(came, right_came_ref[:, part])
            if number < olds:
                total = total + refs[2 * rights + number][:, part].astype(F32)
            out_ref[:, part] = rounded(total)


def outer(left, columns, rights, olds=(), ties=()):
    rows = columns.stop - columns.start
    return whole_call(
        functools.partial(outer_body, columns, len(rights), len(olds)),
        [shape(rows, right[0].shape[1]) for right in rights],
        None,
        [*left, *[value for right in rights for value in right], *olds],
        ties,
        flops=int(COST_OUTER * rows * columns.stop * sum(value[0].shape[1] for value in rights)),
    )


def per_device(
    grid,
    inputs,
    segments,
    cotangent,
    norm_gain_rows,
    query_key_value_weight,
    output_weight,
    gate_up_weight,
    down_weight,
    adapter_query_down,
    adapter_query_lift,
    adapter_output_down,
    adapter_output_lift,
):
    tokens = inputs.shape[0]
    width = inputs.shape[1]
    groups = grid.groups
    gain_cols = norm_gain_rows.shape[1]
    qkv_rows = query_key_value_weight.shape[0]
    out_rows = output_weight.shape[0]
    ql_rows = adapter_query_lift.shape[1]
    ol_rows = adapter_output_lift.shape[1]
    rank = adapter_query_down.shape[2]
    hidden_block = down_weight.shape[0]
    width_q = H * HD

    qkv_up, ql_up = up8(qkv_rows), up8(ql_rows)
    out_up, ol_up = up8(out_rows), up8(ol_rows)
    wide = -(-groups * hidden_block // TILE) * TILE
    block_up = wide // groups
    qkv_cols = query_key_value_weight.shape[1]
    left_cols = left_columns(width)
    coordinates = grid.coordinates()
    straight = ("p", "h", "x", "y", "c")
    turned = ("p", "h", "y", "x", "c")

    def flat(parts):
        return [part.reshape((-1,) + part.shape[-2:]) for part in parts]

    def parts(values, name):
        return grid.parts(values, name)

    segrow = segments[0]
    seq_len = segrow.shape[0]
    position = lax.axis_index("blk")
    places = position * tokens + jnp.arange(tokens, dtype=jnp.int32)
    own_segs = lax.dynamic_slice_in_dim(segrow, position * tokens, tokens, 0)
    below_one = jnp.sum((segrow < 1).astype(jnp.int32))
    below_two = jnp.sum((segrow < 2).astype(jnp.int32))
    starts = jnp.where(own_segs == 0, 0, jnp.where(own_segs == 1, below_one, below_two))
    offsets = (places - starts).astype(F32)
    frequency = jnp.exp(jnp.arange(HD // 2, dtype=F32) * (-2.0 * math.log(ROPE_BASE) / HD))
    angles = offsets[:, None] * frequency[None, :]
    tables = [jnp.cos(angles), jnp.sin(angles)]
    masks = [own_segs[:, None], places[:, None], segments]

    second_rows = max(out_up + 2 * ol_up, qkv_cols // rank * ql_up)
    first, second = whole_call(
        functools.partial(pack_body, (qkv_up, ql_up, out_up, ol_up)),
        [shape(qkv_up + ql_up, qkv_cols + 2 * rank), shape(second_rows, width + 3 * rank)],
        None,
        [
            query_key_value_weight, adapter_query_down, adapter_query_lift, norm_gain_rows,
            output_weight, adapter_output_down, adapter_output_lift,
        ],
    )
    first, second = stack([(parts(first, "p"), None, None), (parts(second, "p"), None, None)])
    cut = whole_call(
        functools.partial(cut_body, groups, hidden_block, block_up),
        [jax.ShapeDtypeStruct((2, qkv_rows, wide), BF)] * 4,
        coordinates,
        [gate_up_weight],
        [first],
        [pltpu.VMEM((4, 2, qkv_rows, wide), BF)],
    )
    down = whole_call(
        rows_body, shape(block_up, width), None, [down_weight], [cut[0]]
    )
    first, second = stack(
        [(parts(first, "h"), None, None), (parts(second, "h"), None, None)], [down]
    )
    gate_up = whole_call(
        pieces_body,
        jax.ShapeDtypeStruct((2, 4 * qkv_rows, wide), BF),
        coordinates,
        [
            cut[0],
            grid.permute(cut[1], {"c": 1}),
            grid.permute(cut[2], {"h": 1}),
            grid.permute(cut[3], {"h": 1, "c": 1}),
        ],
        [first],
    )
    first, second = stack(
        [(parts(first, "x"), None, None), (parts(second, "y"), None, None)], [gate_up]
    )
    gate_up = parts(gate_up, "p")
    first_chunks = [qkv_cols // 3] * 3 + [2 * rank]
    second_chunks = [width - left_cols, left_cols, 2 * rank, rank]
    chunks = stack(
        [
            (parts(first, "y"), None, first_chunks),
            (parts(second, "x"), None, second_chunks),
        ]
    )
    chunks = [flat(parts(chunk, "c")) for chunk in chunks]
    first = [part for chunk in chunks[:4] for part in chunk]
    second = [part for chunk in chunks[4:] for part in chunk]
    gate, up, down = stack(
        [
            (gate_up, 0, None),
            (gate_up, 1, None),
            ([down], None, None),
        ],
        [chunks[0][0]],
    )
    gate, up = parts(gate, "x"), parts(up, "y")
    down = parts(down, "p")
    w_qkv, ql_0, qd, gains = whole_call(
        functools.partial(
            unpack_first_body,
            grid.blocks_of(straight),
            grid.order(straight),
            (qkv_rows, qkv_up, ql_rows, gain_cols),
            2,
        ),
        [shape(width, qkv_cols), shape(rank, qkv_cols), shape(width, 2 * rank), shape(8, width, F32)],
        coordinates,
        first,
        [gate[0]],
    )
    lifts_in = [ql_0, None]

    def project_kv(addends, loop):
        own_kv, normed_b, low_rank_b, residual = whole_call(
            functools.partial(project_kv_body, loop == 0, len(addends)),
            [
                shape(tokens, 2 * HD), shape(tokens, width), shape(tokens, rank),
                shape(tokens, width, F32),
            ],
            None,
            [*addends, gains, qd, w_qkv, lifts_in[loop], *tables],
        )
        return own_kv, normed_b, low_rank_b, residual

    def gather_kv(own_kv):
        chips = {(0, 0): own_kv}
        for p_mask in range(grid.sizes["p"]):
            for h_mask in range(2):
                if p_mask or h_mask:
                    chips[p_mask, h_mask] = grid.permute(own_kv, {"p": p_mask, "h": h_mask})
        kv_parts = {(*mask, 0): value for mask, value in chips.items()}
        for mask, value in chips.items():
            kv_parts[(*mask, 1)] = grid.permute(value, {"c": 1})
        entries = [(mask, number, None) for number, mask in enumerate(kv_parts)]
        return entries, list(kv_parts.values())

    def gather_kv_staged(own_kv, ties):
        (near,) = stack([(parts(own_kv, "p"), None, None)], ties)
        far = grid.permute(near, {"h": 1})
        entries = [
            ((p_mask, h_mask, c_mask), 2 * c_mask + h_mask, p_mask)
            for c_mask in range(2)
            for h_mask in range(2)
            for p_mask in range(grid.sizes["p"])
        ]
        return entries, [near, far, grid.permute(near, {"c": 1}), grid.permute(far, {"c": 1})]

    def project_q(projected, loop, ties=()):
        return whole_call(
            project_q_body,
            shape(tokens, width_q),
            None,
            [projected[1], projected[2], w_qkv, lifts_in[loop], *tables],
            ties,
        )

    def attend(queries, gathered, ties=()):
        entries, operands = gathered
        return whole_call(
            functools.partial(attend_body, entries),
            [
                shape(tokens, width_q),
                jax.ShapeDtypeStruct((H, tokens, 1), F32),
                shape(seq_len, 2 * HD),
            ],
            coordinates,
            [queries, *masks, *operands],
            ties,
            flops=int(COST_ATTEND * tokens * width_q * seq_len),
        )

    projected_one = project_kv([inputs], 0)
    gate, up, own_kv = stack(
        [(gate, None, None), (up, None, None), ([projected_one[0]], None, None)]
    )
    gate, up = parts(gate, "y"), parts(up, "x")
    w_out, ol_0, ol_1, od, ql_1 = whole_call(
        functools.partial(
            unpack_second_body,
            grid.blocks_of(straight),
            grid.order(turned),
            (out_rows, out_up, ol_rows, ol_up, ql_rows, ql_up),
            2,
        ),
        [
            shape(width_q, width), shape(rank, width), shape(rank, width),
            shape(width_q, 2 * rank), shape(rank, qkv_cols),
        ],
        coordinates,
        second,
        [gate[0]],
    )
    queries_one = project_q(projected_one, 0, [gate[0]])
    down_left, down_right = stack([(down, None, [left_cols, width - left_cols])], [queries_one])
    down_left, down_right = parts(down_left, "x"), parts(down_right, "y")
    attended_one = attend(queries_one, gather_kv_staged(own_kv, [down_left[0]]))
    down_left, down_right = stack(
        [(down_left, None, None), (down_right, None, None)], [attended_one[0]]
    )
    down_left, down_right = parts(down_left, "y"), parts(down_right, "x")
    lifts_in[1] = ql_1
    lifts_out = (ol_0, ol_1)

    def leave(loop, mixed_b, residual):
        return whole_call(
            functools.partial(leave_body, loop == 0),
            [shape(tokens, rank), shape(tokens, width, F32), shape(tokens, width)],
            None,
            [mixed_b, od, w_out, lifts_out[loop], residual, gains],
            flops=int(COST_LEAVE * tokens * width_q * width),
        )

    left_one = leave(0, attended_one[0], projected_one[3])
    w_gate = in_order(grid, coordinates, (gate, ("p", "x", "y")))
    w_up = in_order(grid, coordinates, (up, ("p", "y", "x")))
    w_down = in_order(
        grid, coordinates, (down_left, ("p", "x", "y")), (down_right, ("p", "y", "x"))
    )

    qkv_block = qkv_up + 2 * ql_up
    out_block = out_up + 2 * ol_up

    cotangent_in = grid.tokens_in(cotangent)

    def feed_forward(loop, projected, queries, attended, left, ties=()):
        own_kv, normed_b, low_rank_b, residual = projected
        mixed_b, log_total, both = attended
        side_b, middle, normed_ff_b = left
        spread_own, spread_sent = whole_call(
            functools.partial(
                spread_body,
                (
                    grid.devices, qkv_rows, qkv_block, ql_rows, qkv_up + loop * ql_up,
                    out_rows, out_block, ol_rows, out_up + loop * ol_up,
                ),
            ),
            [shape(tokens, grid.devices // 2 * (qkv_block + out_block))] * 2,
            coordinates,
            [normed_b, low_rank_b, mixed_b, side_b],
            (),
            [pltpu.VMEM((2, tokens, grid.devices // 2 * (qkv_block + out_block)), BF)],
        )
        ff_in = grid.tokens_in(normed_ff_b, [spread_sent])
        ff_own, gate_b, up_b, *ff_sent = ff_forward(ff_in, w_gate, w_up, w_down)
        own, other = tokens_out(grid, ff_own, ff_sent, ties)
        cache = (
            residual, (spread_own, grid.permute(spread_sent, {"c": 1})), queries, both, log_total,
            middle, ff_in, gate_b, up_b,
        )
        return [middle, own, other], cache

    addends, cache_one = feed_forward(
        0, projected_one, queries_one, attended_one, left_one, [cotangent_in[1]]
    )
    projected_two = project_kv(addends, 1)
    queries_two = project_q(projected_two, 1)
    attended_two = attend(queries_two, gather_kv(projected_two[0]))
    left_two = leave(1, attended_two[0], projected_two[3])
    addends, cache_two = feed_forward(
        1, projected_two, queries_two, attended_two, left_two
    )
    result = whole_call(result_body, shape(tokens, width), None, addends)

    group_names = ("y", "x", "p")
    names = ("y", "x", "p", "h")
    half = grid.devices // 2
    joined_columns = slice(0, half * qkv_block)
    mixed_columns = slice(half * qkv_block, half * (qkv_block + out_block))

    def step(stages, ties=()):
        return fold(
            grid, coordinates, [(item[0], stage, [item[1]]) for item, stage in stages], ties
        )

    y_size = grid.sizes["y"]

    def with_core(values):
        return values, grid.permute(values, {"c": 1})

    def backward_loop(cache, grad_result, blocks_in, loop, old):
        (
            residual, spreads, queries, both, log_total, middle, ff_in, gate_b, up_b,
        ) = cache
        last = old is not None
        ql, ol = lifts_in[loop], lifts_out[loop]

        def before(name):
            return old[name] if last else None

        def grouped(values):
            return values.reshape(groups, values.shape[0] // groups, values.shape[1])

        own, grad_gate_b, grad_up_b, *down = ff_backward(
            blocks_in, gate_b, up_b, w_gate, w_up, w_down, before("down")
        )
        down, sent = down[:2], down[2:]
        ties = [] if last else [result]
        if last:
            down = fold(
                grid,
                coordinates,
                [
                    (group_names, "x", [[grouped(down[0])]]),
                    (group_names, "y", [[grouped(down[1])]]),
                ],
            )
            ties = [down[0][1][0]]
        own, other = tokens_out(grid, own, sent, ties)
        pair = ff_weights(
            grid,
            coordinates,
            ff_in,
            grad_gate_b,
            grad_up_b,
            (old["gate"], old["up"]) if last else None,
            ("x", "y" if y_size == 2 else "x") if last else None,
            [own],
        )
        ties = [pair[0]]
        if last:
            d_gate = (("y", "p"), [pair[0], grid.permute(pair[1], {"x": 1})])
            if y_size == 2:
                d_up = (("x", "p"), [pair[2], grid.permute(pair[3], {"y": 1})])
            else:
                d_up = (("y", "p"), [pair[2], grid.permute(pair[3], {"x": 1})])
        else:
            d_gate, d_up = pair
        grad_middle, grad_branch_b, grad_side_b, grad_mixed_b, gain_grad_ff = whole_call(
            functools.partial(enter_back_body, loop == 0),
            [
                shape(tokens, width, F32), shape(tokens, width), shape(tokens, rank),
                shape(tokens, width_q), shape(8, width, F32),
            ],
            None,
            [own, other, grad_result, middle, gains, w_out, ol, od],
            ties,
            flops=int(COST_ENTER * tokens * width_q * width),
        )
        ties = []
        if last:
            down = fold(
                grid,
                coordinates,
                [(down[0][0], "y", [down[0][1]]), (down[1][0], "x", [down[1][1]])],
                [grad_mixed_b],
            )
            ties = [down[0][1][0]]
        kv_own, kv_sent, grad_queries_b = pl.pallas_call(
            tied(attend_back_body, 10, ties),
            out_shape=[jax.ShapeDtypeStruct((grid.blk // 2, tokens, 2 * HD), BF)] * 2
            + [shape(tokens, width_q)],
            in_specs=[pl.BlockSpec(memory_space=pltpu.VMEM)] * 9
            + [pl.BlockSpec(memory_space=pltpu.SMEM)]
            + [ANY] * len(ties),
            scratch_shapes=[pltpu.VMEM((seq_len, HD), F32)] * 2,
            cost_estimate=pl.CostEstimate(
                flops=int(COST_ATTEND_BACK * tokens * width_q * seq_len),
                bytes_accessed=0,
                transcendentals=0,
            ),
            compiler_params=pltpu.CompilerParams(vmem_limit_bytes=48 * 1024 * 1024),
        )(queries, both, *masks, log_total, grad_mixed_b, *tables, coordinates, *ties)
        grad_kv = (("p", "h"), [kv_own, grid.permute(kv_sent, {"c": 1})])
        (grad_kv,) = step([(grad_kv, "h")])
        (grad_kv,) = step([(grad_kv, "p")])
        branch, side = with_core(grad_branch_b), with_core(grad_side_b)
        d_out, d_od = outer(
            spreads, mixed_columns, [branch, side], [old["out"]] if last else [], [grad_kv[1][0]]
        )
        (d_queries,) = outer(
            spreads,
            joined_columns,
            [with_core(grad_queries_b)],
            [old["queries"]] if last else [],
            [d_out],
        )
        sums = {"out": d_out, "od": d_od, "queries": d_queries}

        def second_sums(ties):
            sums["gate"], sums["up"], down[0], down[1] = fold(
                grid,
                coordinates,
                [
                    (d_gate[0], "y", [d_gate[1]]),
                    (d_up[0], d_up[0][0], [d_up[1]]),
                    (down[0][0], "p", [down[0][1]]),
                    (down[1][0], "p", [down[1][1]]),
                ],
                ties,
            )

        ties = [] if last else [d_queries, cache_one[1][1]]
        if last:
            sums["out"], sums["queries"] = fold(
                grid,
                coordinates,
                [
                    (names, "x", [[blocks(value)] for value in (d_out, d_od, old["od"])]),
                    (names, "y", [[blocks(value)] for value in (d_queries, old["qd"])]),
                ],
            )
            second_sums([sums["out"][1][0]])
            ties = [sums["gate"][1][0]]
        else:
            sums["gate"], sums["up"] = d_gate, d_up
        sums["down"] = down
        grad_kv_b, grad_low_rank_b = whole_call(
            functools.partial(rope_back_body, len(grad_kv[1])),
            [shape(tokens, 2 * HD), shape(tokens, rank)],
            None,
            [*grad_kv[1], grad_queries_b, ql, *tables],
            ties,
        )
        sums["kv"], sums["qd"] = outer(
            spreads,
            joined_columns,
            [with_core(grad_kv_b), with_core(grad_low_rank_b)],
            [old["kv"]] if last else [],
        )
        following, following_b, gain_grads = whole_call(
            functools.partial(leave_back_body, loop == 0),
            [shape(tokens, width, F32), shape(tokens, width), shape(8, width, F32)],
            None,
            [
                grad_kv_b, grad_queries_b, grad_low_rank_b, w_qkv, qd, residual, gains,
                grad_middle, gain_grad_ff,
            ]
            + ([old["gains"]] if last else []),
        )
        sums["gains"] = gain_grads
        return following, following_b, sums

    def blocks(values):
        return values.reshape(half, values.shape[0] // half, values.shape[1])

    grad_one, grad_one_b, sums_two = backward_loop(cache_two, cotangent, cotangent_in, 1, None)
    grad_inputs, unused, sums = backward_loop(
        cache_one, grad_one, grid.tokens_in(grad_one_b), 0, sums_two
    )

    late = whole_call(
        functools.partial(late_body, (half, qkv_rows, gain_cols)),
        jax.ShapeDtypeStruct((half, qkv_block, 2 * HD + rank), BF),
        coordinates,
        [blocks(sums["kv"]), blocks(sums["qd"]), *with_core(sums["gains"])],
    )
    (late,) = step([((names, [late]), "x")])
    d_down = whole_call(
        functools.partial(down_body, len(sums["down"][0][1])),
        shape(hidden_block, width, F32),
        None,
        sums["down"][0][1] + sums["down"][1][1],
        [late[1][0]],
    )
    gate, up = step([(sums["gate"], "p"), (sums["up"], "p")], [d_down])
    outs, queries = step([(sums["out"], "y"), (sums["queries"], "x")], [gate[1][0]])
    (late,) = step([(late, "y")], [outs[1][0]])
    split = whole_call(
        functools.partial(split_body, len(gate[1])),
        [jax.ShapeDtypeStruct((2, qkv_rows, wide), BF)] * 4,
        coordinates,
        gate[1] + up[1],
        [late[1][0]],
    )
    back = [
        split[0],
        grid.permute(split[1], {"c": 1}),
        grid.permute(split[2], {"h": 1}),
        grid.permute(split[3], {"h": 1, "c": 1}),
    ]
    outs, queries, late = step([(outs, "h"), (queries, "h"), (late, "h")], [split[0]])
    outs, queries, late = step([(outs, "p"), (queries, "p"), (late, "p")])
    d_gate_up = whole_call(
        functools.partial(join_body, groups, hidden_block, block_up),
        shape(qkv_rows, 8 * groups * hidden_block, F32),
        coordinates,
        back,
    )
    last = [outs[1], queries[1], late[1]]
    d_gains, d_qkv, d_out, d_qd, d_ql, d_od, d_ol = whole_call(
        functools.partial(
            finish_body,
            len(outs[1]),
            (
                qkv_rows, qkv_up, ql_rows, ql_up, out_rows, out_up, ol_rows, ol_up, gain_cols,
            ),
        ),
        [
            shape(2, gain_cols, F32),
            shape(qkv_rows, qkv_cols, F32),
            shape(out_rows, width, F32),
            jax.ShapeDtypeStruct(adapter_query_down.shape, F32),
            jax.ShapeDtypeStruct(adapter_query_lift.shape, F32),
            jax.ShapeDtypeStruct(adapter_output_down.shape, F32),
            jax.ShapeDtypeStruct(adapter_output_lift.shape, F32),
        ],
        None,
        [value for values in last for value in values],
    )
    return (
        result, grad_inputs, d_gains, d_qkv, d_out, d_gate_up, d_down, d_qd, d_ql, d_od, d_ol,
    )


def solution(mesh):
    grid = Grid(mesh)
    rows = P(AXES, None)
    deep = P(None, AXES, None)
    in_specs = (
        rows, P("fsdp", None), rows, P(None, AXES), rows, rows, rows, rows, deep, deep, deep, deep,
    )
    out_specs = (
        rows, rows, P(None, AXES), rows, rows, rows, rows, deep, deep, deep, deep,
    )

    def run(*arguments):
        return per_device(grid, *arguments)

    return jax.shard_map(
        run, mesh=mesh, in_specs=in_specs, out_specs=out_specs, check_vma=False
    )
```

```python
import functools
import itertools
import math

import jax
import jax.numpy as jnp
from jax import lax
from jax.experimental import pallas as pl
from jax.experimental.pallas import tpu as pltpu
from jax.sharding import PartitionSpec as P

H = 4
HD = 256
EPS = 1e-06
NEG = -1e30
ROPE_BASE = 10000.0
AXES = ("fsdp", "blk")
BF = jnp.bfloat16
F32 = jnp.float32


def matmul(left_side, right_side):
    return jnp.dot(left_side, right_side, preferred_element_type=F32)


def matmul_nt(left_side, right_side):
    return lax.dot_general(
        left_side, right_side, (((1,), (1,)), ((), ())), preferred_element_type=F32
    )


def matmul_tn(left_side, right_side):
    return lax.dot_general(
        left_side, right_side, (((0,), (0,)), ((), ())), preferred_element_type=F32
    )


def rounded(values):
    return values.astype(BF)


NAMES = ("y", "x", "p", "h", "c")


class Grid:
    def __init__(self, mesh):
        self.fsdp = mesh.shape["fsdp"]
        self.blk = mesh.shape["blk"]
        self.sizes = {"y": self.fsdp // 2, "x": 2, "p": self.blk // 4, "h": 2, "c": 2}
        self.devices = self.fsdp * self.blk
        self.groups = self.devices // 4

    def places(self):
        f = lax.axis_index("fsdp")
        b = lax.axis_index("blk")
        return {"y": f // 2, "x": f % 2, "p": b // 4, "h": (b // 2) % 2, "c": b % 2}

    def coordinates(self):
        places = self.places()
        return jnp.stack([places[name] for name in NAMES]).astype(jnp.int32)

    def permute(self, values, masks):
        pairs = []
        for f in range(self.fsdp):
            for b in range(self.blk):
                at = {"y": f // 2, "x": f % 2, "p": b // 4, "h": (b // 2) % 2, "c": b % 2}
                for name, mask in masks.items():
                    at[name] = at[name] ^ mask
                pairs.append(
                    (
                        f * self.blk + b,
                        (at["y"] * 2 + at["x"]) * self.blk + at["p"] * 4 + at["h"] * 2 + at["c"],
                    )
                )
        return lax.ppermute(values, AXES, pairs)

    def parts(self, values, name):
        return [values] + [
            self.permute(values, {name: mask}) for mask in range(1, self.sizes[name])
        ]

    def order(self, names):
        out = []
        stride = 1
        for name in names:
            out.append((NAMES.index(name), stride))
            stride *= self.sizes[name]
        return tuple(out)

    def blocks_of(self, names):
        out = []
        for y in range(self.sizes["y"]):
            for x in range(2):
                for p in range(self.sizes["p"]):
                    for h in range(2 if "h" in names else 1):
                        for c in range(2 if "c" in names else 1):
                            out.append((y, x, p, h, c))
        return tuple(out)

    def tokens_in(self, rows, ties=()):
        other = self.permute(rows, {"h": 1})
        if ties:
            (other,) = stack([([other], None, None)], ties)
        return [rows, other, self.permute(rows, {"c": 1}), self.permute(other, {"c": 1})]

    def extent(self, names):
        return tuple(self.sizes[name] for name in names)


def up8(rows):
    return -(-rows // 8) * 8


TILE = 256
INNER = math.sqrt(2.0 / math.pi)
CUBIC = 0.044715


def chunk_of(rows):
    return min(rows, 256)


COST_FORWARD = 6
COST_BACKWARD = 0
COST_WEIGHTS = 4
COST_ATTEND = 4
COST_ATTEND_BACK = 10
COST_LEAVE = 2
COST_ENTER = 2
LIGHT = pl.CostEstimate(flops=0, bytes_accessed=0, transcendentals=0)


def full(extent):
    return pl.BlockSpec(extent, lambda j: tuple([0] * len(extent)))


ANY = pl.BlockSpec(memory_space=pl.ANY)


def tied(body, operands, ties):
    if not ties:
        return body

    def run(*refs):
        body(*refs[:operands], *refs[operands + len(ties) :])

    return run


def kernel_call(body, grid, in_specs, out_specs, out_shape, scratch, ties=(), flops=0):
    return pl.pallas_call(
        tied(body, len(in_specs), ties),
        grid=grid,
        in_specs=in_specs + [ANY] * len(ties),
        out_specs=out_specs,
        out_shape=out_shape,
        scratch_shapes=scratch,
        cost_estimate=pl.CostEstimate(flops=flops, bytes_accessed=0, transcendentals=0),
        compiler_params=pltpu.CompilerParams(
            dimension_semantics=("arbitrary",), vmem_limit_bytes=48 * 1024 * 1024
        ),
    )


def whole_call(body, out_shape, coordinates, operands, ties=(), scratch=(), flops=0):
    count = len(operands)
    specs = [pl.BlockSpec(memory_space=pltpu.VMEM)] * count
    if coordinates is not None:
        operands = [coordinates, *operands]
        specs = [pl.BlockSpec(memory_space=pltpu.SMEM)] + specs
    return pl.pallas_call(
        tied(body, len(specs), ties),
        out_shape=out_shape,
        in_specs=specs + [ANY] * len(ties),
        scratch_shapes=list(scratch),
        cost_estimate=pl.CostEstimate(flops=flops, bytes_accessed=0, transcendentals=0),
        compiler_params=pltpu.CompilerParams(vmem_limit_bytes=48 * 1024 * 1024),
    )(*operands, *ties)


def left_columns(width):
    return (width // 256) * 128 + 128


def add_rows(start, size, value, own_ref, other_ref):
    half = own_ref.shape[0]
    if start < half:
        own_ref[start : start + size] += value
    else:
        other_ref[start - half : start - half + size] += value


CHUNKS = 4


def send_rows(other_ref, sent_refs):
    count = sent_refs[0].shape[0]
    for number, sent_ref in enumerate(sent_refs):
        sent_ref[...] = rounded(other_ref[number * count : (number + 1) * count])


def sent_chunks(rows, width):
    count = rows // 2 // CHUNKS
    return [full((count, width))] * CHUNKS, [shape(count, width)] * CHUNKS


def ff_forward_body(
    x0_ref, x1_ref, x2_ref, x3_ref, wg_ref, wu_ref, wd_ref, own_ref, g_ref, u_ref, *sent_refs
):
    *sent_refs, other_ref = sent_refs
    size = x0_ref.shape[0]

    @pl.when(pl.program_id(0) == 0)
    def _():
        own_ref[...] = jnp.zeros_like(own_ref)
        other_ref[...] = jnp.zeros_like(other_ref)

    wg, wu, wd = wg_ref[...], wu_ref[...], wd_ref[...]
    for number, x_ref in enumerate((x0_ref, x1_ref, x2_ref, x3_ref)):
        start = number * size
        part = slice(start, start + size)
        x = x_ref[...]
        gate = matmul(x, wg)
        up = matmul(x, wu)
        g_ref[part] = rounded(gate)
        u_ref[part] = rounded(up)
        bent = jnp.tanh(INNER * (gate + CUBIC * (gate * gate * gate)))
        hidden = rounded(0.5 * gate * (1.0 + bent) * up)
        add_rows(start, size, matmul(hidden, wd), own_ref, other_ref)

    @pl.when(pl.program_id(0) == pl.num_programs(0) - 1)
    def _():
        send_rows(other_ref, sent_refs)


def ff_forward(blocks, w_gate, w_up, w_down, ties=()):
    size, width = blocks[0].shape
    rows = 4 * size
    wide = w_gate.shape[1]
    column = pl.BlockSpec((rows, TILE), lambda j: (0, j))
    return kernel_call(
        ff_forward_body,
        (wide // TILE,),
        [full((size, width))] * 4
        + [
            pl.BlockSpec((width, TILE), lambda j: (0, j)),
            pl.BlockSpec((width, TILE), lambda j: (0, j)),
            pl.BlockSpec((TILE, width), lambda j: (j, 0)),
        ],
        [full((rows // 2, width)), column, column] + sent_chunks(rows, width)[0],
        [
            jax.ShapeDtypeStruct((rows // 2, width), F32),
            jax.ShapeDtypeStruct((rows, wide), BF),
            jax.ShapeDtypeStruct((rows, wide), BF),
        ]
        + sent_chunks(rows, width)[1],
        [pltpu.VMEM((rows // 2, width), F32)],
        ties,
        int(COST_FORWARD * rows * width * wide),
    )(*blocks, w_gate, w_up, w_down, *ties)


def ff_backward_body(with_old, *refs):
    block_refs = refs[:4]
    g_ref, u_ref, wg_ref, wu_ref, wd_ref = refs[4:9]
    old_refs = refs[9:11] if with_old else None
    (
        own_ref, dg_ref, du_ref, dl_ref, dr_ref, *sent_refs, hidden_ref, other_ref, gg_ref,
    ) = refs[11 if with_old else 9 :]
    size = block_refs[0].shape[0]
    rows = 4 * size

    @pl.when(pl.program_id(0) == 0)
    def _():
        own_ref[...] = jnp.zeros_like(own_ref)
        other_ref[...] = jnp.zeros_like(other_ref)
        for number, block_ref in enumerate(block_refs):
            gg_ref[number * size : (number + 1) * size] = block_ref[...]

    wg, wu, wd = wg_ref[...], wu_ref[...], wd_ref[...]
    for start in range(0, rows, size):
        part = slice(start, start + size)
        grad = matmul_nt(gg_ref[part], wd)
        gate = g_ref[part].astype(F32)
        up = u_ref[part].astype(F32)
        square = gate * gate
        bent = jnp.tanh(INNER * (gate + CUBIC * (square * gate)))
        half = 0.5 * (1.0 + bent)
        gelu = gate * half
        slope = half + (0.5 * INNER) * gate * (1.0 - bent * bent) * (1.0 + (3.0 * CUBIC) * square)
        hidden_ref[part] = rounded(gelu * up)
        grad_gate = rounded(grad * up * slope)
        grad_up = rounded(grad * gelu)
        dg_ref[part] = grad_gate
        du_ref[part] = grad_up
        add_rows(
            start, size, matmul_nt(grad_gate, wg) + matmul_nt(grad_up, wu), own_ref, other_ref
        )
    total = matmul_tn(hidden_ref[...], gg_ref[...])
    left = dl_ref.shape[1]
    for number, (out_ref, part) in enumerate(((dl_ref, total[:, :left]), (dr_ref, total[:, left:]))):
        if old_refs is not None:
            part = part + old_refs[number][...].astype(F32)
        out_ref[...] = rounded(part)

    @pl.when(pl.program_id(0) == pl.num_programs(0) - 1)
    def _():
        send_rows(other_ref, sent_refs)


def ff_backward(blocks, gate, up, w_gate, w_up, w_down, old, ties=()):
    size, width = blocks[0].shape
    rows = 4 * size
    wide = w_gate.shape[1]
    left = left_columns(width)
    column = pl.BlockSpec((rows, TILE), lambda j: (0, j))
    halves = [pl.BlockSpec((TILE, cols), lambda j: (j, 0)) for cols in (left, width - left)]
    in_specs = [full((size, width))] * 4 + [
        column,
        column,
        pl.BlockSpec((width, TILE), lambda j: (0, j)),
        pl.BlockSpec((width, TILE), lambda j: (0, j)),
        pl.BlockSpec((TILE, width), lambda j: (j, 0)),
    ]
    operands = [*blocks, gate, up, w_gate, w_up, w_down]
    if old is not None:
        in_specs += halves
        operands += list(old)
    return kernel_call(
        functools.partial(ff_backward_body, old is not None),
        (wide // TILE,),
        in_specs,
        [full((rows // 2, width)), column, column] + halves + sent_chunks(rows, width)[0],
        [
            jax.ShapeDtypeStruct((rows // 2, width), F32),
            jax.ShapeDtypeStruct((rows, wide), BF),
            jax.ShapeDtypeStruct((rows, wide), BF),
            jax.ShapeDtypeStruct((wide, left), BF),
            jax.ShapeDtypeStruct((wide, width - left), BF),
        ]
        + sent_chunks(rows, width)[1],
        [
            pltpu.VMEM((rows, TILE), BF),
            pltpu.VMEM((rows // 2, width), F32),
            pltpu.VMEM((rows, width), BF),
        ],
        ties,
        int(COST_BACKWARD * rows * width * wide),
    )(*operands, *ties)


def ff_weights_body(split, with_old, *refs):
    if split:
        (extent, stages), coords_ref, refs = split, refs[0], refs[1:]
    x_refs = refs[:4]
    dg_ref, du_ref = refs[4:6]
    old_refs = refs[6:8] if with_old else (None, None)
    refs = refs[8 if with_old else 6 :]
    outs, turned_ref = refs[: 4 if split else 2], refs[4 if split else 2]
    size = x_refs[0].shape[0]

    @pl.when(pl.program_id(0) == 0)
    def _():
        for number, x_ref in enumerate(x_refs):
            turned_ref[:, number * size : (number + 1) * size] = x_ref[...].T

    for kind, grad_ref in enumerate((dg_ref, du_ref)):
        total = matmul(turned_ref[...], grad_ref[...])
        if with_old:
            total = total + old_refs[kind][...].astype(F32)
        total = rounded(total)
        if not split:
            outs[kind][...] = total
            continue
        held_ref = refs[5]
        rows = held_ref.shape[-2]
        for number, index in enumerate(itertools.product(*[range(count) for count in extent])):
            held_ref[index] = total[number * rows : (number + 1) * rows]
        name, position = stages[kind]
        rest = [range(count) for number, count in enumerate(extent) if number != position]
        for side in range(2):
            for index in itertools.product(*rest):
                source = index[:position] + (coords_ref[name] ^ side,) + index[position:]
                outs[2 * kind + side][index] = held_ref[source]


def ff_weights(grid, coordinates, blocks, grad_gate, grad_up, old, stages=None, ties=()):
    size, width = blocks[0].shape
    rows = 4 * size
    wide = grad_gate.shape[1]
    column = pl.BlockSpec((rows, TILE), lambda j: (0, j))
    block = pl.BlockSpec((width, TILE), lambda j: (0, j))
    in_specs = [full((size, width))] * 4 + [column, column]
    operands = [*blocks, grad_gate, grad_up]
    scratch = [pltpu.VMEM((width, rows), BF)]
    if old is not None:
        in_specs += [block, block]
        operands += list(old)
    if stages is None:
        split = None
        outs = [jax.ShapeDtypeStruct((width, wide), BF)] * 2
        out_specs = [block, block]
    else:
        names = ("y", "x", "p")
        extent = grid.extent(names)
        split = (extent, [(NAMES.index(stage), names.index(stage)) for stage in stages])
        piece = width // grid.groups
        in_specs = [pl.BlockSpec(memory_space=pltpu.SMEM)] + in_specs
        operands = [coordinates] + operands
        scratch.append(pltpu.VMEM(extent + (piece, TILE), BF))
        outs = []
        out_specs = []
        for stage in stages:
            left = grid.extent([name for name in names if name != stage])
            for side in range(2):
                outs.append(jax.ShapeDtypeStruct(left + (piece, wide), BF))
                out_specs.append(
                    pl.BlockSpec(left + (piece, TILE), lambda j: (0,) * (len(left) + 1) + (j,))
                )
    return kernel_call(
        functools.partial(ff_weights_body, split, old is not None),
        (wide // TILE,),
        in_specs,
        out_specs,
        outs,
        scratch,
        ties,
        int(COST_WEIGHTS * rows * width * wide),
    )(*operands, *ties)


def stack_body(plan, *refs):
    out_at = sum(count for count, pick, columns in plan)
    at = 0
    for count, pick, columns in plan:
        group = refs[at : at + count]
        at += count
        for column in columns:
            out_ref = refs[out_at]
            out_at += 1
            for index, ref in enumerate(group):
                place = () if pick is None else (pick,)
                value = ref[place + (Ellipsis, column)]
                if count == 1:
                    out_ref[...] = value
                else:
                    out_ref[index] = value


def stack(items, ties=()):
    plan = []
    outs = []
    operands = []
    for parts, pick, widths in items:
        extent = parts[0].shape if pick is None else parts[0].shape[1:]
        widths = widths or [extent[-1]]
        if len(parts) > 1:
            extent = (len(parts),) + extent
        columns = []
        start = 0
        for columns_wide in widths:
            columns.append(slice(start, start + columns_wide))
            start += columns_wide
            outs.append(jax.ShapeDtypeStruct(extent[:-1] + (columns_wide,), parts[0].dtype))
        plan.append((len(parts), pick, columns))
        operands += parts
    return whole_call(functools.partial(stack_body, plan), outs, None, operands, ties)


def fold_body(plan, coords_ref, *refs):
    at = 0
    out_at = sum(count for item in plan for count in item["counts"])
    for item in plan:
        names, stage, size = item["names"], item["stage"], item["size"]
        outs = refs[out_at : out_at + size]
        out_at += size
        position = names.index(stage)
        own = coords_ref[NAMES.index(stage)]
        rest = [range(extent) for number, extent in enumerate(item["extent"]) if number != position]
        column = 0
        for count in item["counts"]:
            group = refs[at : at + count]
            at += count
            rows, cols = group[0].shape[-2:]
            for mask in range(size):
                for index in itertools.product(*rest):
                    source = index[:position] + (own ^ mask,) + index[position:]
                    if count == 1:
                        value = group[0][source]
                    else:
                        value = group[0][source].astype(F32)
                        for other in group[1:]:
                            value = value + other[source].astype(F32)
                        value = rounded(value)
                    out = outs[mask]
                    out[index + (slice(0, rows), slice(column, column + cols))] = value
                    if rows < out.shape[-2]:
                        out[index + (slice(rows, None), slice(column, column + cols))] = jnp.zeros(
                            (out.shape[-2] - rows, cols), out.dtype
                        )
            column += cols


def fold(grid, coordinates, items, ties=()):
    plan = []
    outs = []
    operands = []
    for names, stage, groups in items:
        rows = max(group[0].shape[-2] for group in groups)
        cols = sum(group[0].shape[-1] for group in groups)
        left = tuple(name for name in names if name != stage)
        size = grid.sizes[stage]
        plan.append(
            {
                "names": names,
                "stage": stage,
                "size": size,
                "extent": grid.extent(names),
                "counts": [len(group) for group in groups],
            }
        )
        outs += [jax.ShapeDtypeStruct(grid.extent(left) + (rows, cols), BF)] * size
        for group in groups:
            operands += [
                value.reshape(grid.extent(names) + value.shape[-2:]) for value in group
            ]
    results = whole_call(
        functools.partial(fold_body, plan), outs, coordinates, operands, ties
    )
    folded = []
    at = 0
    for names, stage, groups in items:
        size = grid.sizes[stage]
        kept = [results[at]] + [
            grid.permute(results[at + mask], {stage: mask}) for mask in range(1, size)
        ]
        folded.append((tuple(name for name in names if name != stage), kept))
        at += size
    return folded


def pair_body(own_ref, *refs):
    came_refs, (own_out, sent_out) = refs[:-2], refs[-2:]
    count = own_out.shape[0]
    step = came_refs[0].shape[0]
    for number, came_ref in enumerate(came_refs):
        start = number * step
        total = own_ref[start : start + step] + came_ref[...].astype(F32)
        if start < count:
            own_out[start : start + step] = total
        else:
            sent_out[start - count : start - count + step] = rounded(total)


def tokens_out(grid, own, sent, ties=()):
    came = [grid.permute(part, {"c": 1}) for part in sent]
    count, width = own.shape[0] // 2, own.shape[1]
    own, sent = whole_call(
        pair_body, [shape(count, width, F32), shape(count, width)], None, [own, *came], ties
    )
    return own, grid.permute(sent, {"h": 1})


def fetch(coords_ref, refs, order, block, place):
    index = 0
    for number, stride in order[:-1]:
        index = index + (coords_ref[number] ^ block[number]) * stride
    last = order[-1][0]
    side = coords_ref[last] ^ block[last]
    value = refs[-1][(index,) + place]
    for number in range(len(refs) - 1):
        value = jnp.where(side == number, refs[number][(index,) + place], value)
    return value


def quarter_of(coords_ref):
    return coords_ref[3] * 2 + coords_ref[4]


def cut_body(groups, block, block_up, coords_ref, w_ref, *refs):
    out_refs, held_ref = refs[:-1], refs[-1]
    own = quarter_of(coords_ref)
    held_ref[...] = jnp.zeros_like(held_ref)
    for quarter in range(4):
        slot = own ^ quarter
        for kind in range(2):
            for group in range(groups):
                at = kind * groups * 4 * block + (group * 4 + quarter) * block
                held_ref[slot, kind, :, group * block_up : group * block_up + block] = w_ref[
                    :, at : at + block
                ]
    for mask, out_ref in enumerate(out_refs):
        out_ref[...] = held_ref[mask]


def pick_of(own, refs, quarter):
    value = refs[3]
    for mask in range(3):
        value = jnp.where(own == quarter ^ mask, refs[mask], value)
    return value


def pieces_body(coords_ref, p0_ref, p1_ref, p2_ref, p3_ref, out_ref):
    own = quarter_of(coords_ref)
    rows = p0_ref.shape[1]
    for kind in range(2):
        refs = [ref[kind] for ref in (p0_ref, p1_ref, p2_ref, p3_ref)]
        for quarter in range(4):
            out_ref[kind, quarter * rows : (quarter + 1) * rows] = pick_of(own, refs, quarter)


def split_body(count, coords_ref, *refs):
    own = quarter_of(coords_ref)
    outs = refs[2 * count :]
    rows = outs[0].shape[1]
    for kind in range(2):
        total = refs[kind * count][...].astype(F32)
        for ref in refs[kind * count + 1 : (kind + 1) * count]:
            total = total + ref[...].astype(F32)
        total = rounded(total)
        for mask, out_ref in enumerate(outs):
            value = total[3 * rows :]
            for quarter in range(3):
                value = jnp.where(
                    own == quarter ^ mask, total[quarter * rows : (quarter + 1) * rows], value
                )
            out_ref[kind] = value


def join_body(groups, block, block_up, coords_ref, p0_ref, p1_ref, p2_ref, p3_ref, out_ref):
    own = quarter_of(coords_ref)
    for kind in range(2):
        refs = [ref[kind] for ref in (p0_ref, p1_ref, p2_ref, p3_ref)]
        for quarter in range(4):
            piece = pick_of(own, refs, quarter).astype(F32)
            for group in range(groups):
                at = kind * groups * 4 * block + (group * 4 + quarter) * block
                out_ref[:, at : at + block] = piece[
                    :, group * block_up : group * block_up + block
                ]


def order_body(blocks, orders, coords_ref, *refs):
    out_ref = refs[-1]
    count = (len(refs) - 1) // len(orders)
    at = 0
    for group, order in enumerate(orders):
        group_refs = refs[group * count : (group + 1) * count]
        rows, cols = group_refs[0].shape[1:]
        for number, block in enumerate(blocks):
            out_ref[number * rows : (number + 1) * rows, at : at + cols] = fetch(
                coords_ref, group_refs, order, block, (slice(None), slice(None))
            )
        at += cols


def in_order(grid, coordinates, *columns, ties=()):
    blocks = grid.blocks_of("pxy")
    orders = []
    flat = []
    count = max(len(parts) for parts, names in columns)
    for parts, names in columns:
        parts = [part.reshape((-1,) + part.shape[-2:]) for part in parts]
        order = grid.order(names)
        if len(parts) < count:
            parts = [jnp.concatenate(parts)]
            parts += parts * (count - 1)
            order = order + ((order[-1][0], -1),)
        flat += parts
        orders.append(order)
    rows = flat[0].shape[1]
    cols = sum(parts[0].shape[-1] for parts, names in columns)
    return whole_call(
        functools.partial(order_body, blocks, tuple(orders)),
        jax.ShapeDtypeStruct((grid.groups * rows, cols), flat[0].dtype),
        coordinates,
        flat,
        ties,
    )


def spread_body(sizes, coords_ref, normed_ref, low_ref, mixed_ref, side_ref, *refs):
    own_ref, sent_ref, held_ref = refs
    devices, qkv, joined, lift, lift_at, out, mixed, last, last_at = sizes
    held_ref[...] = jnp.zeros_like(held_ref)
    second = devices // 2 * joined
    for number in range(devices):
        core, place = number % 2, number // 2
        at = place * joined
        held_ref[core, :, at : at + qkv] = normed_ref[:, number * qkv : (number + 1) * qkv]
        at = at + lift_at
        held_ref[core, :, at : at + lift] = low_ref[:, number * lift : (number + 1) * lift]
        at = second + place * mixed
        held_ref[core, :, at : at + out] = mixed_ref[:, number * out : (number + 1) * out]
        at = at + last_at
        held_ref[core, :, at : at + last] = side_ref[:, number * last : (number + 1) * last]
    own_ref[...] = held_ref[coords_ref[4]]
    sent_ref[...] = held_ref[1 - coords_ref[4]]


def unpack_first_body(blocks, order, sizes, count, coords_ref, *refs):
    chunks = [refs[at : at + count] for at in range(0, len(refs) - 4, count)]
    w_ref, lift_ref, down_ref, gain_ref = refs[-4:]
    rows, rows_up, lift_rows, gain_cols = sizes
    gain_ref[...] = jnp.zeros_like(gain_ref)
    main = slice(0, rows)
    lift = slice(rows_up, rows_up + lift_rows)
    every = slice(None)
    for number, block in enumerate(blocks):
        place = slice(number * rows, (number + 1) * rows)
        lift_place = slice(number * lift_rows, (number + 1) * lift_rows)
        at = 0
        for chunk in chunks[:-1]:
            columns = slice(at, at + chunk[0].shape[-1])
            w_ref[place, columns] = fetch(coords_ref, chunk, order, block, (main, every))
            lift_ref[lift_place, columns] = fetch(coords_ref, chunk, order, block, (lift, every))
            at = columns.stop
        down_ref[place, :] = fetch(coords_ref, chunks[-1], order, block, (main, every))
        gain_ref[0:2, number * gain_cols : (number + 1) * gain_cols] = fetch(
            coords_ref,
            chunks[-1],
            order,
            block,
            (slice(rows_up, rows_up + 2), slice(0, gain_cols)),
        ).astype(F32)


def unpack_second_body(blocks, order, sizes, count, coords_ref, *refs):
    chunks = [refs[at : at + count] for at in range(0, len(refs) - 5, count)]
    out_ref, lift0_ref, lift1_ref, down_ref, late_ref = refs[-5:]
    rows, rows_up, lift_rows, lift_up, late_rows, late_up = sizes
    every = slice(None)
    main = slice(0, rows)
    fold_cols = chunks[-1][0].shape[-1]
    for number, block in enumerate(blocks):

        def get(chunk, start, size):
            return fetch(coords_ref, chunk, order, block, (slice(start, start + size), every))

        place = slice(number * rows, (number + 1) * rows)
        lift_place = slice(number * lift_rows, (number + 1) * lift_rows)
        at = 0
        for chunk in chunks[:-2]:
            columns = slice(at, at + chunk[0].shape[-1])
            out_ref[place, columns] = get(chunk, 0, rows)
            lift0_ref[lift_place, columns] = get(chunk, rows_up, lift_rows)
            lift1_ref[lift_place, columns] = get(chunk, rows_up + lift_up, lift_rows)
            at = columns.stop
        down_ref[place, :] = get(chunks[-2], 0, rows)
        late_place = slice(number * late_rows, (number + 1) * late_rows)
        for part in range(late_ref.shape[1] // fold_cols):
            late_ref[late_place, part * fold_cols : (part + 1) * fold_cols] = get(
                chunks[-1], part * late_up, late_rows
            )


def rotate(values, cosine_table, sine_table):
    halfway = values.shape[-1] // 2
    first_half = values[..., :halfway]
    second_half = values[..., halfway:]
    return jnp.concatenate(
        [
            first_half * cosine_table - second_half * sine_table,
            second_half * cosine_table + first_half * sine_table,
        ],
        axis=-1,
    )


def inverse_size(values):
    return lax.rsqrt(jnp.mean(values * values, axis=-1, keepdims=True) + EPS)


def norm_back(values, gain_row, grad):
    inverse = inverse_size(values)
    weighted = grad * gain_row
    inner = jnp.mean(weighted * values, axis=-1, keepdims=True)
    gain_grad = jnp.sum(grad * values * inverse, axis=0, keepdims=True)
    return inverse * weighted - values * (inverse * inverse * inverse) * inner, gain_grad


def shape(rows, cols, kind=BF):
    return jax.ShapeDtypeStruct((rows, cols), kind)


def pack_body(
    sizes, wq_ref, qd_ref, ql_ref, gain_ref, wo_ref, od_ref, ol_ref, first_ref, second_ref
):
    qkv_up, ql_up, out_up, ol_up = sizes
    for ref in (first_ref, second_ref):
        ref[...] = jnp.zeros_like(ref)
    rows, cols = wq_ref.shape
    lift_rows = ql_ref.shape[1]
    rank = qd_ref.shape[2]
    first_ref[:rows, :cols] = wq_ref[...]
    first_ref[qkv_up : qkv_up + lift_rows, :cols] = ql_ref[0]
    for loop in range(2):
        at = cols + loop * rank
        first_ref[:rows, at : at + rank] = qd_ref[loop]
    first_ref[qkv_up : qkv_up + 2, cols : cols + gain_ref.shape[1]] = gain_ref[...]
    rows, width = wo_ref.shape
    last_rows = ol_ref.shape[1]
    second_ref[:rows, :width] = wo_ref[...]
    for loop in range(2):
        at = out_up + loop * ol_up
        second_ref[at : at + last_rows, :width] = ol_ref[loop]
        at = width + loop * rank
        second_ref[:rows, at : at + rank] = od_ref[loop]
    for part in range(cols // rank):
        second_ref[part * ql_up : part * ql_up + lift_rows, width + 2 * rank :] = ql_ref[
            1, :, part * rank : (part + 1) * rank
        ]


def rows_body(w_ref, out_ref):
    out_ref[...] = jnp.zeros_like(out_ref)
    out_ref[: w_ref.shape[0]] = w_ref[...]


def project_kv_body(first_loop, addends, *refs):
    add_refs = refs[:addends]
    gain_ref, qd_ref, w_ref, ql_ref, cos_ref, sin_ref = refs[addends : addends + 6]
    kv_ref, normed_ref, low_ref, residual_ref = refs[addends + 6 :]
    rank = low_ref.shape[1]
    width_q = w_ref.shape[1] - 2 * HD
    values = add_refs[0][...].astype(F32)
    for ref in add_refs[1:]:
        values = values + ref[...].astype(F32)
    residual_ref[...] = values
    normed = rounded(values * inverse_size(values) * gain_ref[0:1])
    normed_ref[...] = normed
    down = qd_ref[:, :rank] if first_loop else qd_ref[:, rank:]
    low = rounded(matmul(normed, down))
    low_ref[...] = low
    kv = matmul(normed, w_ref[:, width_q:]) + matmul(low, ql_ref[:, width_q:])
    kv_ref[:, :HD] = rounded(rotate(kv[:, :HD], cos_ref[...], sin_ref[...]))
    kv_ref[:, HD:] = rounded(kv[:, HD:])


def project_q_body(normed_ref, low_ref, w_ref, ql_ref, cos_ref, sin_ref, q_ref):
    for head in range(H):
        at = slice(head * HD, (head + 1) * HD)
        part = matmul(normed_ref[...], w_ref[:, at]) + matmul(low_ref[...], ql_ref[:, at])
        q_ref[:, at] = rounded(rotate(part, cos_ref[...], sin_ref[...]) * HD ** (-0.5))


def mask_of(segs_ref, places_ref, row_ref):
    seq_len = row_ref.shape[1]
    key_places = lax.broadcasted_iota(jnp.int32, (segs_ref.shape[0], seq_len), 1)
    allowed = (segs_ref[...] == row_ref[...]) & (key_places <= places_ref[...])
    return jnp.where(allowed, 0.0, NEG)


def attend_body(entries, coords_ref, q_ref, segs_ref, places_ref, row_ref, *refs):
    mixed_ref, log_ref, kv_ref = refs[-3:]
    for (p_mask, h_mask, c_mask), number, index in entries:
        value = refs[number][...] if index is None else refs[number][index]
        size = value.shape[0]
        block = (coords_ref[2] ^ p_mask) * 4 + (coords_ref[3] ^ h_mask) * 2
        block = block + (coords_ref[4] ^ c_mask)
        kv_ref[pl.ds(pl.multiple_of(block * size, size), size), :] = value
    mask = mask_of(segs_ref, places_ref, row_ref)
    for head in range(H):
        at = slice(head * HD, (head + 1) * HD)
        scores = matmul_nt(q_ref[:, at], kv_ref[:, :HD]) + mask
        top = jnp.max(scores, axis=1, keepdims=True)
        probabilities = jnp.exp(scores - top)
        total = jnp.sum(probabilities, axis=1, keepdims=True)
        mixed_ref[:, at] = rounded(matmul(rounded(probabilities), kv_ref[:, HD:]) / total)
        log_ref[head] = top + jnp.log(total)


def attend_back_body(
    q_ref, kv_ref, segs_ref, places_ref, row_ref, log_ref, grad_ref, cos_ref, sin_ref,
    coords_ref, own_ref, sent_ref, gq_ref, keys_ref, values_ref,
):
    mask = mask_of(segs_ref, places_ref, row_ref)
    size = own_ref.shape[1]
    for head in range(H):
        at = slice(head * HD, (head + 1) * HD)
        queries = q_ref[:, at]
        grad = grad_ref[:, at]
        probabilities = jnp.exp(matmul_nt(queries, kv_ref[:, :HD]) + mask - log_ref[head])
        grad_probs = matmul_nt(grad, kv_ref[:, HD:])
        weighted = probabilities * grad_probs
        delta = jnp.sum(weighted, axis=1, keepdims=True)
        grad_scores = rounded(weighted - probabilities * delta)
        grad_q = matmul(grad_scores, kv_ref[:, :HD])
        gq_ref[:, at] = rounded(rotate(grad_q, cos_ref[...], -sin_ref[...]) * HD ** (-0.5))
        key_term = matmul_tn(grad_scores, queries)
        value_term = matmul_tn(rounded(probabilities), grad)
        if head == 0:
            keys_ref[...] = key_term
            values_ref[...] = value_term
        else:
            keys_ref[...] += key_term
            values_ref[...] += value_term
    core = coords_ref[4]
    for number in range(own_ref.shape[0]):
        for out_ref, which in ((own_ref, core), (sent_ref, 1 - core)):
            place = pl.ds(pl.multiple_of((2 * number + which) * size, size), size)
            out_ref[number, :, :HD] = rounded(keys_ref[place, :])
            out_ref[number, :, HD:] = rounded(values_ref[place, :])


def leave_body(
    first_loop, mixed_ref, od_ref, w_ref, ol_ref, residual_ref, gain_ref,
    side_ref, middle_ref, normed_ref,
):
    rank = side_ref.shape[1]
    down = od_ref[:, :rank] if first_loop else od_ref[:, rank:]
    side = rounded(matmul(mixed_ref[...], down))
    side_ref[...] = side
    middle = residual_ref[...] + (matmul(mixed_ref[...], w_ref[...]) + matmul(side, ol_ref[...]))
    middle_ref[...] = middle
    normed_ref[...] = rounded(middle * inverse_size(middle) * gain_ref[1:2])


def enter_back_body(
    first_loop, own_ref, other_ref, result_ref, middle_ref, gain_ref, w_ref, ol_ref, od_ref,
    grad_ref, branch_ref, mixed_ref, gain_grad_ref,
):
    width = grad_ref.shape[1]
    rank = branch_ref.shape[1] - width
    grad_normed = own_ref[...] + other_ref[...].astype(F32)
    back, gain_grad = norm_back(middle_ref[...], gain_ref[1:2], grad_normed)
    gain_grad_ref[...] = jnp.broadcast_to(gain_grad, gain_grad_ref.shape)
    grad = result_ref[...].astype(F32) + back
    grad_ref[...] = grad
    branch = rounded(grad)
    branch_ref[:, :width] = branch
    side = rounded(matmul_nt(branch, ol_ref[...]))
    branch_ref[:, width:] = side
    down = od_ref[:, :rank] if first_loop else od_ref[:, rank:]
    mixed_ref[...] = rounded(matmul_nt(branch, w_ref[...]) + matmul_nt(side, down))


def rope_back_body(count, *refs):
    gq_ref, ql_ref, cos_ref, sin_ref, out_ref = refs[count:]
    width_q = gq_ref.shape[1]
    kv = refs[0][...].astype(F32)
    for ref in refs[1:count]:
        kv = kv + ref[...].astype(F32)
    keys = rounded(rotate(kv[:, :HD], cos_ref[...], -sin_ref[...]))
    values = rounded(kv[:, HD:])
    out_ref[:, :HD] = keys
    out_ref[:, HD : 2 * HD] = values
    out_ref[:, 2 * HD :] = rounded(
        matmul_nt(gq_ref[...], ql_ref[:, :width_q])
        + matmul_nt(keys, ql_ref[:, width_q : width_q + HD])
        + matmul_nt(values, ql_ref[:, width_q + HD :])
    )


def leave_back_body(
    first_loop, in_ref, gq_ref, w_ref, qd_ref, residual_ref, gain_ref, grad_ref,
    other_gain_ref, *refs,
):
    out_ref, out_b_ref, gain_grad_ref = refs[-3:]
    rank = in_ref.shape[1] - 2 * HD
    width_q = gq_ref.shape[1]
    down = qd_ref[:, :rank] if first_loop else qd_ref[:, rank:]
    grad_normed = (
        matmul_nt(gq_ref[...], w_ref[:, :width_q])
        + matmul_nt(in_ref[:, : 2 * HD], w_ref[:, width_q:])
        + matmul_nt(in_ref[:, 2 * HD :], down)
    )
    back, gain_grad = norm_back(residual_ref[...], gain_ref[0:1], grad_normed)
    gain_grad_ref[0:1] = gain_grad
    gain_grad_ref[1:2] = other_gain_ref[1:2]
    if len(refs) > 3:
        gain_grad_ref[0:2] += refs[0][0:2]
    grad = grad_ref[...] + back
    out_ref[...] = grad
    out_b_ref[...] = rounded(grad)


def late_body(sizes, coords_ref, kv_ref, qd_ref, *refs):
    count, rows, gain_cols = sizes
    gain_refs, out_ref = refs[:-1], refs[-1]
    kv_cols = kv_ref.shape[2]
    out_ref[:, :, :kv_cols] = kv_ref[...]
    out_ref[:, :, kv_cols:] = qd_ref[...]
    for row in range(2):
        gains = rounded(gain_refs[0][row : row + 1] + gain_refs[1][row : row + 1])
        for number in range(count):
            at = 2 * number * gain_cols
            value = jnp.where(
                coords_ref[4] == 0,
                gains[:, at : at + gain_cols],
                gains[:, at + gain_cols : at + 2 * gain_cols],
            )
            out_ref[number, rows + row : rows + row + 1, kv_cols : kv_cols + gain_cols] = value


def down_body(count, *refs):
    out_ref = refs[-1]
    at = 0
    for group in range(2):
        value = refs[group * count][...].astype(F32)
        for ref in refs[group * count + 1 : (group + 1) * count]:
            value = value + ref[...].astype(F32)
        out_ref[:, at : at + value.shape[1]] = value[: out_ref.shape[0]]
        at += value.shape[1]


def result_body(middle_ref, own_ref, other_ref, out_ref):
    out_ref[...] = rounded(middle_ref[...] + (own_ref[...] + other_ref[...].astype(F32)))


def finish_body(count, sizes, *refs):
    rows, rows_up, lift_rows, lift_up, out_rows, out_up, last_rows, last_up, gain_cols = sizes
    totals = []
    for group in range(3):
        value = refs[group * count][...].astype(F32)
        for ref in refs[group * count + 1 : (group + 1) * count]:
            value = value + ref[...].astype(F32)
        totals.append(value)
    outs, queries, late = totals
    gains_ref, qkv_ref, out_ref, qd_ref, ql_ref, od_ref, ol_ref = refs[3 * count :]
    width = out_ref.shape[1]
    rank = qd_ref.shape[2]
    half = queries.shape[1] - rank
    rest = qkv_ref.shape[1] - half
    gains_ref[...] = late[rows : rows + 2, rest : rest + gain_cols]
    qkv_ref[:, :half] = queries[:rows, :half]
    qkv_ref[:, half:] = late[:rows, :rest]
    out_ref[...] = outs[:out_rows, :width]
    qd_ref[0] = late[:rows, rest:]
    qd_ref[1] = queries[:rows, half:]
    for loop in range(2):
        at = rows_up + loop * lift_up
        ql_ref[loop, :, :half] = queries[at : at + lift_rows, :half]
        ql_ref[loop, :, half:] = late[at : at + lift_rows, :rest]
        at = width + loop * rank
        od_ref[loop] = outs[:out_rows, at : at + rank]
        at = out_up + loop * last_up
        ol_ref[loop] = outs[at : at + last_rows, :width]


def outer_body(columns, pieces, olds, own_ref, came_ref, right_ref, right_came_ref, *refs):
    out_refs = refs[olds:]
    own, came = own_ref[:, columns], came_ref[:, columns]
    for number, piece in enumerate(pieces):
        cols = piece.stop - piece.start
        step = 512 if cols % 512 == 0 else 384 if cols % 384 == 0 else cols
        for start in range(0, cols, step):
            part = slice(start, start + step)
            from_right = slice(piece.start + start, piece.start + start + step)
            total = matmul_tn(own, right_ref[:, from_right]) + matmul_tn(
                came, right_came_ref[:, from_right]
            )
            if number < olds:
                total = total + refs[number][:, part].astype(F32)
            out_refs[number][:, part] = rounded(total)


def outer(left, columns, right, widths, olds=(), ties=()):
    rows = columns.stop - columns.start
    pieces = []
    at = 0
    for cols in widths:
        pieces.append(slice(at, at + cols))
        at += cols
    return whole_call(
        functools.partial(outer_body, columns, pieces, len(olds)),
        [shape(rows, cols) for cols in widths],
        None,
        [*left, *right, *olds],
        ties,
    )


def per_device(
    grid,
    inputs,
    segments,
    cotangent,
    norm_gain_rows,
    query_key_value_weight,
    output_weight,
    gate_up_weight,
    down_weight,
    adapter_query_down,
    adapter_query_lift,
    adapter_output_down,
    adapter_output_lift,
):
    tokens = inputs.shape[0]
    width = inputs.shape[1]
    groups = grid.groups
    gain_cols = norm_gain_rows.shape[1]
    qkv_rows = query_key_value_weight.shape[0]
    out_rows = output_weight.shape[0]
    ql_rows = adapter_query_lift.shape[1]
    ol_rows = adapter_output_lift.shape[1]
    rank = adapter_query_down.shape[2]
    hidden_block = down_weight.shape[0]
    width_q = H * HD

    qkv_up, ql_up = up8(qkv_rows), up8(ql_rows)
    out_up, ol_up = up8(out_rows), up8(ol_rows)
    wide = -(-groups * hidden_block // TILE) * TILE
    block_up = wide // groups
    qkv_cols = query_key_value_weight.shape[1]
    left_cols = left_columns(width)
    coordinates = grid.coordinates()
    straight = ("p", "h", "x", "y", "c")
    turned = ("p", "h", "y", "x", "c")

    def flat(parts):
        return [part.reshape((-1,) + part.shape[-2:]) for part in parts]

    def parts(values, name):
        return grid.parts(values, name)

    segrow = segments[0]
    seq_len = segrow.shape[0]
    position = lax.axis_index("blk")
    places = position * tokens + jnp.arange(tokens, dtype=jnp.int32)
    own_segs = lax.dynamic_slice_in_dim(segrow, position * tokens, tokens, 0)
    below_one = jnp.sum((segrow < 1).astype(jnp.int32))
    below_two = jnp.sum((segrow < 2).astype(jnp.int32))
    starts = jnp.where(own_segs == 0, 0, jnp.where(own_segs == 1, below_one, below_two))
    offsets = (places - starts).astype(F32)
    frequency = jnp.exp(jnp.arange(HD // 2, dtype=F32) * (-2.0 * math.log(ROPE_BASE) / HD))
    angles = offsets[:, None] * frequency[None, :]
    tables = [jnp.cos(angles), jnp.sin(angles)]
    masks = [own_segs[:, None], places[:, None], segments]

    second_rows = max(out_up + 2 * ol_up, qkv_cols // rank * ql_up)
    first, second = whole_call(
        functools.partial(pack_body, (qkv_up, ql_up, out_up, ol_up)),
        [shape(qkv_up + ql_up, qkv_cols + 2 * rank), shape(second_rows, width + 3 * rank)],
        None,
        [
            query_key_value_weight, adapter_query_down, adapter_query_lift, norm_gain_rows,
            output_weight, adapter_output_down, adapter_output_lift,
        ],
    )
    first, second = stack([(parts(first, "p"), None, None), (parts(second, "p"), None, None)])
    cut = whole_call(
        functools.partial(cut_body, groups, hidden_block, block_up),
        [jax.ShapeDtypeStruct((2, qkv_rows, wide), BF)] * 4,
        coordinates,
        [gate_up_weight],
        [first],
        [pltpu.VMEM((4, 2, qkv_rows, wide), BF)],
    )
    down = whole_call(
        rows_body, shape(block_up, width), None, [down_weight], [cut[0]]
    )
    first, second = stack(
        [(parts(first, "h"), None, None), (parts(second, "h"), None, None)], [down]
    )
    gate_up = whole_call(
        pieces_body,
        jax.ShapeDtypeStruct((2, 4 * qkv_rows, wide), BF),
        coordinates,
        [
            cut[0],
            grid.permute(cut[1], {"c": 1}),
            grid.permute(cut[2], {"h": 1}),
            grid.permute(cut[3], {"h": 1, "c": 1}),
        ],
        [first],
    )
    first, second = stack(
        [(parts(first, "x"), None, None), (parts(second, "y"), None, None)], [gate_up]
    )
    gate_up = parts(gate_up, "p")
    first_chunks = [qkv_cols // 3] * 3 + [2 * rank]
    second_chunks = [width - left_cols, left_cols, 2 * rank, rank]
    chunks = stack(
        [
            (parts(first, "y"), None, first_chunks),
            (parts(second, "x"), None, second_chunks),
        ]
    )
    chunks = [flat(parts(chunk, "c")) for chunk in chunks]
    first = [part for chunk in chunks[:4] for part in chunk]
    second = [part for chunk in chunks[4:] for part in chunk]
    gate, up, down = stack(
        [
            (gate_up, 0, None),
            (gate_up, 1, None),
            ([down], None, None),
        ],
        [chunks[0][0]],
    )
    gate, up = parts(gate, "x"), parts(up, "y")
    down = parts(down, "p")
    w_qkv, ql_0, qd, gains = whole_call(
        functools.partial(
            unpack_first_body,
            grid.blocks_of(straight),
            grid.order(straight),
            (qkv_rows, qkv_up, ql_rows, gain_cols),
            2,
        ),
        [shape(width, qkv_cols), shape(rank, qkv_cols), shape(width, 2 * rank), shape(8, width, F32)],
        coordinates,
        first,
        [gate[0]],
    )
    lifts_in = [ql_0, None]

    def project_kv(addends, loop):
        own_kv, normed_b, low_rank_b, residual = whole_call(
            functools.partial(project_kv_body, loop == 0, len(addends)),
            [
                shape(tokens, 2 * HD), shape(tokens, width), shape(tokens, rank),
                shape(tokens, width, F32),
            ],
            None,
            [*addends, gains, qd, w_qkv, lifts_in[loop], *tables],
        )
        return own_kv, normed_b, low_rank_b, residual

    def gather_kv(own_kv):
        chips = {(0, 0): own_kv}
        for p_mask in range(grid.sizes["p"]):
            for h_mask in range(2):
                if p_mask or h_mask:
                    chips[p_mask, h_mask] = grid.permute(own_kv, {"p": p_mask, "h": h_mask})
        kv_parts = {(*mask, 0): value for mask, value in chips.items()}
        for mask, value in chips.items():
            kv_parts[(*mask, 1)] = grid.permute(value, {"c": 1})
        entries = [(mask, number, None) for number, mask in enumerate(kv_parts)]
        return entries, list(kv_parts.values())

    def gather_kv_staged(own_kv, ties):
        (near,) = stack([(parts(own_kv, "p"), None, None)], ties)
        far = grid.permute(near, {"h": 1})
        entries = [
            ((p_mask, h_mask, c_mask), 2 * c_mask + h_mask, p_mask)
            for c_mask in range(2)
            for h_mask in range(2)
            for p_mask in range(grid.sizes["p"])
        ]
        return entries, [near, far, grid.permute(near, {"c": 1}), grid.permute(far, {"c": 1})]

    def project_q(projected, loop, ties=()):
        return whole_call(
            project_q_body,
            shape(tokens, width_q),
            None,
            [projected[1], projected[2], w_qkv, lifts_in[loop], *tables],
            ties,
        )

    def attend(queries, gathered, ties=()):
        entries, operands = gathered
        return whole_call(
            functools.partial(attend_body, entries),
            [
                shape(tokens, width_q),
                jax.ShapeDtypeStruct((H, tokens, 1), F32),
                shape(seq_len, 2 * HD),
            ],
            coordinates,
            [queries, *masks, *operands],
            ties,
            flops=int(COST_ATTEND * tokens * width_q * seq_len),
        )

    projected_one = project_kv([inputs], 0)
    gate, up, own_kv = stack(
        [(gate, None, None), (up, None, None), ([projected_one[0]], None, None)]
    )
    gate, up = parts(gate, "y"), parts(up, "x")
    w_out, ol_0, ol_1, od, ql_1 = whole_call(
        functools.partial(
            unpack_second_body,
            grid.blocks_of(straight),
            grid.order(turned),
            (out_rows, out_up, ol_rows, ol_up, ql_rows, ql_up),
            2,
        ),
        [
            shape(width_q, width), shape(rank, width), shape(rank, width),
            shape(width_q, 2 * rank), shape(rank, qkv_cols),
        ],
        coordinates,
        second,
        [gate[0]],
    )
    queries_one = project_q(projected_one, 0, [gate[0]])
    down_left, down_right = stack([(down, None, [left_cols, width - left_cols])], [queries_one])
    down_left, down_right = parts(down_left, "x"), parts(down_right, "y")
    attended_one = attend(queries_one, gather_kv_staged(own_kv, [down_left[0]]))
    down_left, down_right = stack(
        [(down_left, None, None), (down_right, None, None)], [attended_one[0]]
    )
    down_left, down_right = parts(down_left, "y"), parts(down_right, "x")
    lifts_in[1] = ql_1
    lifts_out = (ol_0, ol_1)

    def leave(loop, mixed_b, residual):
        return whole_call(
            functools.partial(leave_body, loop == 0),
            [shape(tokens, rank), shape(tokens, width, F32), shape(tokens, width)],
            None,
            [mixed_b, od, w_out, lifts_out[loop], residual, gains],
            flops=int(COST_LEAVE * tokens * width_q * width),
        )

    left_one = leave(0, attended_one[0], projected_one[3])
    w_gate = in_order(grid, coordinates, (gate, ("p", "x", "y")))
    w_up = in_order(grid, coordinates, (up, ("p", "y", "x")))
    w_down = in_order(
        grid, coordinates, (down_left, ("p", "x", "y")), (down_right, ("p", "y", "x"))
    )

    qkv_block = qkv_up + 2 * ql_up
    out_block = out_up + 2 * ol_up

    cotangent_in = grid.tokens_in(cotangent)

    def feed_forward(loop, projected, queries, attended, left, ties=()):
        own_kv, normed_b, low_rank_b, residual = projected
        mixed_b, log_total, both = attended
        side_b, middle, normed_ff_b = left
        spread_own, spread_sent = whole_call(
            functools.partial(
                spread_body,
                (
                    grid.devices, qkv_rows, qkv_block, ql_rows, qkv_up + loop * ql_up,
                    out_rows, out_block, ol_rows, out_up + loop * ol_up,
                ),
            ),
            [shape(tokens, grid.devices // 2 * (qkv_block + out_block))] * 2,
            coordinates,
            [normed_b, low_rank_b, mixed_b, side_b],
            (),
            [pltpu.VMEM((2, tokens, grid.devices // 2 * (qkv_block + out_block)), BF)],
        )
        ff_in = grid.tokens_in(normed_ff_b, [spread_sent])
        ff_own, gate_b, up_b, *ff_sent = ff_forward(ff_in, w_gate, w_up, w_down)
        own, other = tokens_out(grid, ff_own, ff_sent, ties)
        cache = (
            residual, (spread_own, grid.permute(spread_sent, {"c": 1})), queries, both, log_total,
            middle, ff_in, gate_b, up_b,
        )
        return [middle, own, other], cache

    addends, cache_one = feed_forward(
        0, projected_one, queries_one, attended_one, left_one, [cotangent_in[1]]
    )
    projected_two = project_kv(addends, 1)
    queries_two = project_q(projected_two, 1)
    attended_two = attend(queries_two, gather_kv(projected_two[0]))
    left_two = leave(1, attended_two[0], projected_two[3])
    addends, cache_two = feed_forward(
        1, projected_two, queries_two, attended_two, left_two
    )
    result = whole_call(result_body, shape(tokens, width), None, addends)

    group_names = ("y", "x", "p")
    names = ("y", "x", "p", "h")
    half = grid.devices // 2
    joined_columns = slice(0, half * qkv_block)
    mixed_columns = slice(half * qkv_block, half * (qkv_block + out_block))

    def step(stages, ties=()):
        return fold(
            grid, coordinates, [(item[0], stage, [item[1]]) for item, stage in stages], ties
        )

    y_size = grid.sizes["y"]

    def with_core(values):
        return values, grid.permute(values, {"c": 1})

    def backward_loop(cache, grad_result, blocks_in, loop, old):
        (
            residual, spreads, queries, both, log_total, middle, ff_in, gate_b, up_b,
        ) = cache
        last = old is not None
        ql, ol = lifts_in[loop], lifts_out[loop]

        def before(name):
            return old[name] if last else None

        def grouped(values):
            return values.reshape(groups, values.shape[0] // groups, values.shape[1])

        own, grad_gate_b, grad_up_b, *down = ff_backward(
            blocks_in, gate_b, up_b, w_gate, w_up, w_down, before("down")
        )
        down, sent = down[:2], down[2:]
        ties = [] if last else [result]
        if last:
            down = fold(
                grid,
                coordinates,
                [
                    (group_names, "x", [[grouped(down[0])]]),
                    (group_names, "y", [[grouped(down[1])]]),
                ],
            )
            ties = [down[0][1][0]]
        own, other = tokens_out(grid, own, sent, ties)
        pair = ff_weights(
            grid,
            coordinates,
            ff_in,
            grad_gate_b,
            grad_up_b,
            (old["gate"], old["up"]) if last else None,
            ("x", "y" if y_size == 2 else "x") if last else None,
            [own],
        )
        ties = [pair[0]]
        if last:
            d_gate = (("y", "p"), [pair[0], grid.permute(pair[1], {"x": 1})])
            if y_size == 2:
                d_up = (("x", "p"), [pair[2], grid.permute(pair[3], {"y": 1})])
            else:
                d_up = (("y", "p"), [pair[2], grid.permute(pair[3], {"x": 1})])
        else:
            d_gate, d_up = pair
        grad_middle, grad_branch_b, grad_mixed_b, gain_grad_ff = whole_call(
            functools.partial(enter_back_body, loop == 0),
            [
                shape(tokens, width, F32), shape(tokens, width + rank), shape(tokens, width_q),
                shape(8, width, F32),
            ],
            None,
            [own, other, grad_result, middle, gains, w_out, ol, od],
            ties,
            flops=int(COST_ENTER * tokens * width_q * width),
        )
        ties = []
        if last:
            down = fold(
                grid,
                coordinates,
                [(down[0][0], "y", [down[0][1]]), (down[1][0], "x", [down[1][1]])],
                [grad_mixed_b],
            )
            ties = [down[0][1][0]]
        kv_own, kv_sent, grad_queries_b = pl.pallas_call(
            tied(attend_back_body, 10, ties),
            out_shape=[jax.ShapeDtypeStruct((grid.blk // 2, tokens, 2 * HD), BF)] * 2
            + [shape(tokens, width_q)],
            in_specs=[pl.BlockSpec(memory_space=pltpu.VMEM)] * 9
            + [pl.BlockSpec(memory_space=pltpu.SMEM)]
            + [ANY] * len(ties),
            scratch_shapes=[pltpu.VMEM((seq_len, HD), F32)] * 2,
            cost_estimate=pl.CostEstimate(
                flops=int(COST_ATTEND_BACK * tokens * width_q * seq_len),
                bytes_accessed=0,
                transcendentals=0,
            ),
            compiler_params=pltpu.CompilerParams(vmem_limit_bytes=48 * 1024 * 1024),
        )(queries, both, *masks, log_total, grad_mixed_b, *tables, coordinates, *ties)
        grad_kv = (("p", "h"), [kv_own, grid.permute(kv_sent, {"c": 1})])
        (grad_kv,) = step([(grad_kv, "h")])
        (grad_kv,) = step([(grad_kv, "p")])
        branch = with_core(grad_branch_b)
        d_out, d_od = outer(
            spreads,
            mixed_columns,
            branch,
            [width, rank],
            [old["out"]] if last else [],
            [grad_kv[1][0]],
        )
        (d_queries,) = outer(
            spreads,
            joined_columns,
            with_core(grad_queries_b),
            [width_q],
            [old["queries"]] if last else [],
            [d_out],
        )
        sums = {"out": d_out, "od": d_od, "queries": d_queries}

        def second_sums(ties):
            sums["gate"], sums["up"], down[0], down[1] = fold(
                grid,
                coordinates,
                [
                    (d_gate[0], "y", [d_gate[1]]),
                    (d_up[0], d_up[0][0], [d_up[1]]),
                    (down[0][0], "p", [down[0][1]]),
                    (down[1][0], "p", [down[1][1]]),
                ],
                ties,
            )

        ties = [] if last else [d_queries, cache_one[1][1]]
        if last:
            sums["out"], sums["queries"] = fold(
                grid,
                coordinates,
                [
                    (names, "x", [[blocks(value)] for value in (d_out, d_od, old["od"])]),
                    (names, "y", [[blocks(value)] for value in (d_queries, old["qd"])]),
                ],
            )
            second_sums([sums["out"][1][0]])
            ties = [sums["gate"][1][0]]
        else:
            sums["gate"], sums["up"] = d_gate, d_up
        sums["down"] = down
        grad_in_b = whole_call(
            functools.partial(rope_back_body, len(grad_kv[1])),
            shape(tokens, 2 * HD + rank),
            None,
            [*grad_kv[1], grad_queries_b, ql, *tables],
            ties,
        )
        sums["kv"], sums["qd"] = outer(
            spreads,
            joined_columns,
            with_core(grad_in_b),
            [2 * HD, rank],
            [old["kv"]] if last else [],
        )
        following, following_b, gain_grads = whole_call(
            functools.partial(leave_back_body, loop == 0),
            [shape(tokens, width, F32), shape(tokens, width), shape(8, width, F32)],
            None,
            [
                grad_in_b, grad_queries_b, w_qkv, qd, residual, gains, grad_middle, gain_grad_ff,
            ]
            + ([old["gains"]] if last else []),
        )
        sums["gains"] = gain_grads
        return following, following_b, sums

    def blocks(values):
        return values.reshape(half, values.shape[0] // half, values.shape[1])

    grad_one, grad_one_b, sums_two = backward_loop(cache_two, cotangent, cotangent_in, 1, None)
    grad_inputs, unused, sums = backward_loop(
        cache_one, grad_one, grid.tokens_in(grad_one_b), 0, sums_two
    )

    late = whole_call(
        functools.partial(late_body, (half, qkv_rows, gain_cols)),
        jax.ShapeDtypeStruct((half, qkv_block, 2 * HD + rank), BF),
        coordinates,
        [blocks(sums["kv"]), blocks(sums["qd"]), *with_core(sums["gains"])],
    )
    (late,) = step([((names, [late]), "x")])
    d_down = whole_call(
        functools.partial(down_body, len(sums["down"][0][1])),
        shape(hidden_block, width, F32),
        None,
        sums["down"][0][1] + sums["down"][1][1],
        [late[1][0]],
    )
    gate, up = step([(sums["gate"], "p"), (sums["up"], "p")], [d_down])
    outs, queries = step([(sums["out"], "y"), (sums["queries"], "x")], [gate[1][0]])
    (late,) = step([(late, "y")], [outs[1][0]])
    split = whole_call(
        functools.partial(split_body, len(gate[1])),
        [jax.ShapeDtypeStruct((2, qkv_rows, wide), BF)] * 4,
        coordinates,
        gate[1] + up[1],
        [late[1][0]],
    )
    back = [
        split[0],
        grid.permute(split[1], {"c": 1}),
        grid.permute(split[2], {"h": 1}),
        grid.permute(split[3], {"h": 1, "c": 1}),
    ]
    outs, queries, late = step([(outs, "h"), (queries, "h"), (late, "h")], [split[0]])
    outs, queries, late = step([(outs, "p"), (queries, "p"), (late, "p")])
    d_gate_up = whole_call(
        functools.partial(join_body, groups, hidden_block, block_up),
        shape(qkv_rows, 8 * groups * hidden_block, F32),
        coordinates,
        back,
    )
    last = [outs[1], queries[1], late[1]]
    d_gains, d_qkv, d_out, d_qd, d_ql, d_od, d_ol = whole_call(
        functools.partial(
            finish_body,
            len(outs[1]),
            (
                qkv_rows, qkv_up, ql_rows, ql_up, out_rows, out_up, ol_rows, ol_up, gain_cols,
            ),
        ),
        [
            shape(2, gain_cols, F32),
            shape(qkv_rows, qkv_cols, F32),
            shape(out_rows, width, F32),
            jax.ShapeDtypeStruct(adapter_query_down.shape, F32),
            jax.ShapeDtypeStruct(adapter_query_lift.shape, F32),
            jax.ShapeDtypeStruct(adapter_output_down.shape, F32),
            jax.ShapeDtypeStruct(adapter_output_lift.shape, F32),
        ],
        None,
        [value for values in last for value in values],
    )
    return (
        result, grad_inputs, d_gains, d_qkv, d_out, d_gate_up, d_down, d_qd, d_ql, d_od, d_ol,
    )


def solution(mesh):
    grid = Grid(mesh)
    rows = P(AXES, None)
    deep = P(None, AXES, None)
    in_specs = (
        rows, P("fsdp", None), rows, P(None, AXES), rows, rows, rows, rows, deep, deep, deep, deep,
    )
    out_specs = (
        rows, rows, P(None, AXES), rows, rows, rows, rows, deep, deep, deep, deep,
    )

    def run(*arguments):
        return per_device(grid, *arguments)

    return jax.shard_map(
        run, mesh=mesh, in_specs=in_specs, out_specs=out_specs, check_vma=False
    )
```
